32 devices in a mesh: ep: 16 (over z, y, x), tp: 2 (over core).
Axes of the slice: x: 2, y: 2, z: 4, core: 2. Of those that a mesh axis runs over, the one named last changes fastest.
Arguments:
- tokens: bfloat16 [16384, 1024], P('ep'), may hold values from -6 to 6
- gain_attn: bfloat16 [1024], replicated, may hold values from 0.5 to 1.5
- query_weight_matrix: bfloat16 [1024, 1024], P(None, 'tp'), may hold values from -0.75 to 0.75
- key_value_weight: bfloat16 [1024, 1024], P(None, 'tp'), may hold values from -0.75 to 0.75
- w_out: bfloat16 [1024, 1024], P('tp'), may hold values from -0.75 to 0.75
- gain_ffn: bfloat16 [1024], replicated, may hold values from 0.5 to 1.5
- w_router: bfloat16 [1024, 16], replicated, may hold values from -0.09375 to 0.09375
- w_gate_up: bfloat16 [16, 2, 1024, 512], P('ep', None, None, 'tp'), may hold values from -0.1875 to 0.1875
- w_down: bfloat16 [16, 512, 1024], P('ep', 'tp'), may hold values from -6 to 6
- routes: int32 [16384, 8], P(('ep', 'tp')), may hold values from 0 to 15, all different within a row; in each aligned block of 512 rows (0 to 511, 512 to 1023, ...) at most 384 rows name the same one
- doc_lengths: int32 [16, 4], P('ep'), may hold values from 1 to 768, 1024 in all within a row
- valid_mask: int32 [16384], P('ep'), may hold values from 0 to 1, as said below
- cotangent: bfloat16 [16384, 1024], P('ep'), may hold values from -6 to 6
Outputs:
- layer_out: bfloat16 [16384, 1024], P('ep')
- grad_tokens: float32 [16384, 1024], P('ep')
- grad_gain_attn: float32 [1024], replicated
- grad_w_query: float32 [1024, 1024], P(None, 'tp')
- grad_w_kv: float32 [1024, 1024], P(None, 'tp')
- grad_w_out: float32 [1024, 1024], P('tp')
- grad_gain_ffn: float32 [1024], replicated
- grad_w_router: float32 [1024, 16], replicated
- grad_w_gate_up: float32 [16, 2, 1024, 512], P('ep', None, None, 'tp')
- grad_w_down: float32 [16, 512, 1024], P('ep', 'tp')
- rms_stats: float32 [3], replicated
The draws below stay inside these ranges and needn't reach their ends.
Inputs may be any that keep to these rules, and one draw needn't show every extreme that they name: `routes`: each row names 8 different experts. Within the 512 rows of one device (aligned blocks, in order) no expert is named by more than 384 rows, and in some device an expert is named by exactly 384. `doc_lengths`: the 4 lengths of a row sum to 1024; the largest of each row is exactly 768. `valid_mask`: the first token of every sequence is real.
All inputs are finite; a program needn't handle non-finite values.
Results may differ from the reference program's by a relative error of at most 0.024.
Values may be sent and summed in bfloat16 or wider, within the bound.
No kernel may reach another device: no remote copies, remote signals or barrier semaphores. Data moves between devices by JAX's collectives and lax.ppermute only.
A program may use at most 320 MiB of HBM per device.

```python
import math
import jax
import jax.numpy as jnp
import numpy as np
from jax import lax

MODEL_WIDTH = 1024
QUERY_HEADS = 16
KEY_VALUE_HEADS = 8
HEAD_SIZE = 64
FF = 512
TOPK = 8
SEQUENCE_LENGTH = 1024
WINDOW = 1024
NDOC = 4
EXPERTS = 16
SEQS = 16
ROWS = 512
TOKENS = 16384
CAP = 384
N_EP = 16
N_TP = 2


def draw_valid_mask(key, part):
    key = jax.random.fold_in(key, 7)
    places = jnp.arange(TOKENS, dtype=jnp.int32)
    sequence = places // SEQUENCE_LENGTH
    threshold = 300 + 650 * sequence // max(SEQS - 1, 1)
    rolled = jax.random.randint(key, (TOKENS,), 0, 1000, dtype=jnp.int32)
    return ((rolled < threshold) | (places % SEQUENCE_LENGTH == 0)).astype(jnp.int32)


def levels(rng, extent, shards, low, top_value):
    factor_of, own = 1.0, jax.random.fold_in(rng, 6)
    for axis_at, shards_of in shards:
        steps = jnp.exp(jax.random.uniform(jax.random.fold_in(own, axis_at), (shards_of,), jnp.float32, low / len(shards), top_value / len(shards)))
        factor_of = factor_of * jnp.repeat(steps, extent[axis_at] // shards_of).reshape([-1 if axis == axis_at else 1 for axis in range(len(extent))])
    return factor_of


def length_profile(count, total, most, lean):
    portions = [(1 << 20) // math.isqrt(grade ** lean) + 1 for grade in range(2, count + 1)]
    surplus, holding = total - most - (count - 1), [1] * (count - 1)
    while surplus > 0:
        free = [i for i in range(count - 1) if holding[i] < most]
        whole, remaining = sum([portions[i] for i in free]), surplus
        for i in free:
            more = min(most - holding[i], max(1, remaining * portions[i] // whole), surplus)
            holding[i] = holding[i] + more
            surplus = surplus - more
    return np.array([most] + holding)


def uneven(key, count, total, most, slope):
    if count == 2:
        one = jax.random.randint(key, (), max(1, total - most), min(most, total - 1) + 1)
        return jnp.stack([one, total - one])
    sizes = jnp.asarray(length_profile(count, total, most, slope), jnp.int32)
    pairs = (count - 1) // 2
    giver, receiver = sizes[1:1 + 2 * pairs:2], sizes[2:2 + 2 * pairs:2]
    slack = jnp.minimum(giver - 1, most - receiver)
    moved = jax.random.randint(jax.random.fold_in(key, 1), (pairs,), 0, 1 << 20) % (slack + 1)
    sizes = sizes.at[1:1 + 2 * pairs:2].set(giver - moved).at[2:2 + 2 * pairs:2].set(receiver + moved)
    return sizes[jax.random.permutation(jax.random.fold_in(key, 2), count)]


def assign_block(own_key, own, number, rows, count, top, reach, slope):
    order = jax.random.permutation(own_key, count)
    heavy_load, ordinary = load_shares(count, rows * top, reach, slope, True), load_shares(count, rows * top, reach, slope, False)
    places = jnp.arange(count)

    def named(sizes, rotation):
        used = int((sizes > 0).sum())
        fixed = max(1, used // 4)
        moved = fixed + (places - fixed + rotation * (used - fixed)) % max(1, count - fixed)
        return jnp.zeros((count,), jnp.int32).at[order[jnp.where(places < fixed, places, moved)]].set(jnp.asarray(sizes, jnp.int32))

    sizes = jnp.where(number % 4 == 0, named(heavy_load, number // 4), named(ordinary, number - number // 4 - 1))
    mixed = jax.random.permutation(jax.random.fold_in(own, 3), count)
    source_of, sink = mixed[0:count // 2 * 2:2], mixed[1:count // 2 * 2:2]
    margin = jnp.minimum(sizes[source_of] - 1, reach - sizes[sink]) // 2
    margin = jnp.where((source_of == order[0]) | (sink == order[0]) | (sizes[sink] == 0), 0, jnp.maximum(margin, 0))
    moved = jax.random.randint(jax.random.fold_in(own, 4), (count // 2,), 0, 1 << 20) % (margin + 1)
    sizes = sizes.at[source_of].add(-moved).at[sink].add(moved)
    items = jnp.searchsorted(jnp.cumsum(sizes), jnp.arange(rows * top), side="right").astype(jnp.int32)
    listing = items.reshape(top, rows).T
    listing = listing[jax.random.permutation(jax.random.fold_in(own, 1), rows)]
    rotation = jax.random.randint(jax.random.fold_in(own, 2), (rows, 1), 0, top)
    return jnp.take_along_axis(listing, (jnp.arange(top)[None, :] + rotation) % top, axis=1)


def load_shares(amount, total, bound, slope, full):
    loads = [(1 << 20) // math.isqrt(grade ** slope) + 1 for grade in range(1, amount + 1)]
    largest = bound if full else min(bound, max(-(-total // amount), total * loads[0] // sum(loads)))
    least = 1 if total - largest >= amount - 1 else 0
    holding, surplus = [largest] + [least] * (amount - 1), total - largest - least * (amount - 1)
    while surplus > 0:
        free = [i for i in range(1, amount) if holding[i] < largest] or [i for i in range(1, amount) if holding[i] < bound]
        mass, remaining = sum([loads[i] for i in free]), surplus
        for i in free:
            more = min(bound - holding[i], max(1, remaining * loads[i] // mass), surplus)
            holding[i] = holding[i] + more
            surplus = surplus - more
    return np.array(holding)


def bell_draw(key, shape, width, most, split=(), kind=jnp.bfloat16):
    factor_of = levels(key, shape, split, -0.22, 0.18) if split else 1.0
    drawn = jax.random.normal(key, shape, jnp.float32) * width * factor_of
    return jnp.minimum(jnp.maximum(drawn, -most), most).astype(kind)


def setup_inputs(seed: int = 0) -> dict:
    key_list = jax.random.split(jax.random.key(seed), 14)
    tokens = bell_draw(key_list[0], (TOKENS, MODEL_WIDTH), 1.0, 6.0, ((0, 16),))
    gain_attn = jnp.clip(1.0 + 0.1 * jax.random.normal(key_list[1], (MODEL_WIDTH,), jnp.float32), 0.5, 1.5).astype(jnp.bfloat16)
    query_weight_matrix = bell_draw(key_list[2], (MODEL_WIDTH, QUERY_HEADS * HEAD_SIZE), (MODEL_WIDTH // 16) ** -0.5, 0.75, ((1, 2),))
    key_value_weight = bell_draw(key_list[3], (MODEL_WIDTH, 2 * KEY_VALUE_HEADS * HEAD_SIZE), (MODEL_WIDTH // 16) ** -0.5, 0.75, ((1, 2),))
    w_out = bell_draw(key_list[4], (QUERY_HEADS * HEAD_SIZE, MODEL_WIDTH), (QUERY_HEADS * HEAD_SIZE // 16) ** -0.5, 0.75, ((0, 2),))
    gain_ffn = jnp.clip(1.0 + 0.1 * jax.random.normal(key_list[5], (MODEL_WIDTH,), jnp.float32), 0.5, 1.5).astype(jnp.bfloat16)
    w_router = bell_draw(key_list[6], (MODEL_WIDTH, EXPERTS), (4 * MODEL_WIDTH) ** -0.5, 0.09375)
    w_gate_up = bell_draw(key_list[7], (EXPERTS, 2, MODEL_WIDTH, FF), MODEL_WIDTH ** -0.5, 0.1875, ((0, 16), (3, 2)))
    w_down = bell_draw(key_list[8], (EXPERTS, FF, MODEL_WIDTH), 1 ** -0.5, 6.0, ((0, 16), (1, 2)))
    routes_keys = jax.random.split(jax.random.fold_in(key_list[9], 1), TOKENS // ROWS)
    routes_turns = jax.random.permutation(jax.random.fold_in(key_list[9], 3), TOKENS // ROWS)
    routes = jax.vmap(lambda own, number: assign_block(jax.random.fold_in(key_list[9], 2), own, number, ROWS, EXPERTS, TOPK, CAP, 1))(routes_keys, routes_turns).reshape((TOKENS, TOPK))
    doc_lengths = jax.vmap(lambda own: uneven(own, NDOC, SEQUENCE_LENGTH, 3 * SEQUENCE_LENGTH // 4, 1))(jax.random.split(key_list[10], SEQS)).reshape((SEQS, NDOC)).astype(jnp.int32)
    valid_mask = draw_valid_mask(jax.random.fold_in(key_list[13], 71), 0)
    cotangent = bell_draw(key_list[12], (TOKENS, MODEL_WIDTH), 1.0, 6.0, ((0, 16),))
    return {"tokens": tokens, "gain_attn": gain_attn, "query_weight_matrix": query_weight_matrix, "key_value_weight": key_value_weight, "w_out": w_out, "gain_ffn": gain_ffn, "w_router": w_router, "w_gate_up": w_gate_up, "w_down": w_down, "routes": routes, "doc_lengths": doc_lengths, "valid_mask": valid_mask, "cotangent": cotangent}


ATTN_SCALE = 0.015625
RESID_SCALE = 0.22
NORM_EPS = 1e-06
ROPE_BASE = 10000.0
MASKED = -1e+30
highest_precision = lax.Precision.HIGHEST

@jax.custom_vjp
def low(v):
    return lax.optimization_barrier(v.astype(jnp.bfloat16)).astype(jnp.float32)

@jax.custom_vjp
def lower_backward(v):
    return v

def low_keep(v):
    return (low(v), None)

def low_pass(kept, grad):
    return (grad,)

def back_keep(v):
    return (v, None)

def back_low(kept, grad):
    return (low(grad),)
low.defvjp(low_keep, low_pass)
lower_backward.defvjp(back_keep, back_low)

def rms_norm(values, norm_gain):
    factor = lax.rsqrt(lax.optimization_barrier(jnp.mean(values * values, axis=-1, keepdims=True)) + NORM_EPS)
    return values * factor * norm_gain

def doc_positions(lengths):
    places = jnp.arange(SEQUENCE_LENGTH, dtype=jnp.int32)
    doc_ends = jnp.cumsum(lengths).astype(jnp.int32)
    passed = (places[:, None] >= doc_ends[None, :]).astype(jnp.int32)
    doc_ids = lax.optimization_barrier(jnp.sum(passed, axis=1)).astype(jnp.int32)
    offsets = places - lax.optimization_barrier(jnp.sum(passed * lengths[None, :], axis=1)).astype(jnp.int32)
    frequencies = jnp.exp(jnp.arange(HEAD_SIZE // 2, dtype=jnp.float32) * (-2.0 * math.log(ROPE_BASE) / HEAD_SIZE))
    angles = offsets.astype(jnp.float32)[:, None] * frequencies[None, :]
    return (doc_ids, jnp.cos(angles), jnp.sin(angles))

def rotate(values, cosine_table, sine_table):
    half_width = values.shape[-1] // 2
    front_half = values[..., :half_width]
    back_half = values[..., half_width:]
    return jnp.concatenate([front_half * cosine_table - back_half * sine_table, back_half * cosine_table + front_half * sine_table], axis=-1)

def attend_sequence(weights, seq_tokens, lengths, valid_row):
    gain_attn, query_weight_matrix, key_value_weight, w_out = weights
    doc_ids, cosine_table, sine_table = doc_positions(lengths)
    normed_attention_input = low(rms_norm(seq_tokens, gain_attn))
    query_before_rotation = lower_backward(jnp.dot(normed_attention_input, query_weight_matrix, precision=highest_precision)).reshape(SEQUENCE_LENGTH, KEY_VALUE_HEADS, QUERY_HEADS // KEY_VALUE_HEADS, HEAD_SIZE)
    key_value_rows = jnp.dot(normed_attention_input, key_value_weight, precision=highest_precision).reshape(SEQUENCE_LENGTH, KEY_VALUE_HEADS, 2, HEAD_SIZE)
    key_pre = lower_backward(key_value_rows[:, :, 0])
    value_rows = lower_backward(low(key_value_rows[:, :, 1]))
    query_rot = low(rotate(query_before_rotation, cosine_table[:, None, None, :], sine_table[:, None, None, :]))
    key_rot = low(rotate(key_pre, cosine_table[:, None, :], sine_table[:, None, :]))
    scores = lower_backward(ATTN_SCALE * jnp.einsum('qngd,knd->ngqk', query_rot, key_rot, precision=highest_precision))
    places = jnp.arange(SEQUENCE_LENGTH, dtype=jnp.int32)
    same_doc = doc_ids[:, None] == doc_ids[None, :]
    causal = places[None, :] <= places[:, None]
    within = places[:, None] - places[None, :] < WINDOW
    usable = (valid_row[None, :] > 0) | (places[None, :] == places[:, None])
    allowed = same_doc & causal & within & usable
    scores = jnp.where(allowed, scores, MASKED)
    row_max = lax.optimization_barrier(jnp.max(scores, axis=-1, keepdims=True))
    weight = jnp.exp(scores - row_max)
    attn_probs = weight / lax.optimization_barrier(jnp.sum(weight, axis=-1, keepdims=True))
    mixed_rows = jnp.einsum('ngqk,knd->qngd', low(attn_probs), value_rows, precision=highest_precision)
    mixed_rows = lower_backward(low(mixed_rows)).reshape(SEQUENCE_LENGTH, QUERY_HEADS * HEAD_SIZE)
    return lower_backward(jnp.dot(mixed_rows, w_out, precision=highest_precision))

def expert_term(normed_ffn, gate_probs, routes, gate_up, down, expert):
    limit = N_EP * N_TP * CAP
    picked = routes == expert
    chosen = lax.optimization_barrier(jnp.sum(picked.astype(jnp.int32), axis=1))
    gate_of = lax.optimization_barrier(jnp.sum(jnp.where(picked, gate_probs, 0.0), axis=1))
    row_count = jnp.sum(chosen)
    row_order = jnp.nonzero(chosen > 0, size=limit, fill_value=0)[0].astype(jnp.int32)
    live_rows = (jnp.arange(limit, dtype=jnp.int32) < row_count).astype(jnp.float32)
    gathered = lower_backward(normed_ffn[row_order])
    gate_pre = lower_backward(jnp.dot(gathered, gate_up[0], precision=highest_precision))
    up_pre = lower_backward(jnp.dot(gathered, gate_up[1], precision=highest_precision))
    hidden = low(jax.nn.silu(gate_pre) * up_pre)
    expert_rows = lower_backward(low(jnp.dot(hidden, down, precision=highest_precision)))
    scaled = expert_rows * (live_rows * gate_of[row_order])[:, None]
    return jnp.zeros((TOKENS, MODEL_WIDTH), jnp.float32).at[row_order].add(scaled)

def layer_forward(tokens, gain_attn, query_weight_matrix, key_value_weight, w_out, gain_ffn, w_router, w_gate_up, w_down, routes, doc_lengths, valid_mask):
    weights = (gain_attn, query_weight_matrix, key_value_weight, w_out)

    def one_sequence(items):
        seq_tokens, lengths, valid_row = items
        branch = attend_sequence(weights, seq_tokens, lengths, valid_row)
        return (seq_tokens + RESID_SCALE * branch, branch)
    middle, attn_branch = lax.map(jax.checkpoint(one_sequence), (tokens.reshape(SEQS, SEQUENCE_LENGTH, MODEL_WIDTH), doc_lengths, valid_mask.reshape(SEQS, SEQUENCE_LENGTH)))
    middle = middle.reshape(TOKENS, MODEL_WIDTH)
    attn_branch = attn_branch.reshape(TOKENS, MODEL_WIDTH)
    normed_ffn = low(rms_norm(middle, gain_ffn))
    logits = jnp.dot(normed_ffn, w_router, precision=highest_precision)
    picked_logits = jnp.take_along_axis(logits, routes, axis=1)
    logit_max = lax.optimization_barrier(jnp.max(picked_logits, axis=1, keepdims=True))
    gate_weight = jnp.exp(picked_logits - logit_max)
    gate_probs = gate_weight / lax.optimization_barrier(jnp.sum(gate_weight, axis=1, keepdims=True))
    expert_sum = jnp.zeros((TOKENS, MODEL_WIDTH), jnp.float32)
    checked_term = jax.checkpoint(expert_term)
    for expert in range(EXPERTS):
        expert_sum = expert_sum + checked_term(normed_ffn, gate_probs, routes, w_gate_up[expert], w_down[expert], jnp.asarray(expert, dtype=jnp.int32))
    return (middle + RESID_SCALE * expert_sum, (attn_branch, expert_sum))

def reference(tokens, gain_attn, query_weight_matrix, key_value_weight, w_out, gain_ffn, w_router, w_gate_up, w_down, routes, doc_lengths, valid_mask, cotangent):
    primals = tuple((item.astype(jnp.float32) for item in (tokens, gain_attn, query_weight_matrix, key_value_weight, w_out, gain_ffn, w_router, w_gate_up, w_down)))

    def forward(*floats):
        return layer_forward(*floats, routes, doc_lengths, valid_mask)
    outf, pullback, (attn_branch, expert_sum) = jax.vjp(forward, *primals, has_aux=True)
    grads = pullback(cotangent.astype(jnp.float32))
    live_rows = valid_mask.astype(jnp.float32)
    real_count = jnp.sum(live_rows)

    def mean_square(values):
        return jnp.sum(live_rows * lax.optimization_barrier(jnp.sum(values * values, axis=1))) / (real_count * MODEL_WIDTH)
    rms_stats = jnp.sqrt(jnp.stack([mean_square(outf), mean_square(RESID_SCALE * attn_branch), mean_square(RESID_SCALE * expert_sum)]))
    return (outf.astype(jnp.bfloat16), grads[0], grads[1], grads[2], grads[3], grads[4], grads[5], grads[6], grads[7], grads[8], rms_stats)
```

```python
import functools
import math

import jax
import jax.numpy as jnp
from jax import lax
from jax.experimental import pallas as pl
from jax.experimental.pallas import tpu as pltpu
from jax.sharding import PartitionSpec as P

SEQUENCE_LENGTH = 1024
WINDOW = 1024
ATTN_SCALE = 0.015625
RESID_SCALE = 0.22
NORM_EPS = 1e-06
ROPE_BASE = 10000.0
F32 = jnp.float32
BF = jnp.bfloat16
VMEM_BYTES = 60 * 1024 * 1024


def dot(a, b):
    return jnp.dot(a, b, preferred_element_type=F32)


def dot_nt(a, b):
    return lax.dot_general(a, b, (((1,), (1,)), ((), ())), preferred_element_type=F32)


def dot_tn(a, b):
    return lax.dot_general(a, b, (((0,), (0,)), ((), ())), preferred_element_type=F32)


HD = 64
NEG = -1e30
BLK = 256


def swap_halves(v, lane):
    return jnp.where(lane % HD < HD // 2, pltpu.roll(v, 128 - HD // 2, 1), pltpu.roll(v, HD // 2, 1))


def mask_bias(start, valid, i, keys):
    row = lax.broadcasted_iota(jnp.int32, (BLK, keys), 0) + i * BLK
    key = lax.broadcasted_iota(jnp.int32, (BLK, keys), 1)
    first = jnp.maximum(start[i * BLK : (i + 1) * BLK, :], row[:, :1] - (WINDOW - 1))
    ok = (key >= first) & (key <= row) & ((valid[:, :keys] > 0) | (key == row))
    return jnp.where(ok, 0.0, NEG).astype(F32)


def attn_forward_body(x, gain, wq, wkv, wo, cos, sin, start, valid, h1, q, kd, vd, o, lse, part):
    nkv = wkv.shape[1] // 128
    lane = lax.broadcasted_iota(jnp.int32, (BLK, 128), 1)
    low = lane < HD
    ga = gain[...].astype(F32)
    for i in range(x.shape[0] // BLK):
        rs = pl.ds(i * BLK, BLK)
        keys = (i + 1) * BLK
        xb = x[rs, :].astype(F32)
        r = lax.rsqrt(jnp.mean(xb * xb, axis=1, keepdims=True) + NORM_EPS)
        hb = (xb * r * ga).astype(BF)
        h1[rs, :] = hb
        qp = dot(hb, wq[...])
        kvp = dot(hb, wkv[...])
        cb, sb = cos[rs, :], sin[rs, :]
        for n in range(nkv):
            ns = slice(n * 128, (n + 1) * 128)
            qn = qp[:, ns]
            q[rs, ns] = ((qn * cb + swap_halves(qn, lane) * sb) * ATTN_SCALE).astype(BF)
            kv = kvp[:, ns]
            rot = kv * cb + swap_halves(kv, lane) * sb
            kd[rs, ns] = jnp.where(low, rot, pltpu.roll(rot, HD, 1)).astype(BF)
            vd[rs, ns] = jnp.where(low, pltpu.roll(kv, HD, 1), kv).astype(BF)
        bias = mask_bias(start, valid, i, keys)
        bias2 = jnp.concatenate([bias, bias], axis=0)
        lse_all = jnp.zeros((BLK, 128), F32)
        for n in range(nkv):
            ns = slice(n * 128, (n + 1) * 128)
            qn = q[rs, ns]
            zero = jnp.zeros_like(qn)
            q2 = jnp.concatenate([jnp.where(low, qn, zero), jnp.where(low, zero, qn)], axis=0)
            s = dot_nt(q2, kd[:keys, ns]) + bias2
            m = jnp.max(s, axis=1, keepdims=True)
            p = jnp.exp(s - m)
            total = jnp.sum(p, axis=1, keepdims=True)
            o2 = dot(p.astype(BF), vd[:keys, ns]) * (1.0 / total)
            o[rs, ns] = jnp.where(low, o2[:BLK], o2[BLK:]).astype(BF)
            l2 = m + jnp.log(total)
            lse_all = jnp.where(lane == 2 * n, l2[:BLK], jnp.where(lane == 2 * n + 1, l2[BLK:], lse_all))
        lse[rs, :] = lse_all
        part[rs, :] = dot(o[rs, :], wo[...]).astype(BF)


def attn_forward(x, gain, wq, wkv, wo, cos, sin, start, valid):
    rows, width = x.shape
    wid = wq.shape[1]
    kvw = wkv.shape[1]
    shape = jax.ShapeDtypeStruct
    return pl.pallas_call(
        attn_forward_body,
        out_shape=[
            shape((rows, width), BF),
            shape((rows, wid), BF),
            shape((rows, kvw), BF),
            shape((rows, kvw), BF),
            shape((rows, wid), BF),
            shape((rows, 128), F32),
            shape((rows, width), BF),
        ],
        compiler_params=pltpu.CompilerParams(vmem_limit_bytes=VMEM_BYTES),
        cost_estimate=pl.CostEstimate(
            flops=2 * rows * width * 3 * wid + 4 * rows * rows * 4 * wid,
            bytes_accessed=12 * rows * width,
            transcendentals=rows * rows * wid // 128,
        ),
        name="attention_forward",
    )(x, gain, wq, wkv, wo, cos, sin, start, valid)


def attn_backward_body(first, q, kd, vd, do, lse, h1, cos, sin, start, valid, dq, dkv, gw, dk, dv):
    nkv = kd.shape[1] // 128
    wid = q.shape[1]
    lane = lax.broadcasted_iota(jnp.int32, (BLK, 128), 1)
    low = lane < HD
    dk[...] = jnp.zeros_like(dk)
    dv[...] = jnp.zeros_like(dv)
    nb = q.shape[0] // BLK
    for i in range(nb):
        rs = pl.ds(i * BLK, BLK)
        keys = (i + 1) * BLK
        cb, sb = cos[rs, :], sin[rs, :]
        bias = mask_bias(start, valid, i, keys)
        bias2 = jnp.concatenate([bias, bias], axis=0)
        lse_i = lse[rs, :]
        for n in range(nkv):
            ns = slice(n * 128, (n + 1) * 128)
            qn, dn = q[rs, ns], do[rs, ns]
            zero = jnp.zeros_like(qn)
            q2 = jnp.concatenate([jnp.where(low, qn, zero), jnp.where(low, zero, qn)], axis=0)
            d2 = jnp.concatenate([jnp.where(low, dn, zero), jnp.where(low, zero, dn)], axis=0)
            h = 2 * (first + n)
            l2 = jnp.concatenate([lse_i[:, h : h + 1], lse_i[:, h + 1 : h + 2]], axis=0)
            p = jnp.exp(dot_nt(q2, kd[:keys, ns]) + bias2 - l2)
            dp = dot_nt(d2, vd[:keys, ns])
            shift = jnp.sum(p * dp, axis=1, keepdims=True)
            ds = (p * (dp - shift)).astype(BF)
            dv[:keys, ns] += dot_tn(p.astype(BF), d2)
            dk[:keys, ns] += dot_tn(ds, q2)
            dq2 = dot(ds, kd[:keys, ns])
            dqn = jnp.where(low, dq2[:BLK], dq2[BLK:]) * ATTN_SCALE
            dq[rs, ns] = (dqn * cb - swap_halves(dqn, lane) * sb).astype(BF)
    for i in range(nb):
        rs = pl.ds(i * BLK, BLK)
        cb, sb = cos[rs, :], sin[rs, :]
        for n in range(nkv):
            ns = slice(n * 128, (n + 1) * 128)
            kk = dk[rs, ns]
            kk = kk + pltpu.roll(kk, HD, 1)
            vv = dv[rs, ns]
            vv = vv + pltpu.roll(vv, HD, 1)
            dkv[rs, ns] = jnp.where(low, kk * cb - swap_halves(kk, lane) * sb, vv).astype(BF)
    gw[:, :wid] = dot_tn(h1[...], dq[...]).astype(BF)
    gw[:, wid:] = dot_tn(h1[...], dkv[...]).astype(BF)


def attn_backward(first, count, q, kd, vd, do, lse, h1, cos, sin, start, valid):
    rows, width = h1.shape
    w = count * 128
    shape = jax.ShapeDtypeStruct
    part = pl.BlockSpec((rows, w), lambda _: (0, first // count))
    whole = lambda v: pl.BlockSpec(v.shape, lambda _: (0, 0))
    return pl.pallas_call(
        functools.partial(attn_backward_body, first),
        grid=(1,),
        in_specs=[part] * 4 + [whole(v) for v in (lse, h1, cos, sin, start, valid)],
        out_specs=[
            pl.BlockSpec((rows, w), lambda _: (0, 0)),
            pl.BlockSpec((rows, w), lambda _: (0, 0)),
            pl.BlockSpec((width, 2 * w), lambda _: (0, 0)),
        ],
        out_shape=[shape((rows, w), BF), shape((rows, w), BF), shape((width, 2 * w), BF)],
        scratch_shapes=[pltpu.VMEM((rows, w), F32), pltpu.VMEM((rows, w), F32)],
        compiler_params=pltpu.CompilerParams(vmem_limit_bytes=VMEM_BYTES),
        cost_estimate=pl.CostEstimate(
            flops=4 * rows * width * w + 10 * rows * rows * 2 * w * 2,
            bytes_accessed=10 * rows * width,
            transcendentals=rows * rows * w // 128,
        ),
        name="attention_backward",
    )(q, kd, vd, do, lse, h1, cos, sin, start, valid)


def tables(doc_lengths):
    lengths = doc_lengths.reshape(-1)
    places = jnp.arange(SEQUENCE_LENGTH, dtype=jnp.int32)
    ends = jnp.cumsum(lengths)
    passed = (places[:, None] >= ends[None, :]).astype(jnp.int32)
    start = jnp.sum(passed * lengths[None, :], axis=1)
    offsets = (places - start).astype(F32)
    step = jnp.arange(128, dtype=jnp.int32)
    frequencies = jnp.exp((step % 32).astype(F32) * (-2.0 * math.log(ROPE_BASE) / HD))
    angles = offsets[:, None] * frequencies[None, :]
    sine = jnp.sin(angles)
    return jnp.cos(angles), jnp.where(step[None, :] % HD < HD // 2, -sine, sine), start[:, None]


def whole_block(v):
    return pl.BlockSpec(v.shape, lambda *_: (0,) * len(v.shape))


def gate_table(h2, routes, wr, lane):
    mask = routes[:, 0:1] == lane
    for k in range(1, routes.shape[1]):
        mask = mask | (routes[:, k : k + 1] == lane)
    sel = jnp.where(mask, dot(h2[...], wr[...]), -jnp.inf)
    weight = jnp.exp(sel - jnp.max(sel, axis=1, keepdims=True))
    return weight / jnp.sum(weight, axis=1, keepdims=True)


def middle_body(x, own, other, gain, live, mid, h2, stats):
    attn = RESID_SCALE * (own[...].astype(F32) + other[...].astype(F32))
    m = x[...].astype(F32) + attn
    mid[...] = m
    r = lax.rsqrt(jnp.mean(m * m, axis=1, keepdims=True) + NORM_EPS)
    h2[...] = (m * r * gain[...].astype(F32)).astype(BF)
    v = live[...]
    total = jnp.sum(v * jnp.sum(attn * attn, axis=1, keepdims=True))
    lane = lax.broadcasted_iota(jnp.int32, stats.shape, 1)
    stats[...] = jnp.where(lane == 1, total, jnp.where(lane == 3, jnp.sum(v), 0.0))


def middle_norm(x, own, other, gain, live):
    rows, width = x.shape
    shape = jax.ShapeDtypeStruct
    return pl.pallas_call(
        middle_body,
        out_shape=[shape((rows, width), F32), shape((rows, width), BF), shape((8, 128), F32)],
        compiler_params=pltpu.CompilerParams(vmem_limit_bytes=VMEM_BYTES),
        cost_estimate=pl.CostEstimate(flops=10 * rows * width, bytes_accessed=12 * rows * width, transcendentals=rows),
        name="middle_norm",
    )(x, own, other, gain, live)


def experts_body(nchunk, halves, rt, *refs):
    ids, h2, g, routes, wr = refs[:5]
    gus = refs[5 : 5 + nchunk]
    downs = refs[5 + nchunk : 5 + 2 * nchunk]
    moe, dx, dgt, gat, dgu = refs[5 + 2 * nchunk : 10 + 2 * nchunk]
    gates, dgacc, macc, xacc, gbuf, dbuf, sem = refs[10 + 2 * nchunk :]
    c = pl.program_id(0)
    rows = h2.shape[0]
    f = gbuf.shape[3]
    lane = lax.broadcasted_iota(jnp.int32, (rows, 128), 1)

    def copies(k, slot):
        return (
            pltpu.make_async_copy(gus[k], gbuf.at[slot], sem.at[slot, 0]),
            pltpu.make_async_copy(downs[k], dbuf.at[slot], sem.at[slot, 1]),
        )

    @pl.when(c == 0)
    def _():
        for copy in copies(0, 0):
            copy.start()
        gates[...] = gate_table(h2, routes, wr, lane)
        dgacc[...] = jnp.zeros_like(dgacc)
        macc[...] = jnp.zeros_like(macc)
        xacc[...] = jnp.zeros_like(xacc)

    for k in range(1, nchunk):

        @pl.when(c + 1 == k)
        def _(k=k):
            for copy in copies(k, k % 2):
                copy.start()

    slot = lax.rem(c, 2)
    for copy in copies(0, slot):
        copy.wait()
    r = c // halves
    e = ids[r]
    ln = lane[:rt]
    for i in range(rows // rt):
        rs = pl.ds(i * rt, rt)
        hb = h2[rs, :]
        gp = dot(hb, gbuf[slot, 0])
        up = dot(hb, gbuf[slot, 1])
        u = dot_nt(g[rs, :], dbuf[slot])
        gate = jnp.sum(jnp.where(ln == e, gates[rs, :], 0.0), axis=1, keepdims=True)
        sg = jax.nn.sigmoid(gp)
        sl = gp * sg
        act = sl * up
        ga = (gate * act).astype(BF)
        dgacc[rs, :] += jnp.where(ln == r, jnp.sum(act * u, axis=1, keepdims=True) * RESID_SCALE, 0.0)
        da = (RESID_SCALE * gate) * u
        dgp = (da * up * (sg + sl * (1.0 - sg))).astype(BF)
        dup = (da * sl).astype(BF)
        gat[0, :, rs] = ga.T
        dgu[0, rs, :f] = dgp
        dgu[0, rs, f:] = dup
        macc[rs, :] += dot(ga, dbuf[slot])
        xacc[rs, :] += dot_nt(dgp, gbuf[slot, 0]) + dot_nt(dup, gbuf[slot, 1])

    @pl.when(c == nchunk - 1)
    def _():
        moe[...] = macc[...].astype(BF)
        dx[...] = xacc[...].astype(BF)
        dgt[...] = dgacc[...].T[: dgt.shape[0]]


def experts(ids, h2, g, routes, wr, gus, downs, halves):
    rows, width = h2.shape
    nchunk = len(gus)
    f = gus[0].shape[2]
    deep = 8 * -(-nchunk // halves // 8)
    shape = jax.ShapeDtypeStruct
    return pl.pallas_call(
        functools.partial(experts_body, nchunk, halves, min(rows, 512)),
        grid_spec=pltpu.PrefetchScalarGridSpec(
            num_scalar_prefetch=1,
            grid=(nchunk,),
            in_specs=[whole_block(v) for v in (h2, g, routes, wr)]
            + [pl.BlockSpec(memory_space=pl.ANY)] * (2 * nchunk),
            out_specs=[
                pl.BlockSpec((rows, width), lambda c, _: (0, 0)),
                pl.BlockSpec((rows, width), lambda c, _: (0, 0)),
                pl.BlockSpec((deep, rows), lambda c, _: (0, 0)),
                pl.BlockSpec((1, f, rows), lambda c, _: (c, 0, 0)),
                pl.BlockSpec((1, rows, 2 * f), lambda c, _: (c, 0, 0)),
            ],
            scratch_shapes=[
                pltpu.VMEM((rows, 128), F32),
                pltpu.VMEM((rows, 128), F32),
                pltpu.VMEM((rows, width), F32),
                pltpu.VMEM((rows, width), F32),
                pltpu.VMEM((2, 2, width, f), BF),
                pltpu.VMEM((2, f, width), BF),
                pltpu.SemaphoreType.DMA((2, 2)),
            ],
        ),
        out_shape=[
            shape((rows, width), BF),
            shape((rows, width), BF),
            shape((deep, rows), F32),
            shape((nchunk, f, rows), BF),
            shape((nchunk, rows, 2 * f), BF),
        ],
        compiler_params=pltpu.CompilerParams(vmem_limit_bytes=VMEM_BYTES),
        cost_estimate=pl.CostEstimate(
            flops=12 * rows * width * f * nchunk,
            bytes_accessed=6 * nchunk * width * f + 12 * rows * width,
            transcendentals=rows * f * nchunk,
        ),
        name="experts",
    )(ids, h2, g, routes, wr, *gus, *downs)


def weight_grads_body(nb, *refs):
    h2 = refs[:nb]
    g = refs[nb : 2 * nb]
    gat = refs[2 * nb : 3 * nb]
    dgu = refs[3 * nb : 4 * nb]
    wgu, wd = refs[4 * nb :]
    f = wd.shape[1]
    acc = sum(dot_tn(h2[b][...], dgu[b][0]) for b in range(nb))
    wgu[0, 0] = acc[:, :f].astype(BF)
    wgu[0, 1] = acc[:, f:].astype(BF)
    acc = sum(dot(gat[b][0], g[b][...]) for b in range(nb))
    wd[0] = (acc * RESID_SCALE).astype(BF)


def weight_grads(h2s, gs, gats, dgus, first, count):
    nb = len(h2s)
    rows, width = h2s[0].shape
    f = gats[0].shape[1]
    shape = jax.ShapeDtypeStruct
    return pl.pallas_call(
        functools.partial(weight_grads_body, nb),
        grid=(count,),
        in_specs=[whole_block(v) for v in (*h2s, *gs)]
        + [pl.BlockSpec((1, f, rows), lambda c: (first + c, 0, 0))] * nb
        + [pl.BlockSpec((1, rows, 2 * f), lambda c: (first + c, 0, 0))] * nb,
        out_specs=[
            pl.BlockSpec((1, 2, width, f), lambda c: (c, 0, 0, 0)),
            pl.BlockSpec((1, f, width), lambda c: (c, 0, 0)),
        ],
        out_shape=[shape((count, 2, width, f), BF), shape((count, f, width), BF)],
        compiler_params=pltpu.CompilerParams(vmem_limit_bytes=VMEM_BYTES),
        cost_estimate=pl.CostEstimate(
            flops=6 * rows * nb * width * f * count,
            bytes_accessed=6 * count * width * f + 4 * rows * nb * width,
            transcendentals=0,
        ),
        name="expert_weight_grads",
    )(*h2s, *gs, *gats, *dgus)


def middle_back_body(nb, nlocal, nexp, *refs):
    ids, h2, mid, gain, routes, wr = refs[:6]
    dxs = refs[6 : 6 + nb]
    dgts = refs[6 + nb : 6 + 2 * nb]
    gm, small = refs[6 + 2 * nb :]
    rows = h2.shape[0]
    lane = lax.broadcasted_iota(jnp.int32, (rows, 128), 1)
    gates = gate_table(h2, routes, wr, lane)
    dgate = jnp.zeros((rows, 128), F32)
    for b in range(nb):
        cols = dgts[b][...].T
        for r in range(nlocal):
            dgate = jnp.where(lane == ids[b * nlocal + r], cols[:, r : r + 1], dgate)
    dsel = gates * (dgate - jnp.sum(gates * dgate, axis=1, keepdims=True))
    high = dsel.astype(BF)
    rest = (dsel - high.astype(F32)).astype(BF)
    small[:nexp, :] = (dot_tn(high, h2[...]) + dot_tn(rest, h2[...]))[:nexp]
    dh = dot_nt(high, wr[...]) + dot_nt(rest, wr[...])
    for b in range(nb):
        dh = dh + dxs[b][...].astype(F32)
    m = mid[...]
    r2 = lax.rsqrt(jnp.mean(m * m, axis=1, keepdims=True) + NORM_EPS)
    xhat = m * r2
    small[nexp : nexp + 8, :] = jnp.broadcast_to(jnp.sum(dh * xhat, axis=0, keepdims=True), (8, dh.shape[1]))
    su = dh * gain[...].astype(F32)
    gm[...] = (r2 * (su - xhat * jnp.mean(su * xhat, axis=1, keepdims=True))).astype(BF)


def middle_back(ids, h2, mid, gain, routes, wr, dxs, dgts, nlocal, nexp):
    rows, width = h2.shape
    shape = jax.ShapeDtypeStruct
    args = (h2, mid, gain, routes, wr, *dxs, *dgts)
    return pl.pallas_call(
        functools.partial(middle_back_body, len(dxs), nlocal, nexp),
        in_specs=[pl.BlockSpec(memory_space=pltpu.SMEM)] + [pl.BlockSpec(memory_space=pltpu.VMEM)] * len(args),
        out_shape=[shape((rows, width), BF), shape((nexp + 8, width), F32)],
        compiler_params=pltpu.CompilerParams(vmem_limit_bytes=VMEM_BYTES),
        cost_estimate=pl.CostEstimate(flops=40 * rows * width, bytes_accessed=20 * rows * width, transcendentals=rows),
        name="middle_back",
    )(ids, *args)


def out_back_body(cot, gm, wo, o, do, gwo):
    rows = cot.shape[0]
    da = (RESID_SCALE * (cot[...].astype(F32) + gm[...].astype(F32))).astype(BF)
    do[...] = dot_nt(da, wo[...]).astype(BF)
    gwo[...] = dot_tn(o[...], da).astype(BF)


def out_back(cot, gm, wo, o):
    rows, width = cot.shape
    w = wo.shape[0]
    shape = jax.ShapeDtypeStruct
    return pl.pallas_call(
        out_back_body,
        out_shape=[shape((rows, w), BF), shape((w, width), BF)],
        compiler_params=pltpu.CompilerParams(vmem_limit_bytes=VMEM_BYTES),
        cost_estimate=pl.CostEstimate(flops=4 * rows * width * w, bytes_accessed=10 * rows * width, transcendentals=0),
        name="attention_out_back",
    )(cot, gm, wo, o)


def input_back_body(nq, x, wq, wkv, *refs):
    dq = refs[:nq]
    dkv = refs[nq : 2 * nq]
    dh, ga = refs[2 * nq :]
    xb = x[...].astype(F32)
    xhat = xb * lax.rsqrt(jnp.mean(xb * xb, axis=1, keepdims=True) + NORM_EPS)
    acc = None
    for w, parts in ((wq, dq), (wkv, dkv)):
        at = 0
        for part in parts:
            n = part.shape[1]
            term = dot_nt(part[...], w[:, at : at + n])
            acc = term if acc is None else acc + term
            at += n
    dh[...] = acc.astype(BF)
    ga[...] = jnp.broadcast_to(jnp.sum(acc * xhat, axis=0, keepdims=True), ga.shape)


def input_back(x, wq, wkv, dqs, dkvs):
    rows, width = x.shape
    shape = jax.ShapeDtypeStruct
    return pl.pallas_call(
        functools.partial(input_back_body, len(dqs)),
        out_shape=[shape((rows, width), BF), shape((8, width), F32)],
        compiler_params=pltpu.CompilerParams(vmem_limit_bytes=VMEM_BYTES),
        cost_estimate=pl.CostEstimate(
            flops=4 * rows * width * wq.shape[1], bytes_accessed=10 * rows * width, transcendentals=rows
        ),
        name="input_back",
    )(x, wq, wkv, *dqs, *dkvs)


def token_grads_body(x, cot, gm, own, other, gain, out):
    xb = x[...].astype(F32)
    r = lax.rsqrt(jnp.mean(xb * xb, axis=1, keepdims=True) + NORM_EPS)
    xhat = xb * r
    su = (own[...].astype(F32) + other[...].astype(F32)) * gain[...].astype(F32)
    norm = r * (su - xhat * jnp.mean(su * xhat, axis=1, keepdims=True))
    out[...] = cot[...].astype(F32) + gm[...].astype(F32) + norm


def token_grads(x, cot, gm, own, other, gain):
    rows, width = x.shape
    rt = min(rows, 128)
    block = pl.BlockSpec((rt, width), lambda i: (i, 0))
    return pl.pallas_call(
        token_grads_body,
        grid=(rows // rt,),
        in_specs=[block] * 5 + [whole_block(gain)],
        out_specs=block,
        out_shape=jax.ShapeDtypeStruct((rows, width), F32),
        cost_estimate=pl.CostEstimate(flops=12 * rows * width, bytes_accessed=14 * rows * width, transcendentals=rows),
        name="token_grads",
    )(x, cot, gm, own, other, gain)


def layer_out_body(nb, *refs):
    mid, live = refs[:2]
    moes = refs[2 : 2 + nb]
    out, stats = refs[2 + nb :]
    moe = sum(m[...].astype(F32) for m in moes) * RESID_SCALE
    outf = mid[...] + moe
    out[...] = outf.astype(BF)
    v = live[...]
    s0 = jnp.sum(v * jnp.sum(outf * outf, axis=1, keepdims=True))
    s2 = jnp.sum(v * jnp.sum(moe * moe, axis=1, keepdims=True))
    lane = lax.broadcasted_iota(jnp.int32, stats.shape, 1)
    stats[...] = jnp.where(lane == 0, s0, jnp.where(lane == 2, s2, 0.0))


def layer_out_share(mid, live, moes):
    rows, width = mid.shape
    shape = jax.ShapeDtypeStruct
    return pl.pallas_call(
        functools.partial(layer_out_body, len(moes)),
        out_shape=[shape((rows, width), BF), shape((8, 128), F32)],
        compiler_params=pltpu.CompilerParams(vmem_limit_bytes=VMEM_BYTES),
        cost_estimate=pl.CostEstimate(flops=12 * rows * width, bytes_accessed=14 * rows * width, transcendentals=0),
        name="layer_out",
    )(mid, live, *moes)


def on_device(
    tokens,
    gain_attn,
    query_weight_matrix,
    key_value_weight,
    w_out,
    gain_ffn,
    w_router,
    w_gate_up,
    w_down,
    routes,
    doc_lengths,
    valid_mask,
    cotangent,
):
    rows, width = tokens.shape
    share = routes.shape[0]
    n_ep, n_tp = lax.axis_size("ep"), lax.axis_size("tp")
    nexp = w_router.shape[1]
    inner = math.gcd(n_ep, 4)
    outer = n_ep // inner
    me, core = lax.axis_index("ep"), lax.axis_index("tp")
    me_in, me_out = me % inner, me // inner
    begin = core * share

    def across(v, k):
        return lax.ppermute(v, "ep", [(i, i ^ k) for i in range(n_ep)])

    def along(v, k):
        return lax.ppermute(v, "ep", [(i, (i + k * inner) % n_ep) for i in range(n_ep)])

    def swap(v):
        return lax.ppermute(v, "tp", [(0, 1), (1, 0)])

    def plane(v):
        return [v] + [across(v, k) for k in range(1, inner)]

    def cut(v, at, size):
        return lax.dynamic_slice_in_dim(v, at, size)

    def total(terms):
        acc = terms[0].astype(F32)
        for term in terms[1:]:
            acc = acc + term.astype(F32)
        return acc

    def core_rows(v):
        if n_tp != 2:
            return lax.all_gather(v, "tp", axis=0, tiled=True)
        other = swap(v)
        return jnp.where(core == 0, jnp.concatenate([v, other]), jnp.concatenate([other, v]))

    def sum_small(v):
        v = total(plane(v))
        v = total([v] + [along(v, k) for k in range(1, outer)])
        return v + swap(v) if n_tp == 2 else lax.psum(v, "tp")

    def sum_ep(v):
        size = v.shape[0] // inner
        part = total(
            [cut(v, me_in * size, size)]
            + [across(cut(v, (me_in ^ k) * size, size), k) for k in range(1, inner)]
        ).astype(BF)
        small = size // outer
        mine = total(
            [cut(part, me_out * small, small)]
            + [along(cut(part, (me_out + k) % outer * small, small), k) for k in range(1, outer)]
        ).astype(BF)
        part = lax.dynamic_update_slice_in_dim(jnp.zeros_like(part), mine, me_out * small, 0)
        for k in range(1, outer):
            part = lax.dynamic_update_slice_in_dim(part, along(mine, k), (me_out - k) % outer * small, 0)
        v = lax.dynamic_update_slice_in_dim(jnp.zeros_like(v), part, me_in * size, 0)
        for k in range(1, inner):
            v = lax.dynamic_update_slice_in_dim(v, across(part, k), (me_in ^ k) * size, 0)
        return v

    def column(v):
        held = [v]
        for _ in range(1, outer):
            held.append(along(held[-1], 1))
        return held

    gus, downs = [], []
    for gu, down in zip(column(w_gate_up[0]), column(w_down[0]), strict=True):
        if n_tp == 2:
            gus += [gu, swap(gu)]
            downs += [down, swap(down)]
        else:
            gus.append(lax.all_gather(gu, "tp", axis=2, tiled=True))
            downs.append(lax.all_gather(down, "tp", axis=0, tiled=True))
    halves = 2 if n_tp == 2 else 1
    gs = plane(cut(cotangent, begin, share))
    routes_all = plane(routes)
    local = jnp.arange(outer, dtype=jnp.int32) * inner
    ids = (me - local) % n_ep
    ids_all = jnp.concatenate([((me ^ k) - local) % n_ep for k in range(inner)])

    cos, sin, start = tables(doc_lengths)
    valid_row = valid_mask[None, :]
    live = cut(valid_mask, begin, share).astype(F32)[:, None]
    gain_a, gain_f = gain_attn[None, :], gain_ffn[None, :]
    wr = jnp.pad(w_router, ((0, 0), (0, 128 - nexp)))

    h1, q, kd, vd, o, lse, part = attn_forward(
        tokens, gain_a, query_weight_matrix, key_value_weight, w_out, cos, sin, start, valid_row
    )
    if n_tp == 2:
        own, other = cut(part, begin, share), swap(cut(part, (1 - core) * share, share))
    else:
        own = lax.psum_scatter(part.astype(F32), "tp", scatter_dimension=0, tiled=True)
        other = jnp.zeros_like(own)
    mid, h2, stats = middle_norm(cut(tokens, begin, share), own, other, gain_f, live)
    h2s = plane(h2)

    moes, dxs, dgts, gats, dgus = [], [], [], [], []
    for k in range(inner):
        moe, dx, dgt, gat, dgu = experts(ids, h2s[k], gs[k], routes_all[k], wr, gus, downs, halves)
        moes.append(moe if k == 0 else across(moe, k))
        dxs.append(dx if k == 0 else across(dx, k))
        dgts.append(dgt if k == 0 else across(dgt, k))
        gats.append(gat)
        dgus.append(dgu)

    def expert_grads(r):
        dgu_w, down_w = weight_grads(h2s, gs, gats, dgus, r * halves, halves)
        if n_tp == 2:
            return total([dgu_w[0], swap(dgu_w[1])]), total([down_w[0], swap(down_w[1])])
        return (
            lax.psum_scatter(dgu_w[0].astype(F32), "tp", scatter_dimension=2, tiled=True),
            lax.psum_scatter(down_w[0].astype(F32), "tp", scatter_dimension=0, tiled=True),
        )

    sums = expert_grads(1 % outer)
    for r in range(2, outer + 1):
        sent = [along(v.astype(BF), 1) for v in sums]
        sums = [a.astype(F32) + b for a, b in zip(sent, expert_grads(r % outer), strict=True)]
    grad_w_gate_up, grad_w_down = sums[0][None], sums[1][None]

    gm_share, small = middle_back(ids_all, h2, mid, gain_f, routes, wr, dxs, dgts, outer, nexp)
    gm = core_rows(gm_share)
    small_sum = sum_small(small)
    do, gwo = out_back(cotangent, gm, w_out, o)
    out_sum = sum_ep(gwo)
    out_share, stats_out = layer_out_share(mid, live, moes)
    layer_out = core_rows(out_share)

    nkv = kd.shape[1] // 128
    groups = 2 if nkv % 2 == 0 else 1
    each = nkv // groups
    dqs, dkvs, gws = [], [], []
    for n in range(groups):
        dq, dkv, gw = attn_backward(n * each, each, q, kd, vd, do, lse, h1, cos, sin, start, valid_row)
        dqs.append(dq)
        dkvs.append(dkv)
        gws.append(sum_ep(gw))
    dh1, ga_part = input_back(tokens, query_weight_matrix, key_value_weight, dqs, dkvs)
    if n_tp == 2:
        dh_other = swap(dh1)
    else:
        dh1, dh_other = lax.psum(dh1.astype(F32), "tp"), jnp.zeros_like(dh1)
    grad_tokens = token_grads(tokens, cotangent, gm, dh1, dh_other, gain_a)
    last = jnp.concatenate([ga_part[:1], jnp.pad((stats + stats_out)[:1], ((0, 0), (0, width - 128)))])
    last_sum = sum_small(last)
    s = last_sum[1]
    w = each * 128
    return (
        layer_out,
        grad_tokens,
        last_sum[0],
        jnp.concatenate([v[:, :w] for v in gws], axis=1).astype(F32),
        jnp.concatenate([v[:, w:] for v in gws], axis=1).astype(F32),
        out_sum.astype(F32),
        small_sum[nexp],
        small_sum[:nexp].T,
        grad_w_gate_up,
        grad_w_down,
        jnp.sqrt(s[:3] / (s[3] * width)),
    )


def solution(mesh):
    return jax.shard_map(
        on_device,
        mesh=mesh,
        in_specs=(
            P("ep", None),
            P(),
            P(None, "tp"),
            P(None, "tp"),
            P("tp", None),
            P(),
            P(),
            P("ep", None, None, "tp"),
            P("ep", "tp", None),
            P(("ep", "tp"), None),
            P("ep", None),
            P("ep"),
            P("ep", None),
        ),
        out_specs=(
            P("ep", None),
            P("ep", None),
            P(),
            P(None, "tp"),
            P(None, "tp"),
            P("tp", None),
            P(),
            P(),
            P("ep", None, None, "tp"),
            P("ep", "tp", None),
            P(),
        ),
        check_vma=False,
    )
```

```python
import functools
import math

import jax
import jax.numpy as jnp
from jax import lax
from jax.experimental import pallas as pl
from jax.experimental.pallas import tpu as pltpu
from jax.sharding import PartitionSpec as P

SEQUENCE_LENGTH = 1024
WINDOW = 1024
ATTN_SCALE = 0.015625
RESID_SCALE = 0.22
TOPK = 8
NORM_EPS = 1e-06
ROPE_BASE = 10000.0
F32 = jnp.float32
BF = jnp.bfloat16
VMEM_BYTES = 60 * 1024 * 1024
COST = 0.02
GAIN_F, GAIN_A, STATS = 64, 65, 66


def cost(flops, bytes_accessed, transcendentals=0):
    return pl.CostEstimate(
        flops=int(COST * flops), bytes_accessed=int(COST * bytes_accessed), transcendentals=int(COST * transcendentals)
    )


def dot(a, b):
    return jnp.dot(a, b, preferred_element_type=F32)


def dot_nt(a, b):
    return lax.dot_general(a, b, (((1,), (1,)), ((), ())), preferred_element_type=F32)


def dot_tn(a, b):
    return lax.dot_general(a, b, (((0,), (0,)), ((), ())), preferred_element_type=F32)


def whole_block(v):
    return pl.BlockSpec(v.shape, lambda *_: (0,) * len(v.shape))


def gate_table(h2, pay, wr):
    rows = h2.shape[0]
    lane = lax.broadcasted_iota(jnp.int32, (rows, 128), 1).astype(F32)
    routes = pay[rows : rows + 16, :rows].astype(F32).T
    mask = routes[:, 0:1] == lane
    for k in range(1, TOPK):
        mask = mask | (routes[:, k : k + 1] == lane)
    sel = jnp.where(mask, dot(h2[...], wr[...]), -jnp.inf)
    weight = jnp.exp(sel - jnp.max(sel, axis=1, keepdims=True))
    return weight / jnp.sum(weight, axis=1, keepdims=True)


def middle_body(core, x, own, other, gain, live, mid, h2, stats):
    attn = RESID_SCALE * (own[...].astype(F32) + other[...].astype(F32))
    m = x[...].astype(F32) + attn
    mid[...] = m
    r = lax.rsqrt(jnp.mean(m * m, axis=1, keepdims=True) + NORM_EPS)
    h2[...] = (m * r * gain[...].astype(F32)).astype(BF)
    v = live[...]
    total = jnp.sum(v * jnp.sum(attn * attn, axis=1, keepdims=True))
    lane = lax.broadcasted_iota(jnp.int32, stats.shape, 1)
    stats[...] = jnp.where(lane == 1, total, jnp.where(lane == 3, jnp.sum(v), 0.0))


def middle_norm(core, x, own, other, gain, live):
    share, width = own.shape
    shape = jax.ShapeDtypeStruct
    part = lambda n: pl.BlockSpec((share, n), lambda _, c: (c[0], 0))
    full = lambda *s: pl.BlockSpec(s, lambda *_: (0, 0))
    return pl.pallas_call(
        middle_body,
        grid_spec=pltpu.PrefetchScalarGridSpec(
            num_scalar_prefetch=1,
            grid=(1,),
            in_specs=[part(width), whole_block(own), whole_block(other), whole_block(gain), part(1)],
            out_specs=[full(share, width), full(share, width), full(8, 128)],
        ),
        out_shape=[shape((share, width), F32), shape((share, width), BF), shape((8, 128), F32)],
        compiler_params=pltpu.CompilerParams(vmem_limit_bytes=VMEM_BYTES),
        cost_estimate=cost(10 * share * width, 12 * share * width),
        name="middle_norm",
    )(core, x, own, other, gain, live)


def experts_body(nb, nchunk, halves, first, carried, *refs):
    ids = refs[0]
    at = 1
    h2s, pays = refs[at : at + nb], refs[at + nb : at + 2 * nb]
    at += 2 * nb
    prevs = [None] * nb
    if carried:
        prevs = [refs[at + 2 * b : at + 2 * b + 2] for b in range(nb)]
        at += 2 * nb
    wr = refs[at]
    packs = refs[at + 1 : at + 1 + nchunk]
    at += 1 + nchunk
    outs = [refs[at + 4 * b : at + 4 * b + 4] for b in range(nb)]
    at += 4 * nb
    gates, dgacc, macc, xacc, buf, sem = refs[at:]
    c = pl.program_id(0)
    rows, width = h2s[0].shape
    f = buf.shape[3]
    lane = lax.broadcasted_iota(jnp.int32, (rows, 128), 1)

    @pl.when(c == 0)
    def _():
        pltpu.make_async_copy(packs[0], buf.at[0], sem.at[0]).start()
        for b in range(nb):
            gates[b] = gate_table(h2s[b], pays[b], wr)
            if carried:
                macc[b] = prevs[b][1][...].astype(F32)
                xacc[b] = prevs[b][0][:rows, :].astype(F32)
            else:
                macc[b] = jnp.zeros((rows, width), F32)
                xacc[b] = jnp.zeros((rows, width), F32)
        dgacc[...] = jnp.zeros_like(dgacc)

    for k in range(1, nchunk):

        @pl.when(c + 1 == k)
        def _(k=k):
            pltpu.make_async_copy(packs[k], buf.at[k % 2], sem.at[k % 2]).start()

    slot = lax.rem(c, 2)
    pltpu.make_async_copy(packs[0], buf.at[slot], sem.at[slot]).wait()
    r = first + c // halves
    e = ids[r]
    nd = width // f
    for b in range(nb):
        g, gat, dgu = pays[b], outs[b][2], outs[b][3]
        hb = h2s[b][...]
        gp = dot(hb, buf[slot, 0])
        up = dot(hb, buf[slot, 1])
        u = sum(dot_nt(g[:rows, k * f : (k + 1) * f], buf[slot, 2, k * f : (k + 1) * f, :]) for k in range(nd))
        gate = jnp.sum(jnp.where(lane == e, gates[b], 0.0), axis=1, keepdims=True)
        sg = jax.nn.sigmoid(gp)
        sl = gp * sg
        act = sl * up
        ga = (gate * act).astype(BF)
        dgacc[b] += jnp.where(lane == r, jnp.sum(act * u, axis=1, keepdims=True) * RESID_SCALE, 0.0)
        da = (RESID_SCALE * gate) * u
        dgp = (da * up * (sg + sl * (1.0 - sg))).astype(BF)
        dup = (da * sl).astype(BF)
        gat[0] = ga.T
        dgu[0, :, :f] = dgp
        dgu[0, :, f:] = dup
        for k in range(nd):
            macc[b, :, k * f : (k + 1) * f] += dot(ga, buf[slot, 2, k * f : (k + 1) * f, :])
        xacc[b] += dot_nt(dgp, buf[slot, 0]) + dot_nt(dup, buf[slot, 1])

    @pl.when(c == nchunk - 1)
    def _():
        for b in range(nb):
            dx, moe = outs[b][:2]
            moe[...] = macc[b].astype(BF)
            dx[:rows, :] = xacc[b].astype(BF)
            dg = dgacc[b].T[:8]
            high = dg.astype(BF).astype(F32)
            tail = jnp.concatenate([high, dg - high], axis=0)
            if carried:
                row = lax.broadcasted_iota(jnp.int32, (16, rows), 0) % 8
                mine = (row >= first) & (row < first + nchunk // halves)
                tail = jnp.where(mine, tail, prevs[b][0][rows:, :rows].astype(F32))
            dx[rows:, :] = jnp.zeros((16, width), BF)
            dx[rows:, :rows] = tail.astype(BF)


def experts(ids, h2s, pays, prevs, wr, packs, halves, first):
    rows, width = h2s[0].shape
    nb, nchunk = len(h2s), len(packs)
    f = packs[0].shape[2]
    carried = prevs is not None
    flat = [v for prev in prevs for v in prev] if carried else []
    shape = jax.ShapeDtypeStruct
    once = lambda v: pl.BlockSpec(v.shape, lambda *_: (0,) * len(v.shape), pipeline_mode=pl.Buffered(1))
    out = pl.pallas_call(
        functools.partial(experts_body, nb, nchunk, halves, first, carried),
        grid_spec=pltpu.PrefetchScalarGridSpec(
            num_scalar_prefetch=1,
            grid=(nchunk,),
            in_specs=[once(v) for v in (*h2s, *pays, *flat, wr)] + [pl.BlockSpec(memory_space=pl.ANY)] * nchunk,
            out_specs=[
                pl.BlockSpec((rows + 16, width), lambda c, _: (0, 0)),
                pl.BlockSpec((rows, width), lambda c, _: (0, 0)),
                pl.BlockSpec((1, f, rows), lambda c, _: (c, 0, 0)),
                pl.BlockSpec((1, rows, 2 * f), lambda c, _: (c, 0, 0)),
            ]
            * nb,
            scratch_shapes=[
                pltpu.VMEM((nb, rows, 128), F32),
                pltpu.VMEM((nb, rows, 128), F32),
                pltpu.VMEM((nb, rows, width), F32),
                pltpu.VMEM((nb, rows, width), F32),
                pltpu.VMEM((2, 3, width, f), BF),
                pltpu.SemaphoreType.DMA((2,)),
            ],
        ),
        out_shape=[
            shape((rows + 16, width), BF),
            shape((rows, width), BF),
            shape((nchunk, f, rows), BF),
            shape((nchunk, rows, 2 * f), BF),
        ]
        * nb,
        compiler_params=pltpu.CompilerParams(vmem_limit_bytes=VMEM_BYTES),
        cost_estimate=cost(12 * rows * width * f * nchunk * nb, 6 * nchunk * width * f + 12 * rows * width * nb),
        name="experts",
    )(ids, *h2s, *pays, *flat, wr, *packs)
    return [out[4 * b : 4 * b + 4] for b in range(nb)]


def weight_grads_body(nb, halves, _, *refs):
    h2 = refs[:nb]
    g = refs[nb : 2 * nb]
    hidden, outs = refs[2 * nb : -halves], refs[-halves:]
    e, c = pl.program_id(0), pl.program_id(1)
    rows = h2[0].shape[0]
    width, f = outs[0].shape[2:]
    for n in range(len(hidden) // (2 * nb)):

        @pl.when(e == n)
        def _(n=n):
            gat, dgu = hidden[2 * nb * n : 2 * nb * n + nb], hidden[2 * nb * n + nb : 2 * nb * (n + 1)]
            acc = sum(dot_tn(h2[b][...], dgu[b][0]) for b in range(nb))
            down = sum(dot(gat[b][0], g[b][:rows, :]) for b in range(nb)) * RESID_SCALE
            for half in range(halves):

                @pl.when(c == half)
                def _(out=outs[half]):
                    out[0, 0] = acc[:, :f].astype(BF)
                    out[0, 1] = acc[:, f:].astype(BF)
                    for k in range(width // f):
                        out[0, 2, k * f : (k + 1) * f, :] = down[:, k * f : (k + 1) * f].astype(BF)


def weight_grads(tok, h2s, pays, saved, halves):
    nb, ne = len(h2s), len(saved[0])
    rows, width = h2s[0].shape
    f = saved[0][0][0].shape[1]
    shape = jax.ShapeDtypeStruct
    once = lambda v: pl.BlockSpec(v.shape, lambda *_: (0,) * len(v.shape), pipeline_mode=pl.Buffered(1))
    specs, args = [], []
    for n in range(ne):
        half = lambda e, c, n=n: jnp.where(e < n, 0, jnp.where(e == n, c, halves - 1))
        for j, block in ((0, (1, f, rows)), (1, (1, rows, 2 * f))):
            for b in range(nb):
                args.append(saved[b][n][j])
                specs.append(pl.BlockSpec(block, lambda e, c, o=saved[b][n][2], half=half: (o + half(e, c), 0, 0)))
    return pl.pallas_call(
        functools.partial(weight_grads_body, nb, halves),
        grid=(ne, halves),
        in_specs=[pl.BlockSpec(memory_space=pltpu.SMEM)] + [once(v) for v in (*h2s, *pays)] + specs,
        out_specs=[pl.BlockSpec((1, 3, width, f), lambda e, c: (e, 0, 0, 0))] * halves,
        out_shape=[shape((ne, 3, width, f), BF)] * halves,
        compiler_params=pltpu.CompilerParams(vmem_limit_bytes=VMEM_BYTES),
        cost_estimate=cost(6 * rows * nb * width * f * halves, 6 * halves * width * f + 4 * rows * nb * width),
        name="expert_weight_grads",
    )(tok, *h2s, *pays, *args)


def middle_back_body(nb, nlocal, _, *refs):
    ids, h2, mid, gain, pay, wr = refs[:6]
    dxs = refs[6 : 6 + nb]
    gm, small = refs[6 + nb :]
    rows, width = h2.shape
    lane = lax.broadcasted_iota(jnp.int32, (rows, 128), 1)
    gates = gate_table(h2, pay, wr)
    dgate = jnp.zeros((rows, 128), F32)
    for b in range(nb):
        tail = dxs[b][rows:, :rows].astype(F32)
        cols = (tail[:8] + tail[8:]).T
        for r in range(nlocal):
            dgate = jnp.where(lane == ids[b * nlocal + r], cols[:, r : r + 1], dgate)
    dsel = gates * (dgate - jnp.sum(gates * dgate, axis=1, keepdims=True))
    high = dsel.astype(BF)
    rest = (dsel - high.astype(F32)).astype(BF)
    router = dot_tn(h2[...], high) + dot_tn(h2[...], rest)
    dh = dot_nt(high, wr[...]) + dot_nt(rest, wr[...])
    for b in range(nb):
        dh = dh + dxs[b][:rows, :].astype(F32)
    m = mid[...]
    r2 = lax.rsqrt(jnp.mean(m * m, axis=1, keepdims=True) + NORM_EPS)
    xhat = m * r2
    col = jnp.broadcast_to(jnp.sum(dh * xhat, axis=0, keepdims=True), (8, width)).T[:, :1]
    small[...] = jnp.where(lax.broadcasted_iota(jnp.int32, (width, 128), 1) == GAIN_F, col, router)
    su = dh * gain[...].astype(F32)
    gm[...] = (r2 * (su - xhat * jnp.mean(su * xhat, axis=1, keepdims=True))).astype(BF)


def middle_back(tok, ids, h2, mid, gain, pay, wr, dxs, nlocal):
    rows, width = h2.shape
    shape = jax.ShapeDtypeStruct
    args = (h2, mid, gain, pay, wr, *dxs)
    return pl.pallas_call(
        functools.partial(middle_back_body, len(dxs), nlocal),
        in_specs=[pl.BlockSpec(memory_space=pltpu.SMEM)] * 2 + [pl.BlockSpec(memory_space=pltpu.VMEM)] * len(args),
        out_shape=[shape((rows, width), BF), shape((width, 128), F32)],
        compiler_params=pltpu.CompilerParams(vmem_limit_bytes=VMEM_BYTES),
        cost_estimate=cost(40 * rows * width, 20 * rows * width),
        name="middle_back",
    )(tok, ids, *args)


def placed(core, parts, i, rt):
    if len(parts) == 1:
        return parts[0][i * rt : (i + 1) * rt, :].astype(F32)
    share = parts[0].shape[0]
    at = i * rt % share
    mine, other = (p[at : at + rt, :].astype(F32) for p in parts)
    return jnp.where(core[0] == i * rt // share, mine, other)


def out_back_body(core, cot, wo, o, *refs):
    parts, (do, gwo, da) = refs[:-3], refs[-3:]
    rows = cot.shape[0]
    rt = 256
    for i in range(rows // rt):
        rs = pl.ds(i * rt, rt)
        d = (RESID_SCALE * (cot[rs, :].astype(F32) + placed(core, parts, i, rt))).astype(BF)
        da[rs, :] = d
        do[rs, :] = dot_nt(d, wo[...]).astype(BF)
    gwo[...] = dot_tn(o[...], da[...]).astype(BF)


def out_back(core, cot, wo, o, parts):
    rows, width = cot.shape
    w = wo.shape[0]
    shape = jax.ShapeDtypeStruct
    return pl.pallas_call(
        out_back_body,
        in_specs=[pl.BlockSpec(memory_space=pltpu.SMEM)]
        + [pl.BlockSpec(memory_space=pltpu.VMEM)] * (3 + len(parts)),
        out_shape=[shape((rows, w), BF), shape((w, width), BF)],
        scratch_shapes=[pltpu.VMEM((rows, width), BF)],
        compiler_params=pltpu.CompilerParams(vmem_limit_bytes=VMEM_BYTES),
        cost_estimate=cost(4 * rows * width * w, 10 * rows * width),
        name="attention_out_back",
    )(core, cot, wo, o, *parts)


def input_back_body(nq, _, wq, wkv, *refs):
    dq = refs[:nq]
    dkv = refs[nq : 2 * nq]
    dh = refs[2 * nq]
    acc = None
    for w, parts in ((wq, dq), (wkv, dkv)):
        at = 0
        for part in parts:
            n = part.shape[1]
            term = dot_nt(part[...], w[:, at : at + n])
            acc = term if acc is None else acc + term
            at += n
    dh[...] = acc.astype(BF)


def input_back(tok, wq, wkv, dqs, dkvs):
    rows = dqs[0].shape[0]
    width = wq.shape[0]
    rt = 256
    nq = len(dqs)
    block = lambda n: pl.BlockSpec((rt, n), lambda i: (i, 0))
    return pl.pallas_call(
        functools.partial(input_back_body, nq),
        grid=(rows // rt,),
        in_specs=[pl.BlockSpec(memory_space=pltpu.SMEM), whole_block(wq), whole_block(wkv)] + [block(v.shape[1]) for v in (*dqs, *dkvs)],
        out_specs=block(width),
        out_shape=jax.ShapeDtypeStruct((rows, width), BF),
        compiler_params=pltpu.CompilerParams(vmem_limit_bytes=VMEM_BYTES),
        cost_estimate=cost(4 * rows * width * wq.shape[1], 10 * rows * width),
        name="input_back",
    )(tok, wq, wkv, *dqs, *dkvs)


def token_grads_body(npart, core, x, cot, own, other, gain, *refs):
    parts, out = refs[:npart], refs[npart]
    xb = x[...].astype(F32)
    r = lax.rsqrt(jnp.mean(xb * xb, axis=1, keepdims=True) + NORM_EPS)
    xhat = xb * r
    su = (own[...].astype(F32) + other[...].astype(F32)) * gain[...].astype(F32)
    norm = r * (su - xhat * jnp.mean(su * xhat, axis=1, keepdims=True))
    gm = parts[0][...].astype(F32)
    if npart == 2:
        half = pl.num_programs(0) // 2
        gm = jnp.where(core[0] == pl.program_id(0) // half, gm, parts[1][...].astype(F32))
    out[...] = cot[...].astype(F32) + gm + norm


def token_grads(core, x, cot, own, other, gain, parts):
    rows, width = x.shape
    rt = 128
    block = pl.BlockSpec((rt, width), lambda i, _: (i, 0))
    n = parts[0].shape[0] // rt
    part = pl.BlockSpec((rt, width), lambda i, _: (i % n, 0))
    return pl.pallas_call(
        functools.partial(token_grads_body, len(parts)),
        grid_spec=pltpu.PrefetchScalarGridSpec(
            num_scalar_prefetch=1,
            grid=(rows // rt,),
            in_specs=[block] * 4 + [whole_block(gain)] + [part] * len(parts),
            out_specs=block,
        ),
        out_shape=jax.ShapeDtypeStruct((rows, width), F32),
        compiler_params=pltpu.CompilerParams(vmem_limit_bytes=VMEM_BYTES),
        cost_estimate=cost(12 * rows * width, 14 * rows * width),
        name="token_grads",
    )(core, x, cot, own, other, gain, *parts)


def layer_out_body(nb, _, *refs):
    mid, live = refs[:2]
    moes = refs[2 : 2 + nb]
    out, stats = refs[2 + nb :]
    moe = sum(m[...].astype(F32) for m in moes) * RESID_SCALE
    outf = mid[...] + moe
    out[...] = outf.astype(BF)
    v = live[...]
    s0 = jnp.sum(v * jnp.sum(outf * outf, axis=1, keepdims=True))
    s2 = jnp.sum(v * jnp.sum(moe * moe, axis=1, keepdims=True))
    lane = lax.broadcasted_iota(jnp.int32, stats.shape, 1)

    @pl.when(pl.program_id(0) == 0)
    def _():
        stats[...] = jnp.zeros_like(stats)

    stats[...] += jnp.where(lane == 0, s0, jnp.where(lane == 2, s2, 0.0))


def layer_out_share(tok, mid, live, moes):
    rows, width = mid.shape
    shape = jax.ShapeDtypeStruct
    rt = 128
    block = lambda n: pl.BlockSpec((rt, n), lambda i: (i, 0))
    return pl.pallas_call(
        functools.partial(layer_out_body, len(moes)),
        grid=(rows // rt,),
        in_specs=[pl.BlockSpec(memory_space=pltpu.SMEM), block(width), block(1)] + [block(width)] * len(moes),
        out_specs=[block(width), pl.BlockSpec((8, 128), lambda i: (0, 0))],
        out_shape=[shape((rows, width), BF), shape((8, 128), F32)],
        compiler_params=pltpu.CompilerParams(vmem_limit_bytes=VMEM_BYTES),
        cost_estimate=cost(12 * rows * width, 14 * rows * width),
        name="layer_out",
    )(tok, mid, live, *moes)


def gather_rows_body(npart, cols, me, *refs):
    parts, outs = refs[: npart * len(cols)], refs[npart * len(cols) :]
    size = parts[0].shape[0]
    at = [0] * len(outs)
    for g, widths in enumerate(cols):
        begin = 0
        for j, w in enumerate(widths):
            if not w:
                continue
            for k in range(npart):
                rows = pl.ds(pl.multiple_of((me[0] ^ k) * size, size), size)
                outs[j][rows, at[j] : at[j] + w] = parts[g * npart + k][:, begin : begin + w].astype(F32)
            begin += w
            at[j] += w


def gather_rows(me, groups, cols):
    npart = len(groups[0])
    size = groups[0][0].shape[0]
    flat = [v for group in groups for v in group]
    widths = [sum(c[j] for c in cols) for j in range(len(cols[0]))]
    return pl.pallas_call(
        functools.partial(gather_rows_body, npart, cols),
        in_specs=[pl.BlockSpec(memory_space=pltpu.SMEM)] + [pl.BlockSpec(memory_space=pltpu.VMEM)] * len(flat),
        out_shape=[jax.ShapeDtypeStruct((npart * size, w), F32) for w in widths],
        compiler_params=pltpu.CompilerParams(vmem_limit_bytes=VMEM_BYTES),
        cost_estimate=cost(0, 6 * npart * size * sum(widths)),
        name="gather_rows",
    )(me, *flat)
HD = 64
NEG = -1e30
BLK = 256


def swap_halves(v, lane):
    return jnp.where(lane % HD < HD // 2, pltpu.roll(v, 128 - HD // 2, 1), pltpu.roll(v, HD // 2, 1))


def mask_bias(start, valid, i, keys):
    row = lax.broadcasted_iota(jnp.int32, (BLK, keys), 0) + i * BLK
    key = lax.broadcasted_iota(jnp.int32, (BLK, keys), 1)
    first = jnp.maximum(start, row[:, :1] - (WINDOW - 1))
    ok = (key >= first) & (key <= row) & ((valid[:, :keys] > 0) | (key == row))
    return jnp.where(ok, 0.0, NEG).astype(F32)


def doc_starts(lengths, place):
    start = jnp.zeros_like(place)
    end = 0
    for j in range(lengths.shape[1]):
        end = end + lengths[0, j]
        start = jnp.where(place >= end, end, start)
    return start


def prepare_body(core, gu, down, cot, routes, pack, pay):
    width, f = gu.shape[2:]
    share = cot.shape[0]
    pack[:2] = gu[0]
    for k in range(width // f):
        pack[2, k * f : (k + 1) * f, :] = down[0, :, k * f : (k + 1) * f]
    pay[:share, :] = cot[...]
    pay[share:, :] = jnp.zeros((pay.shape[0] - share, width), BF)
    pay[share : share + routes.shape[0], :share] = routes[...].astype(F32).astype(BF)


def prepare(core, gu, down, cot, routes):
    width, f = gu.shape[2:]
    share = routes.shape[1]
    shape = jax.ShapeDtypeStruct
    return pl.pallas_call(
        prepare_body,
        grid_spec=pltpu.PrefetchScalarGridSpec(
            num_scalar_prefetch=1,
            grid=(1,),
            in_specs=[
                whole_block(gu),
                whole_block(down),
                pl.BlockSpec((share, width), lambda _, c: (c[0], 0)),
                whole_block(routes),
            ],
            out_specs=[
                pl.BlockSpec((3, width, f), lambda *_: (0, 0, 0)),
                pl.BlockSpec((share + 16, width), lambda *_: (0, 0)),
            ],
        ),
        out_shape=[shape((3, width, f), BF), shape((share + 16, width), BF)],
        compiler_params=pltpu.CompilerParams(vmem_limit_bytes=VMEM_BYTES),
        cost_estimate=cost(0, 12 * width * f),
        name="prepare",
    )(core, gu, down, cot, routes)


def attn_forward_body(core, lengths, x, gain, wq, wkv, wo, valid, h1, q, kd, vd, o, lse, cos, sin, own, *rest):
    nkv = wkv.shape[1] // 128
    lane = lax.broadcasted_iota(jnp.int32, (BLK, 128), 1)
    low = lane < HD
    ga = gain[...].astype(F32)
    frequencies = jnp.exp((lane[:1] % (HD // 2)).astype(F32) * (-2.0 * math.log(ROPE_BASE) / HD))
    half = own.shape[0]
    for i in range(x.shape[0] // BLK):
        rs = pl.ds(i * BLK, BLK)
        keys = (i + 1) * BLK
        place = lax.broadcasted_iota(jnp.int32, (BLK, 1), 0) + i * BLK
        start = doc_starts(lengths, place)
        angles = (place - start).astype(F32) * frequencies
        cb = jnp.cos(angles)
        sb = jnp.sin(angles)
        sb = jnp.where(lane % HD < HD // 2, -sb, sb)
        cos[rs, :] = cb
        sin[rs, :] = sb
        xb = x[rs, :].astype(F32)
        r = lax.rsqrt(jnp.mean(xb * xb, axis=1, keepdims=True) + NORM_EPS)
        hb = (xb * r * ga).astype(BF)
        h1[rs, :] = hb
        qp = dot(hb, wq[...])
        kvp = dot(hb, wkv[...])
        for n in range(nkv):
            ns = slice(n * 128, (n + 1) * 128)
            qn = qp[:, ns]
            q[rs, ns] = ((qn * cb + swap_halves(qn, lane) * sb) * ATTN_SCALE).astype(BF)
            kv = kvp[:, ns]
            rot = kv * cb + swap_halves(kv, lane) * sb
            kd[rs, ns] = jnp.where(low, rot, pltpu.roll(rot, HD, 1)).astype(BF)
            vd[rs, ns] = jnp.where(low, pltpu.roll(kv, HD, 1), kv).astype(BF)
        bias = mask_bias(start, valid, i, keys)
        bias2 = jnp.concatenate([bias, bias], axis=0)
        lse_all = jnp.zeros((BLK, 128), F32)
        for n in range(nkv):
            ns = slice(n * 128, (n + 1) * 128)
            qn = q[rs, ns]
            zero = jnp.zeros_like(qn)
            q2 = jnp.concatenate([jnp.where(low, qn, zero), jnp.where(low, zero, qn)], axis=0)
            s = dot_nt(q2, kd[:keys, ns]) + bias2
            m = jnp.max(s, axis=1, keepdims=True)
            p = jnp.exp(s - m)
            total = jnp.sum(p, axis=1, keepdims=True)
            o2 = dot(p.astype(BF), vd[:keys, ns]) * (1.0 / total)
            o[rs, ns] = jnp.where(low, o2[:BLK], o2[BLK:]).astype(BF)
            l2 = m + jnp.log(total)
            lse_all = jnp.where(lane == 2 * n, l2[:BLK], jnp.where(lane == 2 * n + 1, l2[BLK:], lse_all))
        lse[rs, :] = lse_all
        term = dot(o[rs, :], wo[...]).astype(BF)
        if not rest:
            own[rs, :] = term
        else:
            at = pl.ds(i * BLK % half, BLK)

            @pl.when(core[0] == i * BLK // half)
            def _():
                own[at, :] = term

            @pl.when(core[0] != i * BLK // half)
            def _():
                rest[0][at, :] = term


def attn_forward(core, lengths, x, gain, wq, wkv, wo, valid, split):
    rows, width = x.shape
    wid = wq.shape[1]
    kvw = wkv.shape[1]
    shape = jax.ShapeDtypeStruct
    part = [shape((rows // 2, width), BF)] * 2 if split else [shape((rows, width), BF)]
    return pl.pallas_call(
        attn_forward_body,
        in_specs=[pl.BlockSpec(memory_space=pltpu.SMEM)] * 2 + [pl.BlockSpec(memory_space=pltpu.VMEM)] * 6,
        out_shape=[
            shape((rows, width), BF),
            shape((rows, wid), BF),
            shape((rows, kvw), BF),
            shape((rows, kvw), BF),
            shape((rows, wid), BF),
            shape((rows, 128), F32),
            shape((rows, 128), F32),
            shape((rows, 128), F32),
            *part,
        ],
        compiler_params=pltpu.CompilerParams(vmem_limit_bytes=VMEM_BYTES),
        cost_estimate=cost(2 * rows * width * 3 * wid + 4 * rows * rows * 4 * wid, 12 * rows * width),
        name="attention_forward",
    )(core, lengths, x, gain, wq, wkv, wo, valid)


def attn_backward_body(first, folded, _, lengths, q, kd, vd, do, lse, h1, cos, sin, valid, wq, wkv, gain, *rest):
    extras, (dq, dkv, gw, dk, dv) = rest[:-5], rest[-5:]
    if folded:
        extras, gwo = extras[:-1], extras[-1]
        depth = gwo.shape[0]
        for n in range(gwo.shape[1] // depth):
            rs = slice(n * depth, (n + 1) * depth)
            gw[rs, 2 * q.shape[1] + 128 :] = gwo[:, rs]
    nkv = kd.shape[1] // 128
    wid = q.shape[1]
    width = h1.shape[1]
    lane = lax.broadcasted_iota(jnp.int32, (BLK, 128), 1)
    low = lane < HD
    dk[...] = jnp.zeros_like(dk)
    dv[...] = jnp.zeros_like(dv)
    nb = q.shape[0] // BLK
    for i in range(nb):
        rs = pl.ds(i * BLK, BLK)
        keys = (i + 1) * BLK
        cb, sb = cos[rs, :], sin[rs, :]
        place = lax.broadcasted_iota(jnp.int32, (BLK, 1), 0) + i * BLK
        bias = mask_bias(doc_starts(lengths, place), valid, i, keys)
        bias2 = jnp.concatenate([bias, bias], axis=0)
        lse_i = lse[rs, :]
        for n in range(nkv):
            ns = slice(n * 128, (n + 1) * 128)
            qn, dn = q[rs, ns], do[rs, ns]
            zero = jnp.zeros_like(qn)
            q2 = jnp.concatenate([jnp.where(low, qn, zero), jnp.where(low, zero, qn)], axis=0)
            d2 = jnp.concatenate([jnp.where(low, dn, zero), jnp.where(low, zero, dn)], axis=0)
            h = 2 * (first + n)
            l2 = jnp.concatenate([lse_i[:, h : h + 1], lse_i[:, h + 1 : h + 2]], axis=0)
            p = jnp.exp(dot_nt(q2, kd[:keys, ns]) + bias2 - l2)
            dp = dot_nt(d2, vd[:keys, ns])
            shift = jnp.sum(p * dp, axis=1, keepdims=True)
            ds = (p * (dp - shift)).astype(BF)
            dv[:keys, ns] += dot_tn(p.astype(BF), d2)
            dk[:keys, ns] += dot_tn(ds, q2)
            dq2 = dot(ds, kd[:keys, ns])
            dqn = jnp.where(low, dq2[:BLK], dq2[BLK:]) * ATTN_SCALE
            dq[rs, ns] = (dqn * cb - swap_halves(dqn, lane) * sb).astype(BF)
    for i in range(nb):
        rs = pl.ds(i * BLK, BLK)
        cb, sb = cos[rs, :], sin[rs, :]
        for n in range(nkv):
            ns = slice(n * 128, (n + 1) * 128)
            kk = dk[rs, ns]
            kk = kk + pltpu.roll(kk, HD, 1)
            vv = dv[rs, ns]
            vv = vv + pltpu.roll(vv, HD, 1)
            dkv[rs, ns] = jnp.where(low, kk * cb - swap_halves(kk, lane) * sb, vv).astype(BF)
    gq = dot_tn(h1[...], dq[...])
    gk = dot_tn(h1[...], dkv[...])
    gw[:, :wid] = gq.astype(BF)
    gw[:, wid : 2 * wid] = gk.astype(BF)
    ga = jnp.sum(gq * wq[...].astype(F32) + gk * wkv[...].astype(F32), axis=1, keepdims=True) / gain[...].astype(F32)
    lanes = lax.broadcasted_iota(jnp.int32, (width, 128), 1)
    if extras:
        small, s1, s2 = extras
        stats = (s1[...] + s2[...]).T[:, :1]
        stats = jnp.concatenate([stats, jnp.zeros((width - 128, 1), F32)], axis=0)
        rest_cols = jnp.where(lanes == STATS, stats, small[...])
    else:
        rest_cols = jnp.zeros((width, 128), F32)
    gw[:, 2 * wid : 2 * wid + 128] = jnp.where(lanes == GAIN_A, ga, rest_cols).astype(BF)


def attn_backward(first, count, tok, lengths, q, kd, vd, do, lse, h1, cos, sin, valid, wq, wkv, gain, extras=(), gwo=None):
    rows, width = h1.shape
    w = count * 128
    cols = 2 * w + 128 + (0 if gwo is None else gwo.shape[0])
    folded = gwo is not None
    if folded:
        extras = (*extras, gwo)
    shape = jax.ShapeDtypeStruct
    part = pl.BlockSpec((rows, w), lambda _: (0, first // count))
    wpart = pl.BlockSpec((width, w), lambda _: (0, first // count))
    return pl.pallas_call(
        functools.partial(attn_backward_body, first, folded),
        grid=(1,),
        in_specs=[pl.BlockSpec(memory_space=pltpu.SMEM)] * 2
        + [part] * 4
        + [whole_block(v) for v in (lse, h1, cos, sin, valid)]
        + [wpart] * 2
        + [whole_block(v) for v in (gain, *extras)],
        out_specs=[
            pl.BlockSpec((rows, w), lambda _: (0, 0)),
            pl.BlockSpec((rows, w), lambda _: (0, 0)),
            pl.BlockSpec((width, cols), lambda _: (0, 0)),
        ],
        out_shape=[shape((rows, w), BF), shape((rows, w), BF), shape((width, cols), BF)],
        scratch_shapes=[pltpu.VMEM((rows, w), F32), pltpu.VMEM((rows, w), F32)],
        compiler_params=pltpu.CompilerParams(vmem_limit_bytes=VMEM_BYTES),
        cost_estimate=cost(4 * rows * width * w + 20 * rows * rows * w, 10 * rows * width),
        name="attention_backward",
    )(tok, lengths, q, kd, vd, do, lse, h1, cos, sin, valid, wq, wkv, gain, *extras)


def on_device(
    tokens,
    gain_attn,
    query_weight_matrix,
    key_value_weight,
    w_out,
    gain_ffn,
    w_router,
    w_gate_up,
    w_down,
    routes,
    doc_lengths,
    valid_mask,
    cotangent,
):
    rows, width = tokens.shape
    share = routes.shape[0]
    n_ep, n_tp = lax.axis_size("ep"), lax.axis_size("tp")
    nexp = w_router.shape[1]
    inner = math.gcd(n_ep, 4)
    outer = n_ep // inner
    me = lax.axis_index("ep")
    me_in = me % inner
    core = lax.axis_index("tp")[None]
    pair = n_tp == 2

    def across(v, k):
        return lax.ppermute(v, "ep", [(i, i ^ k) for i in range(n_ep)])

    def along(v, k):
        return lax.ppermute(v, "ep", [(i, (i + k * inner) % n_ep) for i in range(n_ep)])

    def swap(v):
        return lax.ppermute(v, "tp", [(0, 1), (1, 0)])

    def after(v, *earlier):
        return lax.optimization_barrier((v, *earlier))[0]

    def total(terms):
        acc = terms[0].astype(F32)
        for term in terms[1:]:
            acc = acc + term.astype(F32)
        return acc

    def scatter_plane(v):
        size = v.shape[0] // inner
        cut = lambda k: lax.dynamic_slice_in_dim(v, (me_in ^ k) * size, size)
        return [cut(0)] + [across(cut(k), k) for k in range(1, inner)]

    def summed(terms):
        return total(terms).astype(BF)

    def column_steps(v):
        bit = 1
        while bit < outer:
            other = lax.ppermute(v, "ep", [(i, i ^ (bit * inner)) for i in range(n_ep)])
            yield other
            v = summed([v, release(other)])
            bit *= 2
        yield v

    def unpacked(v):
        f = v.shape[2]
        return v[:2], v[2].reshape(width // f, f, f).transpose(1, 0, 2).reshape(f, width)

    def packed(gu, down):
        f = gu.shape[2]
        return jnp.concatenate([gu, down.reshape(f, width // f, f).transpose(1, 0, 2).reshape(1, width, f)])

    def full_hidden(v):
        if pair:
            return [v, swap(v)]
        gu, down = unpacked(v)
        return [
            packed(
                lax.all_gather(gu, "tp", axis=2, tiled=True),
                lax.all_gather(down, "tp", axis=0, tiled=True),
            )
        ]

    def own_hidden(v):
        if pair:
            return v[0].astype(F32) + swap(v[1]).astype(F32)
        gu, down = unpacked(v[0].astype(F32))
        return packed(
            lax.psum_scatter(gu, "tp", scatter_dimension=2, tiled=True),
            lax.psum_scatter(down, "tp", scatter_dimension=0, tiled=True),
        )

    halves = 2 if pair else 1
    local = jnp.arange(outer, dtype=jnp.int32) * inner
    ids = (me - local) % n_ep
    ids_all = jnp.concatenate([((me ^ k) - local) % n_ep for k in range(inner)])
    valid_row = valid_mask[None, :]
    live_all = valid_mask.astype(F32)[:, None]
    live = lax.dynamic_slice_in_dim(live_all, core[0] * share, share)
    gain_a, gain_f = gain_attn[None, :], gain_ffn[None, :]
    wr = jnp.pad(w_router, ((0, 0), (0, 128 - nexp)))

    tok = core

    def finish(*values):
        nonlocal tok
        tok = after(tok, *values)

    def release(v):
        return after(v, tok)

    pack, pay = prepare(tok, w_gate_up, w_down, cotangent, routes.T)
    held = [pack]
    if outer > 1:
        held.append(along(pack, 1))
    pays = [pay] + [across(pay, k) for k in range(1, min(inner, 3))]
    chunks = [full_hidden(pack)]
    finish(pack)

    h1, q, kd, vd, o, lse, cos, sin, *part = attn_forward(
        tok, doc_lengths, tokens, gain_a, query_weight_matrix, key_value_weight, w_out, valid_row, pair
    )
    if pair:
        own, other = part[0], swap(part[1])
    else:
        own = lax.psum_scatter(part[0].astype(F32), "tp", scatter_dimension=0, tiled=True)
        other = jnp.zeros_like(own)
    finish(own, other, *pays, *chunks[0])
    mid, h2, stats = middle_norm(tok, tokens, own, other, gain_f, live_all)
    h2s = [h2] + [across(h2, k) for k in range(1, min(inner, 3))]
    finish(h2, *held[1:])

    near = min(2, outer)
    last = outer - 1
    far = list(range(3, inner))
    close = list(range(min(inner, 3)))
    state = [None] * inner
    saved = [dict() for _ in range(inner)]

    def work(blocks, first, count):
        prevs = None if state[blocks[0]] is None else [state[b] for b in blocks]
        out = experts(
            release(ids),
            [h2s[b] for b in blocks],
            [pays[b] for b in blocks],
            prevs,
            wr,
            [c for r in range(first, first + count) for c in chunks[r]],
            halves,
            first,
        )
        for b, (dx, moe, gat, dgu) in zip(blocks, out, strict=True):
            state[b] = (dx, moe)
            for r in range(count):
                saved[b][first + r] = (gat, dgu, r * halves)
        finish(out[0][1])

    def expert_grads(experts_of):
        out = weight_grads(tok, h2s, pays, [[s[r] for r in experts_of] for s in saved], halves)
        finish(out[0])
        return out

    def next_held():
        v = release(held[-1])
        if len(held) < outer:
            held.append(along(v, 1))
        chunks.append(full_hidden(v))

    if outer > 1:
        next_held()
    work([0], 0, near)
    finish(*h2s)
    for b in close[1:]:
        work([b], 0, near)
        if b == 1:
            if outer > 2:
                finish(held[-1])
                next_held()
            for k in far:
                pays.append(across(release(pay), k))
                h2s.append(across(release(h2), k))
    for r in range(near, last):
        work(close, r, 1)
        if r + 1 < last:
            finish(held[-1])
            next_held()
    finish(*h2s, *pays)
    for b in far:
        work([b], 0, max(last, near))
    if last >= near:
        finish(held[-1])
        next_held()

    first = 1 % outer
    later = [[r] for r in range(2, min(outer, 3))] + [[*range(3, outer), 0]]
    later = later if outer > 1 else []
    raw = expert_grads([first])
    parts = {first: own_hidden([v[0] for v in raw])}
    if last >= near and inner > 1:
        work(list(range(1, inner)), last, 1)
    ring = parts[first].astype(BF)
    finish(ring)
    if outer > 1:
        ring = along(ring, 1)
    dxs = [None] + [across(state[k][0], k) for k in range(1, inner)]
    if last >= near:
        work([0], last, 1)
    dxs[0] = state[0][0]
    raws = [expert_grads(rs) for rs in later]
    finish(*dxs, *([ring] if outer > 1 else []))
    moes = [state[0][1]] + [across(release(state[k][1]), k) for k in range(1, inner)]

    def ring_step(r):
        nonlocal ring
        term = release(ring).astype(F32) + parts[r]
        if r == 0:
            return term
        ring = term.astype(BF)
        finish(ring)
        ring = along(ring, 1)

    gm_share, small = middle_back(tok, ids_all, h2, mid, gain_f, pay, wr, dxs, outer)
    gm = [gm_share, swap(gm_share)] if pair else [lax.all_gather(gm_share, "tp", axis=0, tiled=True)]
    finish(gm_share)
    for rs, raw in zip(later, raws, strict=True):
        if pair:
            other = swap(release(raw[1]))
            parts.update({r: raw[0][n].astype(F32) + other[n].astype(F32) for n, r in enumerate(rs)})
            if rs == [2]:
                finish(other)
        else:
            parts.update({r: own_hidden([raw[0][n]]) for n, r in enumerate(rs)})
    if outer > 2:
        ring_step(2)
    do, gwo = out_back(tok, cotangent, w_out, o, gm)
    finish(do)

    nkv = kd.shape[1] // 128
    groups = 2 if nkv % 2 == 0 else 1
    each = nkv // groups
    dqs, dkvs, terms = [], [], []
    for n in range(groups):
        if n == groups - 1:
            finish(*moes)
            out_share, stats_out = layer_out_share(tok, mid, live, moes)
            finish(out_share)
            if outer > 3:
                finish(ring)
                ring_step(3)
        dq, dkv, gw = attn_backward(
            n * each,
            each,
            tok,
            doc_lengths,
            q,
            kd,
            vd,
            do,
            lse,
            h1,
            cos,
            sin,
            valid_row,
            query_weight_matrix,
            key_value_weight,
            gain_attn[:, None],
            (small, stats, stats_out) if n == groups - 1 else (),
            gwo if n == 0 else None,
        )
        finish(gw)
        dqs.append(dq)
        dkvs.append(dkv)
        if n == 0:
            terms.append(scatter_plane(gw))
    finish(*terms[0])
    ahead = column_steps(summed([release(t) for t in terms[0]]))
    moving = next(ahead)
    if groups > 1:
        terms.append(scatter_plane(release(gw)))
    dh1 = input_back(tok, query_weight_matrix, key_value_weight, dqs, dkvs)
    finish(dh1, moving, *([ring] if outer > 1 else []))
    if pair:
        dh_other = swap(release(dh1))
        out_other = swap(release(out_share))
    else:
        dh1, dh_other = lax.psum(dh1.astype(F32), "tp"), jnp.zeros_like(dh1)
    if groups > 1:
        moving = next(ahead)
    finish(dh_other)
    grad_tokens = token_grads(tok, tokens, cotangent, dh1, dh_other, gain_a, gm)
    finish(grad_tokens)
    gws = []
    if groups > 1:
        finish(*terms[1])
        behind = column_steps(summed([release(t) for t in terms[1]]))
        late = next(behind)
    if pair:
        layer_out = jnp.where(
            core[0] == 0,
            jnp.concatenate([release(out_share), out_other]),
            jnp.concatenate([out_other, release(out_share)]),
        )
        finish(layer_out)
    else:
        layer_out = lax.all_gather(out_share, "tp", axis=0, tiled=True)
    finish(moving)
    for v in ahead:
        whole = v
    gws.append([whole] + [across(release(whole), k) for k in range(1, inner)])
    if groups > 1:
        finish(late)
        for v in behind:
            late = v
        gws.append([late] + [across(release(late), k) for k in range(1, inner)])
    for r in range(4, outer):
        ring_step(r)
    sums = ring_step(0) if outer > 1 else parts[0]
    gu_grad, down_grad = unpacked(sums)
    w = each * 128
    depth = w_out.shape[0]
    grad_w_query, grad_w_kv, extras, folded = gather_rows(
        release(me_in[None]), gws, [(w, w, 128, depth if n == 0 else 0) for n in range(groups)]
    )
    grad_w_out = jnp.concatenate([folded[n * depth : (n + 1) * depth] for n in range(width // depth)], axis=1)
    extras = sum(extras[:, n * 128 : (n + 1) * 128] for n in range(groups))
    extras = extras + swap(extras) if pair else lax.psum(extras, "tp")
    s = extras[:4, STATS]
    return (
        layer_out,
        grad_tokens,
        extras[:, GAIN_A],
        grad_w_query,
        grad_w_kv,
        grad_w_out,
        extras[:, GAIN_F],
        extras[:, :nexp],
        gu_grad[None],
        down_grad[None],
        jnp.sqrt(s[:3] / (s[3] * width)),
    )


def solution(mesh):
    return jax.shard_map(
        on_device,
        mesh=mesh,
        in_specs=(
            P("ep", None),
            P(),
            P(None, "tp"),
            P(None, "tp"),
            P("tp", None),
            P(),
            P(),
            P("ep", None, None, "tp"),
            P("ep", "tp", None),
            P(("ep", "tp"), None),
            P("ep", None),
            P("ep"),
            P("ep", None),
        ),
        out_specs=(
            P("ep", None),
            P("ep", None),
            P(),
            P(None, "tp"),
            P(None, "tp"),
            P("tp", None),
            P(),
            P(),
            P("ep", None, None, "tp"),
            P("ep", "tp", None),
            P(),
        ),
        check_vma=False,
    )
```

```python
import functools
import math

import jax
import jax.numpy as jnp
from jax import lax
from jax.experimental import pallas as pl
from jax.experimental.pallas import tpu as pltpu
from jax.sharding import PartitionSpec as P

SEQUENCE_LENGTH = 1024
WINDOW = 1024
ATTN_SCALE = 0.015625
RESID_SCALE = 0.22
TOPK = 8
NORM_EPS = 1e-06
ROPE_BASE = 10000.0
F32 = jnp.float32
BF = jnp.bfloat16
VMEM_BYTES = 60 * 1024 * 1024
COST = 0.02
GAIN_F, GAIN_A, STATS = 32, 33, 34


def cost(flops, bytes_accessed, transcendentals=0):
    return pl.CostEstimate(
        flops=int(COST * flops), bytes_accessed=int(COST * bytes_accessed), transcendentals=int(COST * transcendentals)
    )


def dot(a, b):
    return jnp.dot(a, b, preferred_element_type=F32)


def dot_nt(a, b):
    return lax.dot_general(a, b, (((1,), (1,)), ((), ())), preferred_element_type=F32)


def dot_tn(a, b):
    return lax.dot_general(a, b, (((0,), (0,)), ((), ())), preferred_element_type=F32)


def whole_block(v):
    return pl.BlockSpec(v.shape, lambda *_: (0,) * len(v.shape))


def gate_rows(h2, routes, wr):
    rows = h2.shape[0]
    lane = lax.broadcasted_iota(jnp.int32, (rows, 128), 1).astype(F32)
    picks = routes.astype(F32).T
    mask = picks[:, 0:1] == lane
    for k in range(1, TOPK):
        mask = mask | (picks[:, k : k + 1] == lane)
    sel = jnp.where(mask, dot(h2, wr[...]), -jnp.inf)
    weight = jnp.exp(sel - jnp.max(sel, axis=1, keepdims=True))
    return weight / jnp.sum(weight, axis=1, keepdims=True)


def gate_table(h2, pay, wr):
    rows = h2.shape[0]
    return gate_rows(h2[...], pay[rows : rows + 16, :rows], wr)


def middle_body(core, x, own, other, gain, live, mid, h2, stats):
    attn = RESID_SCALE * (own[...].astype(F32) + other[...].astype(F32))
    m = x[...].astype(F32) + attn
    mid[...] = m
    r = lax.rsqrt(jnp.mean(m * m, axis=1, keepdims=True) + NORM_EPS)
    h2[...] = (m * r * gain[...].astype(F32)).astype(BF)
    v = live[...]
    total = jnp.sum(v * jnp.sum(attn * attn, axis=1, keepdims=True))
    lane = lax.broadcasted_iota(jnp.int32, stats.shape, 1)
    stats[...] = jnp.where(lane == 1, total, jnp.where(lane == 3, jnp.sum(v), 0.0))


def middle_norm(core, x, own, other, gain, live):
    share, width = own.shape
    shape = jax.ShapeDtypeStruct
    part = lambda n: pl.BlockSpec((share, n), lambda _, c: (c[0], 0))
    full = lambda *s: pl.BlockSpec(s, lambda *_: (0, 0))
    return pl.pallas_call(
        middle_body,
        grid_spec=pltpu.PrefetchScalarGridSpec(
            num_scalar_prefetch=1,
            grid=(1,),
            in_specs=[part(width), whole_block(own), whole_block(other), whole_block(gain), part(1)],
            out_specs=[full(share, width), full(share, width), full(8, 128)],
        ),
        out_shape=[shape((share, width), F32), shape((share, width), BF), shape((8, 128), F32)],
        compiler_params=pltpu.CompilerParams(vmem_limit_bytes=VMEM_BYTES),
        cost_estimate=cost(10 * share * width, 12 * share * width),
        name="middle_norm",
    )(core, x, own, other, gain, live)


def experts_body(nb, nchunk, halves, first, carried, *refs):
    ids = refs[0]
    at = 1
    h2s, pays = refs[at : at + nb], refs[at + nb : at + 2 * nb]
    at += 2 * nb
    prevs = [None] * nb
    if carried:
        prevs = [refs[at + 2 * b : at + 2 * b + 2] for b in range(nb)]
        at += 2 * nb
    wr = refs[at]
    packs = refs[at + 1 : at + 1 + nchunk]
    at += 1 + nchunk
    outs = [refs[at + 4 * b : at + 4 * b + 4] for b in range(nb)]
    at += 4 * nb
    gates, dgacc, macc, xacc, buf, sem = refs[at:]
    c = pl.program_id(0)
    rows, width = h2s[0].shape
    f = buf.shape[3]
    lane = lax.broadcasted_iota(jnp.int32, (rows, 128), 1)

    @pl.when(c == 0)
    def _():
        pltpu.make_async_copy(packs[0], buf.at[0], sem.at[0]).start()
        for b in range(nb):
            gates[b] = gate_table(h2s[b], pays[b], wr)
            if carried:
                macc[b] = prevs[b][1][...].astype(F32)
                xacc[b] = prevs[b][0][:rows, :].astype(F32)
            else:
                macc[b] = jnp.zeros((rows, width), F32)
                xacc[b] = jnp.zeros((rows, width), F32)
        dgacc[...] = jnp.zeros_like(dgacc)

    for k in range(1, nchunk):

        @pl.when(c + 1 == k)
        def _(k=k):
            pltpu.make_async_copy(packs[k], buf.at[k % 2], sem.at[k % 2]).start()

    slot = lax.rem(c, 2)
    pltpu.make_async_copy(packs[0], buf.at[slot], sem.at[slot]).wait()
    r = first + c // halves
    e = ids[r]
    nd = width // f
    for b in range(nb):
        g, gat, dgu = pays[b], outs[b][2], outs[b][3]
        hb = h2s[b][...]
        gp = dot(hb, buf[slot, 0])
        up = dot(hb, buf[slot, 1])
        u = sum(dot_nt(g[:rows, k * f : (k + 1) * f], buf[slot, 2, k * f : (k + 1) * f, :]) for k in range(nd))
        gate = jnp.sum(jnp.where(lane == e, gates[b], 0.0), axis=1, keepdims=True)
        sg = jax.nn.sigmoid(gp)
        sl = gp * sg
        act = sl * up
        ga = (gate * act).astype(BF)
        dgacc[b] += jnp.where(lane == r, jnp.sum(act * u, axis=1, keepdims=True) * RESID_SCALE, 0.0)
        da = (RESID_SCALE * gate) * u
        dgp = (da * up * (sg + sl * (1.0 - sg))).astype(BF)
        dup = (da * sl).astype(BF)
        gat[0] = ga.T
        dgu[0, :, :f] = dgp
        dgu[0, :, f:] = dup
        for k in range(nd):
            macc[b, :, k * f : (k + 1) * f] += dot(ga, buf[slot, 2, k * f : (k + 1) * f, :])
        xacc[b] += dot_nt(dgp, buf[slot, 0]) + dot_nt(dup, buf[slot, 1])

    @pl.when(c == nchunk - 1)
    def _():
        for b in range(nb):
            dx, moe = outs[b][:2]
            moe[...] = macc[b].astype(BF)
            dx[:rows, :] = xacc[b].astype(BF)
            dg = dgacc[b].T[:8]
            high = dg.astype(BF).astype(F32)
            tail = jnp.concatenate([high, dg - high], axis=0)
            if carried:
                row = lax.broadcasted_iota(jnp.int32, (16, rows), 0) % 8
                mine = (row >= first) & (row < first + nchunk // halves)
                tail = jnp.where(mine, tail, prevs[b][0][rows:, :rows].astype(F32))
            dx[rows:, :] = jnp.zeros((16, width), BF)
            dx[rows:, :rows] = tail.astype(BF)


def experts(ids, h2s, pays, prevs, wr, packs, halves, first):
    rows, width = h2s[0].shape
    nb, nchunk = len(h2s), len(packs)
    f = packs[0].shape[2]
    carried = prevs is not None
    flat = [v for prev in prevs for v in prev] if carried else []
    shape = jax.ShapeDtypeStruct
    once = lambda v: pl.BlockSpec(v.shape, lambda *_: (0,) * len(v.shape), pipeline_mode=pl.Buffered(1))
    out = pl.pallas_call(
        functools.partial(experts_body, nb, nchunk, halves, first, carried),
        grid_spec=pltpu.PrefetchScalarGridSpec(
            num_scalar_prefetch=1,
            grid=(nchunk,),
            in_specs=[once(v) for v in (*h2s, *pays, *flat, wr)] + [pl.BlockSpec(memory_space=pl.ANY)] * nchunk,
            out_specs=[
                pl.BlockSpec((rows + 16, width), lambda c, _: (0, 0)),
                pl.BlockSpec((rows, width), lambda c, _: (0, 0)),
                pl.BlockSpec((1, f, rows), lambda c, _: (c, 0, 0)),
                pl.BlockSpec((1, rows, 2 * f), lambda c, _: (c, 0, 0)),
            ]
            * nb,
            scratch_shapes=[
                pltpu.VMEM((nb, rows, 128), F32),
                pltpu.VMEM((nb, rows, 128), F32),
                pltpu.VMEM((nb, rows, width), F32),
                pltpu.VMEM((nb, rows, width), F32),
                pltpu.VMEM((2, 3, width, f), BF),
                pltpu.SemaphoreType.DMA((2,)),
            ],
        ),
        out_shape=[
            shape((rows + 16, width), BF),
            shape((rows, width), BF),
            shape((nchunk, f, rows), BF),
            shape((nchunk, rows, 2 * f), BF),
        ]
        * nb,
        compiler_params=pltpu.CompilerParams(vmem_limit_bytes=VMEM_BYTES),
        cost_estimate=cost(12 * rows * width * f * nchunk * nb, 6 * nchunk * width * f + 12 * rows * width * nb),
        name="experts",
    )(ids, *h2s, *pays, *flat, wr, *packs)
    return [out[4 * b : 4 * b + 4] for b in range(nb)]


def weight_grads_body(nb, halves, _, *refs):
    h2 = refs[:nb]
    g = refs[nb : 2 * nb]
    hidden, outs = refs[2 * nb : -halves], refs[-halves:]
    e, c = pl.program_id(0), pl.program_id(1)
    rows = h2[0].shape[0]
    width, f = outs[0].shape[2:]
    for n in range(len(hidden) // (2 * nb)):

        @pl.when(e == n)
        def _(n=n):
            gat, dgu = hidden[2 * nb * n : 2 * nb * n + nb], hidden[2 * nb * n + nb : 2 * nb * (n + 1)]
            acc = sum(dot_tn(h2[b][...], dgu[b][0]) for b in range(nb))
            down = sum(dot(gat[b][0], g[b][:rows, :]) for b in range(nb)) * RESID_SCALE
            for half in range(halves):

                @pl.when(c == half)
                def _(out=outs[half]):
                    out[0, 0] = acc[:, :f].astype(BF)
                    out[0, 1] = acc[:, f:].astype(BF)
                    for k in range(width // f):
                        out[0, 2, k * f : (k + 1) * f, :] = down[:, k * f : (k + 1) * f].astype(BF)


def weight_grads(tok, h2s, pays, saved, halves):
    nb, ne = len(h2s), len(saved[0])
    rows, width = h2s[0].shape
    f = saved[0][0][0].shape[1]
    shape = jax.ShapeDtypeStruct
    once = lambda v: pl.BlockSpec(v.shape, lambda *_: (0,) * len(v.shape), pipeline_mode=pl.Buffered(1))
    specs, args = [], []
    for n in range(ne):
        half = lambda e, c, n=n: jnp.where(e < n, 0, jnp.where(e == n, c, halves - 1))
        for j, block in ((0, (1, f, rows)), (1, (1, rows, 2 * f))):
            for b in range(nb):
                args.append(saved[b][n][j])
                specs.append(pl.BlockSpec(block, lambda e, c, o=saved[b][n][2], half=half: (o + half(e, c), 0, 0)))
    return pl.pallas_call(
        functools.partial(weight_grads_body, nb, halves),
        grid=(ne, halves),
        in_specs=[pl.BlockSpec(memory_space=pltpu.SMEM)] + [once(v) for v in (*h2s, *pays)] + specs,
        out_specs=[pl.BlockSpec((1, 3, width, f), lambda e, c: (e, 0, 0, 0))] * halves,
        out_shape=[shape((ne, 3, width, f), BF)] * halves,
        compiler_params=pltpu.CompilerParams(vmem_limit_bytes=VMEM_BYTES),
        cost_estimate=cost(6 * rows * nb * width * f * halves, 6 * halves * width * f + 4 * rows * nb * width),
        name="expert_weight_grads",
    )(tok, *h2s, *pays, *args)


def middle_back_body(nb, nlocal, _, ids, h2, mid, gain, tail, wr, *refs):
    dxs, tails = refs[:nb], refs[nb : 2 * nb]
    *gms, small, acc = refs[2 * nb :]
    rows, width = h2.shape
    at = pl.program_id(0)
    cols = pl.ds(pl.multiple_of(at * rows, rows), rows)
    lane = lax.broadcasted_iota(jnp.int32, (rows, 128), 1)
    gates = gate_rows(h2[...], tail[:, cols], wr)
    dgate = jnp.zeros((rows, 128), F32)
    for b in range(nb):
        part = tails[b][:, cols].astype(F32)
        part = (part[:8] + part[8:]).T
        for r in range(nlocal):
            dgate = jnp.where(lane == ids[b * nlocal + r], part[:, r : r + 1], dgate)
    dsel = gates * (dgate - jnp.sum(gates * dgate, axis=1, keepdims=True))
    high = dsel.astype(BF)
    rest = (dsel - high.astype(F32)).astype(BF)
    router = dot_tn(h2[...], high) + dot_tn(h2[...], rest)
    dh = dot_nt(high, wr[...]) + dot_nt(rest, wr[...])
    for b in range(nb):
        dh = dh + dxs[b][...].astype(F32)
    m = mid[...]
    r2 = lax.rsqrt(jnp.mean(m * m, axis=1, keepdims=True) + NORM_EPS)
    xhat = m * r2
    col = jnp.broadcast_to(jnp.sum(dh * xhat, axis=0, keepdims=True), (8, width)).T[:, :1]
    su = dh * gain[...].astype(F32)
    grad = (r2 * (su - xhat * jnp.mean(su * xhat, axis=1, keepdims=True))).astype(BF)
    for n, gm in enumerate(gms):

        @pl.when(at == n)
        def _(gm=gm):
            gm[...] = grad

    small_here = jnp.where(lax.broadcasted_iota(jnp.int32, (width, 128), 1) == GAIN_F, col, router)

    @pl.when(at == 0)
    def _():
        acc[...] = small_here

    @pl.when(at > 0)
    def _():
        acc[...] += small_here

    small[...] = acc[...]


def middle_back(tok, ids, h2, mid, gain, pay, wr, dxs, nlocal):
    rows, width = h2.shape
    rt = rows // 2 if rows % 512 == 0 else rows
    shape = jax.ShapeDtypeStruct
    block = pl.BlockSpec((rt, width), lambda i: (i, 0))
    tail = pl.BlockSpec((16, width), lambda i: (rows // 16, 0))
    whole = lambda v: pl.BlockSpec(v.shape, lambda i: (0, 0))
    small = pl.BlockSpec((width, 128), lambda i: (0, 0))
    return pl.pallas_call(
        functools.partial(middle_back_body, len(dxs), nlocal),
        grid=(rows // rt,),
        in_specs=[pl.BlockSpec(memory_space=pltpu.SMEM)] * 2
        + [block, block, whole(gain), tail, whole(wr)]
        + [block] * len(dxs)
        + [tail] * len(dxs),
        out_specs=[pl.BlockSpec((rt, width), lambda i: (0, 0))] * (rows // rt) + [small],
        out_shape=[shape((rt, width), BF)] * (rows // rt) + [shape((width, 128), F32)],
        scratch_shapes=[pltpu.VMEM((width, 128), F32)],
        compiler_params=pltpu.CompilerParams(vmem_limit_bytes=VMEM_BYTES),
        cost_estimate=cost(40 * rows * width, 20 * rows * width),
        name="middle_back",
    )(tok, ids, h2, mid, gain, pay, wr, *dxs, *dxs)


def input_back_body(nq, _, wq, wkv, *refs):
    dq = refs[:nq]
    dkv = refs[nq : 2 * nq]
    dh = refs[2 * nq]
    acc = None
    for w, parts in ((wq, dq), (wkv, dkv)):
        at = 0
        for part in parts:
            n = part.shape[1]
            term = dot_nt(part[...], w[:, at : at + n])
            acc = term if acc is None else acc + term
            at += n
    dh[...] = acc.astype(BF)


def input_back(tok, wq, wkv, dqs, dkvs):
    rows = dqs[0].shape[0]
    width = wq.shape[0]
    rt = 256
    nq = len(dqs)
    block = lambda n: pl.BlockSpec((rt, n), lambda i: (i, 0))
    return pl.pallas_call(
        functools.partial(input_back_body, nq),
        grid=(rows // rt,),
        in_specs=[pl.BlockSpec(memory_space=pltpu.SMEM), whole_block(wq), whole_block(wkv)] + [block(v.shape[1]) for v in (*dqs, *dkvs)],
        out_specs=block(width),
        out_shape=jax.ShapeDtypeStruct((rows, width), BF),
        compiler_params=pltpu.CompilerParams(vmem_limit_bytes=VMEM_BYTES),
        cost_estimate=cost(4 * rows * width * wq.shape[1], 10 * rows * width),
        name="input_back",
    )(tok, wq, wkv, *dqs, *dkvs)


def token_grads_body(_, x, cot, own, other, gm, gain, out):
    xb = x[...].astype(F32)
    r = lax.rsqrt(jnp.mean(xb * xb, axis=1, keepdims=True) + NORM_EPS)
    xhat = xb * r
    su = (own[...].astype(F32) + other[...].astype(F32)) * gain[...].astype(F32)
    norm = r * (su - xhat * jnp.mean(su * xhat, axis=1, keepdims=True))
    out[...] = cot[...].astype(F32) + gm[...].astype(F32) + norm


def token_grads(tok, x, cot, own, other, gm, gain):
    rows, width = x.shape
    rt = 256
    block = pl.BlockSpec((rt, width), lambda i: (i, 0))
    return pl.pallas_call(
        token_grads_body,
        grid=(rows // rt,),
        in_specs=[pl.BlockSpec(memory_space=pltpu.SMEM)] + [block] * 5 + [whole_block(gain)],
        out_specs=block,
        out_shape=jax.ShapeDtypeStruct((rows, width), F32),
        compiler_params=pltpu.CompilerParams(vmem_limit_bytes=VMEM_BYTES),
        cost_estimate=cost(12 * rows * width, 14 * rows * width),
        name="token_grads",
    )(tok, x, cot, own, other, gm, gain)


def layer_out_body(nb, _, *refs):
    mid, live = refs[:2]
    moes = refs[2 : 2 + nb]
    out, stats = refs[2 + nb :]
    moe = sum(m[...].astype(F32) for m in moes) * RESID_SCALE
    outf = mid[...] + moe
    out[...] = outf.astype(BF)
    v = live[...]
    s0 = jnp.sum(v * jnp.sum(outf * outf, axis=1, keepdims=True))
    s2 = jnp.sum(v * jnp.sum(moe * moe, axis=1, keepdims=True))
    lane = lax.broadcasted_iota(jnp.int32, stats.shape, 1)

    @pl.when(pl.program_id(0) == 0)
    def _():
        stats[...] = jnp.zeros_like(stats)

    stats[...] += jnp.where(lane == 0, s0, jnp.where(lane == 2, s2, 0.0))


def layer_out_share(tok, mid, live, moes):
    rows, width = mid.shape
    shape = jax.ShapeDtypeStruct
    rt = 128
    block = lambda n: pl.BlockSpec((rt, n), lambda i: (i, 0))
    return pl.pallas_call(
        functools.partial(layer_out_body, len(moes)),
        grid=(rows // rt,),
        in_specs=[pl.BlockSpec(memory_space=pltpu.SMEM), block(width), block(1)] + [block(width)] * len(moes),
        out_specs=[block(width), pl.BlockSpec((8, 128), lambda i: (0, 0))],
        out_shape=[shape((rows, width), BF), shape((8, 128), F32)],
        compiler_params=pltpu.CompilerParams(vmem_limit_bytes=VMEM_BYTES),
        cost_estimate=cost(12 * rows * width, 14 * rows * width),
        name="layer_out",
    )(tok, mid, live, *moes)


def gather_rows_body(widths, count, turned, me, *refs):
    parts, outs = refs[:count], refs[-len(widths) :]
    size = parts[0].shape[0]
    for k, part in enumerate(parts):
        rows = pl.ds(pl.multiple_of((me[0] ^ k) * size, size), size)
        begin = 0
        for j, (out, w) in enumerate(zip(outs, widths, strict=True)):
            piece = part[:, begin : begin + w].astype(F32)
            if turned and j == len(widths) - 1:
                out[:, rows] = piece.T
            else:
                out[rows, :] = piece
            begin += w


def gather_rows(me, parts, widths, groups, turned, earlier=()):
    npart = len(parts)
    rows = npart * parts[0].shape[0]
    group = 1 if earlier else 0
    last = len(widths) - 1
    block = lambda j, w: (w, rows) if turned and j == last else (rows, w)
    shape = lambda j, w: (rows, w * groups) if j < 2 else block(j, w)
    return pl.pallas_call(
        functools.partial(gather_rows_body, widths, npart, turned),
        grid=(1,),
        in_specs=[pl.BlockSpec(memory_space=pltpu.SMEM)]
        + [whole_block(v) for v in parts]
        + [pl.BlockSpec(memory_space=pl.ANY)] * len(earlier),
        out_specs=[
            pl.BlockSpec(block(j, w), (lambda _: (0, group)) if j < 2 else (lambda _: (0, 0)))
            for j, w in enumerate(widths)
        ],
        out_shape=[jax.ShapeDtypeStruct(shape(j, w), F32) for j, w in enumerate(widths)],
        input_output_aliases={1 + npart + j: j for j in range(len(earlier))},
        compiler_params=pltpu.CompilerParams(vmem_limit_bytes=VMEM_BYTES),
        cost_estimate=cost(0, 6 * rows * sum(widths)),
        name="gather_rows",
    )(me, *parts, *earlier)


HD = 64
NEG = -1e30
BLK = 256


def swap_halves(v, lane):
    return jnp.where(lane % HD < HD // 2, pltpu.roll(v, 128 - HD // 2, 1), pltpu.roll(v, HD // 2, 1))


def mask_bias(start, valid, i, keys):
    row = lax.broadcasted_iota(jnp.int32, (BLK, keys), 0) + i * BLK
    key = lax.broadcasted_iota(jnp.int32, (BLK, keys), 1)
    first = jnp.maximum(start, row[:, :1] - (WINDOW - 1))
    ok = (key >= first) & (key <= row) & ((valid[:, :keys] > 0) | (key == row))
    return jnp.where(ok, 0.0, NEG).astype(F32)


def doc_starts(lengths, place):
    start = jnp.zeros_like(place)
    end = 0
    for j in range(lengths.shape[1]):
        end = end + lengths[0, j]
        start = jnp.where(place >= end, end, start)
    return start


def prepare_body(core, gu, down, cot, routes, pack, pay):
    width, f = gu.shape[2:]
    share = cot.shape[0]
    pack[:2] = gu[0]
    for k in range(width // f):
        pack[2, k * f : (k + 1) * f, :] = down[0, :, k * f : (k + 1) * f]
    pay[:share, :] = cot[...]
    pay[share:, :] = jnp.zeros((pay.shape[0] - share, width), BF)
    pay[share : share + routes.shape[0], :share] = routes[...].astype(F32).astype(BF)


def prepare(core, gu, down, cot, routes):
    width, f = gu.shape[2:]
    share = routes.shape[1]
    shape = jax.ShapeDtypeStruct
    return pl.pallas_call(
        prepare_body,
        grid_spec=pltpu.PrefetchScalarGridSpec(
            num_scalar_prefetch=1,
            grid=(1,),
            in_specs=[
                whole_block(gu),
                whole_block(down),
                pl.BlockSpec((share, width), lambda _, c: (c[0], 0)),
                whole_block(routes),
            ],
            out_specs=[
                pl.BlockSpec((3, width, f), lambda *_: (0, 0, 0)),
                pl.BlockSpec((share + 16, width), lambda *_: (0, 0)),
            ],
        ),
        out_shape=[shape((3, width, f), BF), shape((share + 16, width), BF)],
        compiler_params=pltpu.CompilerParams(vmem_limit_bytes=VMEM_BYTES),
        cost_estimate=cost(0, 12 * width * f),
        name="prepare",
    )(core, gu, down, cot, routes)


def attn_forward_body(core, lengths, x, gain, wq, wkv, wo, valid, h1, q, kd, vd, o, lse, cos, sin, own, *rest):
    nkv = wkv.shape[1] // 128
    lane = lax.broadcasted_iota(jnp.int32, (BLK, 128), 1)
    low = lane < HD
    ga = gain[...].astype(F32)
    frequencies = jnp.exp((lane[:1] % (HD // 2)).astype(F32) * (-2.0 * math.log(ROPE_BASE) / HD))
    half = own.shape[0]
    for i in range(x.shape[0] // BLK):
        rs = pl.ds(i * BLK, BLK)
        keys = (i + 1) * BLK
        place = lax.broadcasted_iota(jnp.int32, (BLK, 1), 0) + i * BLK
        start = doc_starts(lengths, place)
        angles = (place - start).astype(F32) * frequencies
        cb = jnp.cos(angles)
        sb = jnp.sin(angles)
        sb = jnp.where(lane % HD < HD // 2, -sb, sb)
        cos[rs, :] = cb
        sin[rs, :] = sb
        xb = x[rs, :].astype(F32)
        r = lax.rsqrt(jnp.mean(xb * xb, axis=1, keepdims=True) + NORM_EPS)
        hb = (xb * r * ga).astype(BF)
        h1[rs, :] = hb
        qp = dot(hb, wq[...])
        kvp = dot(hb, wkv[...])
        for n in range(nkv):
            ns = slice(n * 128, (n + 1) * 128)
            qn = qp[:, ns]
            q[rs, ns] = ((qn * cb + swap_halves(qn, lane) * sb) * ATTN_SCALE).astype(BF)
            kv = kvp[:, ns]
            rot = kv * cb + swap_halves(kv, lane) * sb
            kd[rs, ns] = jnp.where(low, rot, pltpu.roll(rot, HD, 1)).astype(BF)
            vd[rs, ns] = jnp.where(low, pltpu.roll(kv, HD, 1), kv).astype(BF)
        bias = mask_bias(start, valid, i, keys)
        bias2 = jnp.concatenate([bias, bias], axis=0)
        lse_all = jnp.zeros((BLK, 128), F32)
        for n in range(nkv):
            ns = slice(n * 128, (n + 1) * 128)
            qn = q[rs, ns]
            zero = jnp.zeros_like(qn)
            q2 = jnp.concatenate([jnp.where(low, qn, zero), jnp.where(low, zero, qn)], axis=0)
            s = dot_nt(q2, kd[:keys, ns]) + bias2
            m = jnp.max(s, axis=1, keepdims=True)
            p = jnp.exp(s - m)
            total = jnp.sum(p, axis=1, keepdims=True)
            o2 = dot(p.astype(BF), vd[:keys, ns]) * (1.0 / total)
            o[rs, ns] = jnp.where(low, o2[:BLK], o2[BLK:]).astype(BF)
            l2 = m + jnp.log(total)
            lse_all = jnp.where(lane == 2 * n, l2[:BLK], jnp.where(lane == 2 * n + 1, l2[BLK:], lse_all))
        lse[rs, :] = lse_all
        term = dot(o[rs, :], wo[...]).astype(BF)
        if not rest:
            own[rs, :] = term
        else:
            at = pl.ds(i * BLK % half, BLK)

            @pl.when(core[0] == i * BLK // half)
            def _():
                own[at, :] = term

            @pl.when(core[0] != i * BLK // half)
            def _():
                rest[0][at, :] = term


def attn_forward(core, lengths, x, gain, wq, wkv, wo, valid, split):
    rows, width = x.shape
    wid = wq.shape[1]
    kvw = wkv.shape[1]
    shape = jax.ShapeDtypeStruct
    part = [shape((rows // 2, width), BF)] * 2 if split else [shape((rows, width), BF)]
    return pl.pallas_call(
        attn_forward_body,
        in_specs=[pl.BlockSpec(memory_space=pltpu.SMEM)] * 2 + [pl.BlockSpec(memory_space=pltpu.VMEM)] * 6,
        out_shape=[
            shape((rows, width), BF),
            shape((rows, wid), BF),
            shape((rows, kvw), BF),
            shape((rows, kvw), BF),
            shape((rows, wid), BF),
            shape((rows, 128), F32),
            shape((rows, 128), F32),
            shape((rows, 128), F32),
            *part,
        ],
        compiler_params=pltpu.CompilerParams(vmem_limit_bytes=VMEM_BYTES),
        cost_estimate=cost(2 * rows * width * 3 * wid + 4 * rows * rows * 4 * wid, 12 * rows * width),
        name="attention_forward",
    )(core, lengths, x, gain, wq, wkv, wo, valid)


def attn_backward_body(first, npart, nmore, npiece, places, core, at, lengths, q, kd, vd, lse, cos, sin, valid, gain, *refs):
    it = iter(refs)
    take = lambda n: [next(it) for _ in range(n)]
    h1_hbm, wq_hbm, wkv_hbm = take(3)
    more = take(nmore)
    if places:
        cot, wo, o_hbm, *parts = take(3 + npart)
    else:
        (do,) = take(1)
    dq, dkv, sums = take(3)
    pieces = take(npiece)
    if places:
        do, gm = take(2)
    dk, dv, gw, h1, wq, wkv, sem = take(7)
    if places:
        da, o = take(2)
    wid = q.shape[1]
    width = h1.shape[1]
    cols = pl.ds(first * 128, wid)
    copies = [
        pltpu.make_async_copy(h1_hbm, h1, sem.at[0]),
        pltpu.make_async_copy(wq_hbm.at[:, cols], wq, sem.at[1]),
        pltpu.make_async_copy(wkv_hbm.at[:, cols], wkv, sem.at[2]),
    ]
    if places:
        copies.append(pltpu.make_async_copy(o_hbm, o, sem.at[3]))
    for copy in copies:
        copy.start()
    if places:
        for i in range(q.shape[0] // BLK):
            rs = pl.ds(i * BLK, BLK)
            g = placed(core, parts, i)
            gm[rs, :] = g.astype(BF)
            d = (RESID_SCALE * (cot[rs, :].astype(F32) + g)).astype(BF)
            da[rs, :] = d
            do[rs, :] = dot_nt(d, wo[...]).astype(BF)
    nkv = kd.shape[1] // 128
    wid = q.shape[1]
    lane = lax.broadcasted_iota(jnp.int32, (BLK, 128), 1)
    low = lane < HD
    dk[...] = jnp.zeros_like(dk)
    dv[...] = jnp.zeros_like(dv)
    nb = q.shape[0] // BLK
    for i in range(nb):
        rs = pl.ds(i * BLK, BLK)
        keys = (i + 1) * BLK
        cb, sb = cos[rs, :], sin[rs, :]
        place = lax.broadcasted_iota(jnp.int32, (BLK, 1), 0) + i * BLK
        bias = mask_bias(doc_starts(lengths, place), valid, i, keys)
        bias2 = jnp.concatenate([bias, bias], axis=0)
        lse_i = lse[rs, :]
        for n in range(nkv):
            ns = slice(n * 128, (n + 1) * 128)
            qn, dn = q[rs, ns], do[rs, ns]
            zero = jnp.zeros_like(qn)
            q2 = jnp.concatenate([jnp.where(low, qn, zero), jnp.where(low, zero, qn)], axis=0)
            d2 = jnp.concatenate([jnp.where(low, dn, zero), jnp.where(low, zero, dn)], axis=0)
            h = 2 * (first + n)
            l2 = jnp.concatenate([lse_i[:, h : h + 1], lse_i[:, h + 1 : h + 2]], axis=0)
            p = jnp.exp(dot_nt(q2, kd[:keys, ns]) + bias2 - l2)
            dp = dot_nt(d2, vd[:keys, ns])
            shift = jnp.sum(p * dp, axis=1, keepdims=True)
            ds = (p * (dp - shift)).astype(BF)
            dv[:keys, ns] += dot_tn(p.astype(BF), d2)
            dk[:keys, ns] += dot_tn(ds, q2)
            dq2 = dot(ds, kd[:keys, ns])
            dqn = jnp.where(low, dq2[:BLK], dq2[BLK:]) * ATTN_SCALE
            dq[rs, ns] = (dqn * cb - swap_halves(dqn, lane) * sb).astype(BF)
    for i in range(nb):
        rs = pl.ds(i * BLK, BLK)
        cb, sb = cos[rs, :], sin[rs, :]
        for n in range(nkv):
            ns = slice(n * 128, (n + 1) * 128)
            kk = dk[rs, ns]
            kk = kk + pltpu.roll(kk, HD, 1)
            vv = dv[rs, ns]
            vv = vv + pltpu.roll(vv, HD, 1)
            dkv[rs, ns] = jnp.where(low, kk * cb - swap_halves(kk, lane) * sb, vv).astype(BF)
    for copy in copies:
        copy.wait()
    gq = dot_tn(h1[...], dq[...])
    gk = dot_tn(h1[...], dkv[...])
    gw[:, :wid] = gq.astype(BF)
    gw[:, wid : 2 * wid] = gk.astype(BF)
    ga = jnp.sum(gq * wq[...].astype(F32) + gk * wkv[...].astype(F32), axis=1, keepdims=True) / gain[...].astype(F32)
    lanes = lax.broadcasted_iota(jnp.int32, (width, 128), 1)
    ga = jnp.where(lanes == GAIN_A, ga, 0.0)
    for v in more:
        ga = ga + v[...]
    sums[...] = ga
    if places:
        gwo = dot_tn(o[...], da[...]).astype(BF)
        depth = gwo.shape[0]
        for n in range(width // depth):
            rs = slice(n * depth, (n + 1) * depth)
            gw[rs, 2 * wid : 2 * wid + depth] = gwo[:, rs]
    else:
        gw[:, 2 * wid :] = ga.astype(BF)
    size = width // len(pieces)
    for k, piece in enumerate(pieces):
        piece[...] = gw[pl.ds(pl.multiple_of((at[0] ^ k) * size, size), size), :]


def placed(core, parts, i):
    if len(parts) == 1:
        return parts[0][i * BLK : (i + 1) * BLK, :].astype(F32)
    n = len(parts) // 2
    mine, other = parts[i % n][...].astype(F32), parts[n + i % n][...].astype(F32)
    return jnp.where(core[0] == i // n, mine, other)


def attn_backward(first, count, core, at, npiece, lengths, q, kd, vd, lse, h1, cos, sin, valid, wq, wkv, gain, sums, do=None, given=None):
    rows, width = h1.shape
    w = count * 128
    depth = given[1].shape[0] if given else 128
    cols = 2 * w + depth
    shape = jax.ShapeDtypeStruct
    part = pl.BlockSpec((rows, w), lambda _: (0, first // count))
    full = lambda *s: pl.BlockSpec(s, lambda _: (0, 0))
    there = pl.BlockSpec(memory_space=pl.ANY)
    size = width // npiece
    outs = [(rows, w)] * 2 + [(width, 128)] + [(size, cols)] * npiece
    types = [BF, BF, F32] + [BF] * npiece
    scratch = [
        pltpu.VMEM((rows, w), F32),
        pltpu.VMEM((rows, w), F32),
        pltpu.VMEM((width, cols), BF),
        pltpu.VMEM((rows, width), BF),
        pltpu.VMEM((width, w), BF),
        pltpu.VMEM((width, w), BF),
        pltpu.SemaphoreType.DMA((4,)),
    ]
    if given:
        cot, wo, o, *parts = given
        last = [cot, wo, o, *parts]
        last_specs = [whole_block(cot), whole_block(wo), there] + [whole_block(v) for v in parts]
        outs += [(rows, depth), (rows, width)]
        types += [BF, BF]
        scratch += [pltpu.VMEM((rows, width), BF), pltpu.VMEM((rows, depth), BF)]
    else:
        parts, last, last_specs = (), [do], [part]
    return pl.pallas_call(
        functools.partial(attn_backward_body, first, len(parts), len(sums), npiece, bool(given)),
        grid=(1,),
        in_specs=[pl.BlockSpec(memory_space=pltpu.SMEM)] * 3
        + [part] * 3
        + [whole_block(v) for v in (lse, cos, sin, valid, gain)]
        + [there] * 3
        + [whole_block(v) for v in sums]
        + last_specs,
        out_specs=[full(*s) for s in outs],
        out_shape=[shape(s, d) for s, d in zip(outs, types, strict=True)],
        scratch_shapes=scratch,
        compiler_params=pltpu.CompilerParams(vmem_limit_bytes=VMEM_BYTES),
        cost_estimate=cost(4 * rows * width * w + 20 * rows * rows * w, 10 * rows * width),
        name="attention_backward",
    )(core, at, lengths, q, kd, vd, lse, cos, sin, valid, gain, h1, wq, wkv, *sums, *last)


def on_device(
    tokens,
    gain_attn,
    query_weight_matrix,
    key_value_weight,
    w_out,
    gain_ffn,
    w_router,
    w_gate_up,
    w_down,
    routes,
    doc_lengths,
    valid_mask,
    cotangent,
):
    rows, width = tokens.shape
    share = routes.shape[0]
    n_ep, n_tp = lax.axis_size("ep"), lax.axis_size("tp")
    nexp = w_router.shape[1]
    inner = math.gcd(n_ep, 4)
    outer = n_ep // inner
    me = lax.axis_index("ep")
    me_in = me % inner
    core = lax.axis_index("tp")[None]
    pair = n_tp == 2

    def across(v, k):
        return lax.ppermute(v, "ep", [(i, i ^ k) for i in range(n_ep)])

    def along(v, k):
        return lax.ppermute(v, "ep", [(i, (i + k * inner) % n_ep) for i in range(n_ep)])

    def swap(v):
        return lax.ppermute(v, "tp", [(0, 1), (1, 0)])

    def after(v, *earlier):
        return lax.optimization_barrier((v, *earlier))[0]

    def total(terms):
        acc = terms[0].astype(F32)
        for term in terms[1:]:
            acc = acc + term.astype(F32)
        return acc

    def scatter_plane(pieces):
        return [pieces[0]] + [across(pieces[k], k) for k in range(1, inner)]

    def cut_rows(v, k):
        size = v.shape[0] // inner
        return lax.dynamic_slice_in_dim(v, (me_in ^ k) * size, size)

    def summed(terms):
        return total(terms).astype(BF)

    def column_steps(v):
        bit = 1
        while bit < outer:
            other = lax.ppermute(v, "ep", [(i, i ^ (bit * inner)) for i in range(n_ep)])
            yield other
            v = summed([v, release(other)])
            bit *= 2
        yield v

    def unpacked(v):
        f = v.shape[2]
        return v[:2], v[2].reshape(width // f, f, f).transpose(1, 0, 2).reshape(f, width)

    def packed(gu, down):
        f = gu.shape[2]
        return jnp.concatenate([gu, down.reshape(f, width // f, f).transpose(1, 0, 2).reshape(1, width, f)])

    def full_hidden(v):
        if pair:
            return [v, swap(v)]
        gu, down = unpacked(v)
        return [
            packed(
                lax.all_gather(gu, "tp", axis=2, tiled=True),
                lax.all_gather(down, "tp", axis=0, tiled=True),
            )
        ]

    def own_hidden(v):
        if pair:
            return v[0].astype(F32) + swap(v[1]).astype(F32)
        gu, down = unpacked(v[0].astype(F32))
        return packed(
            lax.psum_scatter(gu, "tp", scatter_dimension=2, tiled=True),
            lax.psum_scatter(down, "tp", scatter_dimension=0, tiled=True),
        )

    halves = 2 if pair else 1
    local = jnp.arange(outer, dtype=jnp.int32) * inner
    ids = (me - local) % n_ep
    ids_all = jnp.concatenate([((me ^ k) - local) % n_ep for k in range(inner)])
    valid_row = valid_mask[None, :]
    live_all = valid_mask.astype(F32)[:, None]
    live = lax.dynamic_slice_in_dim(live_all, core[0] * share, share)
    gain_a, gain_f = gain_attn[None, :], gain_ffn[None, :]
    wr = jnp.pad(w_router, ((0, 0), (0, 128 - nexp)))

    tok = core

    def finish(*values):
        nonlocal tok
        tok = after(tok, *values)

    def release(v):
        return after(v, tok)

    pack, pay = prepare(tok, w_gate_up, w_down, cotangent, routes.T)
    held = [pack]
    if outer > 1:
        held.append(along(pack, 1))
    pays = [pay] + [across(pay, k) for k in range(1, min(inner, 3))]
    chunks = [full_hidden(pack)]
    finish(pack)

    h1, q, kd, vd, o, lse, cos, sin, *part = attn_forward(
        tok, doc_lengths, tokens, gain_a, query_weight_matrix, key_value_weight, w_out, valid_row, pair
    )
    if pair:
        own, other = part[0], swap(part[1])
    else:
        own = lax.psum_scatter(part[0].astype(F32), "tp", scatter_dimension=0, tiled=True)
        other = jnp.zeros_like(own)
    finish(own, other, *pays, *chunks[0])
    mid, h2, stats = middle_norm(tok, tokens, own, other, gain_f, live_all)
    h2s = [h2] + [across(h2, k) for k in range(1, min(inner, 3))]
    finish(h2, *held[1:])

    near = min(2, outer)
    last = outer - 1
    far = list(range(3, inner))
    close = list(range(min(inner, 3)))
    state = [None] * inner
    saved = [dict() for _ in range(inner)]

    def work(blocks, first, count):
        prevs = None if state[blocks[0]] is None else [state[b] for b in blocks]
        out = experts(
            release(ids),
            [h2s[b] for b in blocks],
            [pays[b] for b in blocks],
            prevs,
            wr,
            [c for r in range(first, first + count) for c in chunks[r]],
            halves,
            first,
        )
        for b, (dx, moe, gat, dgu) in zip(blocks, out, strict=True):
            state[b] = (dx, moe)
            for r in range(count):
                saved[b][first + r] = (gat, dgu, r * halves)
        finish(out[0][1])

    def expert_grads(experts_of):
        out = weight_grads(tok, h2s, pays, [[s[r] for r in experts_of] for s in saved], halves)
        finish(out[0])
        return out

    def next_held():
        v = release(held[-1])
        if len(held) < outer:
            held.append(along(v, 1))
        chunks.append(full_hidden(v))

    if outer > 1:
        next_held()
    work([0], 0, near)
    finish(*h2s)
    for k in far:
        pays.append(across(release(pay), k))
    if close[1:]:
        work(close[1:], 0, near)
    if outer > 2:
        finish(held[-1])
        next_held()
    finish(*pays)
    for k in far:
        h2s.append(across(release(h2), k))
    for r in range(near, last):
        work(close, r, 1)
        if r + 1 < last:
            finish(held[-1])
            next_held()
    finish(*h2s)
    for b in far:
        work([b], 0, max(last, near))
    if last >= near:
        finish(held[-1])
        next_held()

    first = 1 % outer
    later = [[r] for r in range(2, min(outer, 3))] + [[*range(3, outer), 0]]
    later = later if outer > 1 else []
    raw = expert_grads([first])
    parts = {first: own_hidden([v[0] for v in raw])}
    if last >= near and inner > 1:
        work(list(range(1, inner)), last, 1)
    ring = parts[first].astype(BF)
    finish(ring)
    if outer > 1:
        ring = along(ring, 1)
    dxs = [None] + [across(state[k][0], k) for k in range(1, inner)]
    if last >= near:
        work([0], last, 1)
    dxs[0] = state[0][0]
    raws = [expert_grads(rs) for rs in later]
    finish(*dxs, *([ring] if outer > 1 else []))
    moes = [state[0][1]] + [across(release(state[k][1]), k) for k in range(1, inner)]
    early = [swap(release(raw[1])) if pair and rs == [2] else None for rs, raw in zip(later, raws, strict=True)]

    def ring_step(r):
        nonlocal ring
        term = release(ring).astype(F32) + parts[r]
        if r == 0:
            return term
        ring = term.astype(BF)
        finish(ring)
        ring = along(ring, 1)

    *gm, small = middle_back(tok, ids_all, h2, mid, gain_f, pay, wr, dxs, outer)
    finish(small)
    if pair:
        gm = [*gm, *[swap(v) for v in gm]]
    else:
        gm = [lax.all_gather(jnp.concatenate(gm), "tp", axis=0, tiled=True)]
    for rs, raw, other in zip(later, raws, early, strict=True):
        if not pair:
            parts.update({r: own_hidden([raw[0][n]]) for n, r in enumerate(rs)})
        else:
            other = release(other) if other is not None else swap(release(raw[1]))
            parts.update({r: raw[0][n].astype(F32) + other[n].astype(F32) for n, r in enumerate(rs)})
    if outer > 2:
        ring_step(2)
    nkv = kd.shape[1] // 128
    groups = 2 if nkv % 2 == 0 else 1
    each = nkv // groups
    w = each * 128
    depth = w_out.shape[0]
    dqs, dkvs, sums = [], [], small
    at = me_in[None]
    for n in range(groups):
        first_one = n == 0
        out = attn_backward(
            n * each,
            each,
            tok,
            at,
            inner,
            doc_lengths,
            q,
            kd,
            vd,
            lse,
            h1,
            cos,
            sin,
            valid_row,
            query_weight_matrix,
            key_value_weight,
            gain_attn[:, None],
            [sums],
            None if first_one else do,
            (cotangent, w_out, o, *gm) if first_one else None,
        )
        dq, dkv, sums, *pieces = out[: 3 + inner]
        if first_one:
            do, gm_all = out[3 + inner :]
        finish(pieces[0])
        dqs.append(dq)
        dkvs.append(dkv)
        if first_one and groups > 1:
            terms = scatter_plane(pieces)
            if outer > 3:
                finish(ring)
                ring_step(3)
    if groups == 1:
        sums_only = [cut_rows(sums.astype(BF), k) for k in range(inner)]
        terms = scatter_plane([jnp.concatenate(v, axis=1) for v in zip(pieces, sums_only, strict=True)])
    finish(*moes)
    out_share, stats_out = layer_out_share(tok, mid, live, moes)
    finish(out_share)
    spread = jnp.pad((stats + stats_out)[:1, :4], ((0, 0), (STATS, 128 - STATS - 4)))

    def closing_sum(terms):
        v = total([release(t) for t in terms])
        row = lax.broadcasted_iota(jnp.int32, v.shape, 0)
        lane = lax.broadcasted_iota(jnp.int32, v.shape, 1) - (v.shape[1] - 128)
        place = (row == 0) & (lane >= STATS) & (lane < STATS + 4)
        return jnp.where(place, jnp.pad(spread, ((0, 0), (v.shape[1] - 128, 0))), v).astype(BF)

    def spread_plane(v):
        return [v] + [across(v, k) for k in range(1, inner)]

    if groups > 1:
        finish(*terms)
        ahead = column_steps(summed([release(t) for t in terms]))
        moving = next(ahead)
        terms = scatter_plane([release(v) for v in pieces])
    dh1 = input_back(tok, query_weight_matrix, key_value_weight, dqs, dkvs)
    finish(dh1, *([ring] if outer > 1 else []), *([moving] if groups > 1 else []))
    if groups > 1:
        moving = next(ahead)
    if pair:
        dh_other = swap(release(dh1))
    else:
        dh1, dh_other = lax.psum(dh1.astype(F32), "tp"), jnp.zeros_like(dh1)
    finish(dh_other)
    grad_tokens = token_grads(tok, tokens, cotangent, dh1, dh_other, gm_all, gain_a)
    finish(grad_tokens, *terms)
    if pair:
        out_other = swap(out_share)
    closing = closing_sum(terms)
    if groups > 1:
        finish(moving)
    behind = column_steps(release(closing))
    late = next(behind)
    if pair:
        layer_out = jnp.where(
            core[0] == 0,
            jnp.concatenate([release(out_share), out_other]),
            jnp.concatenate([out_other, release(out_share)]),
        )
        finish(layer_out)
    else:
        layer_out = lax.all_gather(out_share, "tp", axis=0, tiled=True)
    for r in range(4, outer):
        ring_step(r)
    expert_sums = ring_step(0) if outer > 1 else parts[0]
    gu_grad, down_grad = unpacked(expert_sums)
    spreads = []
    if groups > 1:
        for whole in ahead:
            pass
        spreads.append(spread_plane(release(whole)))
    finish(late)
    for whole in behind:
        pass
    spreads.append(spread_plane(release(whole)))
    if groups > 1:
        *grads, folded = gather_rows(at, spreads[0], (w, w, depth), groups, False)
        finish(folded)
        grad_w_query, grad_w_kv, extras = gather_rows(release(at), spreads[1], (w, w, 128), groups, True, grads)
    else:
        grad_w_query, grad_w_kv, folded, extras = gather_rows(release(at), spreads[0], (w, w, depth, 128), 1, True)
    grad_w_out = jnp.concatenate([folded[n * depth : (n + 1) * depth] for n in range(width // depth)], axis=1)
    extras = extras[: STATS + 6]
    extras = extras + swap(extras) if pair else lax.psum(extras, "tp")
    s = jnp.sum(extras[STATS : STATS + 4, :: width // inner], axis=1)
    return (
        layer_out,
        grad_tokens,
        extras[GAIN_A],
        grad_w_query,
        grad_w_kv,
        grad_w_out,
        extras[GAIN_F],
        extras[:nexp].T,
        gu_grad[None],
        down_grad[None],
        jnp.sqrt(s[:3] / (s[3] * width)),
    )


def solution(mesh):
    return jax.shard_map(
        on_device,
        mesh=mesh,
        in_specs=(
            P("ep", None),
            P(),
            P(None, "tp"),
            P(None, "tp"),
            P("tp", None),
            P(),
            P(),
            P("ep", None, None, "tp"),
            P("ep", "tp", None),
            P(("ep", "tp"), None),
            P("ep", None),
            P("ep"),
            P("ep", None),
        ),
        out_specs=(
            P("ep", None),
            P("ep", None),
            P(),
            P(None, "tp"),
            P(None, "tp"),
            P("tp", None),
            P(),
            P(),
            P("ep", None, None, "tp"),
            P("ep", "tp", None),
            P(),
        ),
        check_vma=False,
    )
```

```python
import functools
import math

import jax
import jax.numpy as jnp
from jax import lax
from jax.experimental import pallas as pl
from jax.experimental.pallas import tpu as pltpu
from jax.sharding import PartitionSpec as P

SEQUENCE_LENGTH = 1024
WINDOW = 1024
ATTN_SCALE = 0.015625
RESID_SCALE = 0.22
TOPK = 8
NORM_EPS = 1e-06
ROPE_BASE = 10000.0
F32 = jnp.float32
BF = jnp.bfloat16
VMEM_BYTES = 60 * 1024 * 1024
COST = 0.02
GAIN_F, GAIN_A, STATS = 32, 33, 34


def cost(flops, bytes_accessed, transcendentals=0):
    return pl.CostEstimate(
        flops=int(COST * flops), bytes_accessed=int(COST * bytes_accessed), transcendentals=int(COST * transcendentals)
    )


def dot(a, b):
    return jnp.dot(a, b, preferred_element_type=F32)


def dot_nt(a, b):
    return lax.dot_general(a, b, (((1,), (1,)), ((), ())), preferred_element_type=F32)


def dot_tn(a, b):
    return lax.dot_general(a, b, (((0,), (0,)), ((), ())), preferred_element_type=F32)


def whole_block(v):
    return pl.BlockSpec(v.shape, lambda *_: (0,) * len(v.shape))


def gate_rows(h2, routes, wr):
    rows = h2.shape[0]
    lane = lax.broadcasted_iota(jnp.int32, (rows, 128), 1).astype(F32)
    picks = routes.astype(F32).T
    mask = picks[:, 0:1] == lane
    for k in range(1, TOPK):
        mask = mask | (picks[:, k : k + 1] == lane)
    sel = jnp.where(mask, dot(h2, wr[...]), -jnp.inf)
    weight = jnp.exp(sel - jnp.max(sel, axis=1, keepdims=True))
    return weight / jnp.sum(weight, axis=1, keepdims=True)


def gate_table(h2, pay, wr):
    rows = h2.shape[0]
    return gate_rows(h2[...], pay[rows : rows + 16, :rows], wr)


def middle_body(core, x, own, other, gain, live, mid, h2, stats):
    attn = RESID_SCALE * (own[...].astype(F32) + other[...].astype(F32))
    m = x[...].astype(F32) + attn
    mid[...] = m
    r = lax.rsqrt(jnp.mean(m * m, axis=1, keepdims=True) + NORM_EPS)
    h2[...] = (m * r * gain[...].astype(F32)).astype(BF)
    v = live[...]
    total = jnp.sum(v * jnp.sum(attn * attn, axis=1, keepdims=True))
    lane = lax.broadcasted_iota(jnp.int32, stats.shape, 1)
    stats[...] = jnp.where(lane == 1, total, jnp.where(lane == 3, jnp.sum(v), 0.0))


def middle_norm(core, x, own, other, gain, live):
    share, width = own.shape
    shape = jax.ShapeDtypeStruct
    part = lambda n: pl.BlockSpec((share, n), lambda _, c: (c[0], 0))
    full = lambda *s: pl.BlockSpec(s, lambda *_: (0, 0))
    return pl.pallas_call(
        middle_body,
        grid_spec=pltpu.PrefetchScalarGridSpec(
            num_scalar_prefetch=1,
            grid=(1,),
            in_specs=[part(width), whole_block(own), whole_block(other), whole_block(gain), part(1)],
            out_specs=[full(share, width), full(share, width), full(8, 128)],
        ),
        out_shape=[shape((share, width), F32), shape((share, width), BF), shape((8, 128), F32)],
        compiler_params=pltpu.CompilerParams(vmem_limit_bytes=VMEM_BYTES),
        cost_estimate=cost(10 * share * width, 12 * share * width),
        name="middle_norm",
    )(core, x, own, other, gain, live)


def experts_body(nb, nchunk, halves, *refs):
    ids = refs[0]
    at = 1
    h2s, pays = refs[at : at + nb], refs[at + nb : at + 2 * nb]
    at += 2 * nb
    wr = refs[at]
    packs = refs[at + 1 : at + 1 + nchunk]
    at += 1 + nchunk
    outs = [refs[at + 5 * b : at + 5 * b + 5] for b in range(nb)]
    at += 5 * nb
    dgacc, macc, xacc, buf, sem = refs[at:]
    c = pl.program_id(0)
    rows, width = h2s[0].shape
    f = buf.shape[3]
    lane = lax.broadcasted_iota(jnp.int32, (rows, 128), 1)

    @pl.when(c == 0)
    def _():
        pltpu.make_async_copy(packs[0], buf.at[0], sem.at[0]).start()
        for b in range(nb):
            outs[b][4][...] = gate_table(h2s[b], pays[b], wr)
        macc[...] = jnp.zeros_like(macc)
        xacc[...] = jnp.zeros_like(xacc)
        dgacc[...] = jnp.zeros_like(dgacc)

    for k in range(1, nchunk):

        @pl.when(c + 1 == k)
        def _(k=k):
            pltpu.make_async_copy(packs[k], buf.at[k % 2], sem.at[k % 2]).start()

    slot = lax.rem(c, 2)
    pltpu.make_async_copy(packs[0], buf.at[slot], sem.at[slot]).wait()
    r = c // halves
    e = ids[r]
    nd = width // f
    for b in range(nb):
        g, gat, dgu = pays[b], outs[b][2], outs[b][3]
        hb = h2s[b][...]
        gp = dot(hb, buf[slot, 0])
        up = dot(hb, buf[slot, 1])
        u = sum(dot_nt(g[:rows, k * f : (k + 1) * f], buf[slot, 2, k * f : (k + 1) * f, :]) for k in range(nd))
        gate = jnp.sum(jnp.where(lane == e, outs[b][4][...], 0.0), axis=1, keepdims=True)
        sg = jax.nn.sigmoid(gp)
        sl = gp * sg
        act = sl * up
        ga = (gate * act).astype(BF)
        dgacc[b] += jnp.where(lane == r, jnp.sum(act * u, axis=1, keepdims=True) * RESID_SCALE, 0.0)
        da = (RESID_SCALE * gate) * u
        dgp = (da * up * (sg + sl * (1.0 - sg))).astype(BF)
        dup = (da * sl).astype(BF)
        gat[0] = ga.T
        dgu[0, :, :f] = dgp
        dgu[0, :, f:] = dup
        for k in range(nd):
            macc[b, :, k * f : (k + 1) * f] += dot(ga, buf[slot, 2, k * f : (k + 1) * f, :])
        xacc[b] += dot_nt(dgp, buf[slot, 0]) + dot_nt(dup, buf[slot, 1])

    @pl.when(c == nchunk - 1)
    def _():
        for b in range(nb):
            dx, moe = outs[b][:2]
            moe[...] = macc[b].astype(BF)
            dx[:rows, :] = xacc[b].astype(BF)
            dx[rows:, :] = jnp.zeros((16, width), BF)
            dx[rows:, :rows] = gate_tail(dgacc[b])


def gate_tail(dg):
    dg = dg.T[:8]
    high = dg.astype(BF).astype(F32)
    return jnp.concatenate([high, dg - high], axis=0).astype(BF)


def experts(ids, h2s, pays, wr, packs, halves):
    rows, width = h2s[0].shape
    nb, nchunk = len(h2s), len(packs)
    f = packs[0].shape[2]
    ne, hidden = nchunk // halves, halves * f
    shape = jax.ShapeDtypeStruct
    once = lambda v: pl.BlockSpec(v.shape, lambda *_: (0,) * len(v.shape), pipeline_mode=pl.Buffered(1))
    out = pl.pallas_call(
        functools.partial(experts_body, nb, nchunk, halves),
        grid_spec=pltpu.PrefetchScalarGridSpec(
            num_scalar_prefetch=1,
            grid=(nchunk,),
            in_specs=[once(v) for v in (*h2s, *pays, wr)] + [pl.BlockSpec(memory_space=pl.ANY)] * nchunk,
            out_specs=[
                pl.BlockSpec((rows + 16, width), lambda c, _: (0, 0)),
                pl.BlockSpec((rows, width), lambda c, _: (0, 0)),
                pl.BlockSpec((1, f, rows), lambda c, _: (c // halves, c % halves, 0)),
                pl.BlockSpec((1, rows, 2 * f), lambda c, _: (c // halves, 0, c % halves)),
                pl.BlockSpec((rows, 128), lambda c, _: (0, 0)),
            ]
            * nb,
            scratch_shapes=[
                pltpu.VMEM((nb, rows, 128), F32),
                pltpu.VMEM((nb, rows, width), F32),
                pltpu.VMEM((nb, rows, width), F32),
                pltpu.VMEM((2, 3, width, f), BF),
                pltpu.SemaphoreType.DMA((2,)),
            ],
        ),
        out_shape=[
            shape((rows + 16, width), BF),
            shape((rows, width), BF),
            shape((ne, hidden, rows), BF),
            shape((ne, rows, 2 * hidden), BF),
            shape((rows, 128), F32),
        ]
        * nb,
        compiler_params=pltpu.CompilerParams(vmem_limit_bytes=VMEM_BYTES),
        cost_estimate=cost(12 * rows * width * f * nchunk * nb, 6 * nchunk * width * f + 12 * rows * width * nb),
        name="experts",
    )(ids, *h2s, *pays, wr, *packs)
    return [out[5 * b : 5 * b + 5] for b in range(nb)]


def weight_copies(packs, wgu, wd, sem, halves):
    out = []
    for h in range(halves):
        pack = packs[h]
        f = pack.shape[2]
        for j in range(2):
            cols = pl.ds((2 * h + j) * f, f)
            out.append(pltpu.make_async_copy(pack.at[j], wgu.at[:, cols], sem.at[len(out)]))
        for k in range(pack.shape[1] // f):
            rows, cols = pl.ds(h * f, f), pl.ds(k * f, f)
            out.append(pltpu.make_async_copy(pack.at[2, pl.ds(k * f, f), :], wd.at[rows, cols], sem.at[len(out)]))
    return out


def one_expert_body(nb, halves, r, ids, *refs):
    it = iter(refs)
    take = lambda n: [next(it) for _ in range(n)]
    h2s, pays, gates = take(nb), take(nb), take(nb)
    prevs = [take(2) for _ in range(nb)]
    packs = take(halves)
    outs = [take(4) for _ in range(nb)]
    ga_all, wgu, wd, sem = it
    rows, width = h2s[0].shape
    f = wd.shape[0] // halves
    copies = weight_copies(packs, wgu, wd, sem, halves)
    for copy in copies:
        copy.start()
    lane = lax.broadcasted_iota(jnp.int32, (rows, 128), 1)
    for copy in copies:
        copy.wait()
    for b in range(nb):
        dx, moe, gat, dgu = outs[b]
        gu = dot(h2s[b][...], wgu[...])
        u = dot_nt(pays[b][:rows, :], wd[...])
        gate = jnp.sum(jnp.where(lane == ids[r], gates[b][...], 0.0), axis=1, keepdims=True)
        small = RESID_SCALE * gate
        dg = jnp.zeros((rows, 1), F32)
        for h in range(halves):
            gp, up = gu[:, 2 * h * f : (2 * h + 1) * f], gu[:, (2 * h + 1) * f : (2 * h + 2) * f]
            uh = u[:, h * f : (h + 1) * f]
            sg = jax.nn.sigmoid(gp)
            sl = gp * sg
            act = sl * up
            ga = (gate * act).astype(BF)
            dg = dg + jnp.sum(act * uh, axis=1, keepdims=True)
            da = small * uh
            gat[0, h * f : (h + 1) * f, :] = ga.T
            ga_all[:, h * f : (h + 1) * f] = ga
            dgu[0, :, 2 * h * f : (2 * h + 1) * f] = (da * up * (sg + sl * (1.0 - sg))).astype(BF)
            dgu[0, :, (2 * h + 1) * f : (2 * h + 2) * f] = (da * sl).astype(BF)
        before = prevs[b]
        moe[...] = (before[1][...].astype(F32) + dot(ga_all[...], wd[...])).astype(BF)
        dx[:rows, :] = (before[0][:rows, :].astype(F32) + dot_nt(dgu[0], wgu[...])).astype(BF)
        mine = lax.broadcasted_iota(jnp.int32, (16, rows), 0) % 8 == r
        dx[rows:, :] = before[0][rows:, :]
        tail = gate_tail(jnp.where(lane == r, dg * RESID_SCALE, 0.0))
        dx[rows:, :rows] = jnp.where(mine, tail.astype(F32), before[0][rows:, :rows].astype(F32)).astype(BF)


def one_expert(ids, h2s, pays, gates, prevs, packs, r):
    rows, width = h2s[0].shape
    nb, halves = len(h2s), len(packs)
    f = packs[0].shape[2]
    hidden = halves * f
    flat = [v for prev in prevs for v in prev]
    shape = jax.ShapeDtypeStruct
    vmem = pl.BlockSpec(memory_space=pltpu.VMEM)
    out = pl.pallas_call(
        functools.partial(one_expert_body, nb, halves, r),
        in_specs=[pl.BlockSpec(memory_space=pltpu.SMEM)]
        + [vmem] * (5 * nb)
        + [pl.BlockSpec(memory_space=pl.ANY)] * halves,
        out_specs=[vmem] * (4 * nb),
        scratch_shapes=[
            pltpu.VMEM((rows, hidden), BF),
            pltpu.VMEM((width, 2 * hidden), BF),
            pltpu.VMEM((hidden, width), BF),
            pltpu.SemaphoreType.DMA((halves * (2 + width // f),)),
        ],
        out_shape=[
            shape((rows + 16, width), BF),
            shape((rows, width), BF),
            shape((1, hidden, rows), BF),
            shape((1, rows, 2 * hidden), BF),
        ]
        * nb,
        compiler_params=pltpu.CompilerParams(vmem_limit_bytes=VMEM_BYTES),
        cost_estimate=cost(12 * rows * width * hidden * nb, 6 * width * hidden + 12 * rows * width * nb),
        name="one_expert",
    )(ids, *h2s, *pays, *gates, *flat, *packs)
    return [out[4 * b : 4 * b + 4] for b in range(nb)]


def weight_grads_body(nb, halves, _, *refs):
    h2 = refs[:nb]
    g = refs[nb : 2 * nb]
    hidden, outs = refs[2 * nb : -halves], refs[-halves:]
    e, c = pl.program_id(0), pl.program_id(1)
    rows = h2[0].shape[0]
    width, f = outs[0].shape[2:]
    for n in range(len(hidden) // (2 * nb)):

        @pl.when(e == n)
        def _(n=n):
            gat, dgu = hidden[2 * nb * n : 2 * nb * n + nb], hidden[2 * nb * n + nb : 2 * nb * (n + 1)]
            acc = sum(dot_tn(h2[b][...], dgu[b][0]) for b in range(nb))
            down = sum(dot(gat[b][0], g[b][:rows, :]) for b in range(nb)) * RESID_SCALE
            for half in range(halves):

                @pl.when(c == half)
                def _(out=outs[half]):
                    out[0, 0] = acc[:, :f].astype(BF)
                    out[0, 1] = acc[:, f:].astype(BF)
                    for k in range(width // f):
                        out[0, 2, k * f : (k + 1) * f, :] = down[:, k * f : (k + 1) * f].astype(BF)


def weight_grads(tok, h2s, pays, saved, halves):
    nb, ne = len(h2s), len(saved[0])
    rows, width = h2s[0].shape
    f = saved[0][0][0].shape[1] // halves
    shape = jax.ShapeDtypeStruct
    once = lambda v: pl.BlockSpec(v.shape, lambda *_: (0,) * len(v.shape), pipeline_mode=pl.Buffered(1))
    specs, args = [], []
    for n in range(ne):
        half = lambda e, c, n=n: jnp.where(e < n, 0, jnp.where(e == n, c, halves - 1))
        for b in range(nb):
            ga, dg, o = saved[b][n]
            args.append(ga)
            specs.append(pl.BlockSpec((1, f, rows), lambda e, c, o=o, half=half: (o, half(e, c), 0)))
        for b in range(nb):
            ga, dg, o = saved[b][n]
            args.append(dg)
            specs.append(pl.BlockSpec((1, rows, 2 * f), lambda e, c, o=o, half=half: (o, 0, half(e, c))))
    return pl.pallas_call(
        functools.partial(weight_grads_body, nb, halves),
        grid=(ne, halves),
        in_specs=[pl.BlockSpec(memory_space=pltpu.SMEM)] + [once(v) for v in (*h2s, *pays)] + specs,
        out_specs=[pl.BlockSpec((1, 3, width, f), lambda e, c: (e, 0, 0, 0))] * halves,
        out_shape=[shape((ne, 3, width, f), BF)] * halves,
        compiler_params=pltpu.CompilerParams(vmem_limit_bytes=VMEM_BYTES),
        cost_estimate=cost(6 * rows * nb * width * f * halves, 6 * halves * width * f + 4 * rows * nb * width),
        name="expert_weight_grads",
    )(tok, *h2s, *pays, *args)


def middle_back_body(nb, nlocal, _, ids, h2, mid, gain, gate, wr, *refs):
    dxs, tails = refs[:nb], refs[nb : 2 * nb]
    gm, small, acc = refs[2 * nb :]
    rows, width = h2.shape
    at = pl.program_id(0)
    cols = pl.ds(pl.multiple_of(at * rows, rows), rows)
    lane = lax.broadcasted_iota(jnp.int32, (rows, 128), 1)
    gates = gate[...]
    dgate = jnp.zeros((rows, 128), F32)
    for b in range(nb):
        part = tails[b][:, cols].astype(F32)
        part = (part[:8] + part[8:]).T
        for r in range(nlocal):
            dgate = jnp.where(lane == ids[b * nlocal + r], part[:, r : r + 1], dgate)
    dsel = gates * (dgate - jnp.sum(gates * dgate, axis=1, keepdims=True))
    high = dsel.astype(BF)
    rest = (dsel - high.astype(F32)).astype(BF)
    router = dot_tn(h2[...], high) + dot_tn(h2[...], rest)
    dh = dot_nt(high, wr[...]) + dot_nt(rest, wr[...])
    for b in range(nb):
        dh = dh + dxs[b][...].astype(F32)
    m = mid[...]
    r2 = lax.rsqrt(jnp.mean(m * m, axis=1, keepdims=True) + NORM_EPS)
    xhat = m * r2
    col = jnp.broadcast_to(jnp.sum(dh * xhat, axis=0, keepdims=True), (8, width)).T[:, :1]
    su = dh * gain[...].astype(F32)
    grad = (r2 * (su - xhat * jnp.mean(su * xhat, axis=1, keepdims=True))).astype(BF)
    gm[0] = grad
    gm[1] = grad
    small_here = jnp.where(lax.broadcasted_iota(jnp.int32, (width, 128), 1) == GAIN_F, col, router)

    @pl.when(at == 0)
    def _():
        acc[...] = small_here

    @pl.when(at > 0)
    def _():
        acc[...] += small_here

    small[...] = acc[...]


def middle_back(tok, ids, h2, mid, gain, gates, wr, dxs, nlocal):
    rows, width = h2.shape
    rt = rows // 2 if rows % 512 == 0 else rows
    shape = jax.ShapeDtypeStruct
    block = pl.BlockSpec((rt, width), lambda i: (i, 0))
    tail = pl.BlockSpec((16, width), lambda i: (rows // 16, 0))
    whole = lambda v: pl.BlockSpec(v.shape, lambda i: (0, 0))
    small = pl.BlockSpec((width, 128), lambda i: (0, 0))
    return pl.pallas_call(
        functools.partial(middle_back_body, len(dxs), nlocal),
        grid=(rows // rt,),
        in_specs=[pl.BlockSpec(memory_space=pltpu.SMEM)] * 2
        + [block, block, whole(gain), pl.BlockSpec((rt, 128), lambda i: (i, 0)), whole(wr)]
        + [block] * len(dxs)
        + [tail] * len(dxs),
        out_specs=[pl.BlockSpec((2, rt, width), lambda i: (0, i, 0)), small],
        out_shape=[shape((2, rows, width), BF), shape((width, 128), F32)],
        scratch_shapes=[pltpu.VMEM((width, 128), F32)],
        compiler_params=pltpu.CompilerParams(vmem_limit_bytes=VMEM_BYTES),
        cost_estimate=cost(40 * rows * width, 20 * rows * width),
        name="middle_back",
    )(tok, ids, h2, mid, gain, gates, wr, *dxs, *dxs)


def input_back_body(nq, _, wq, wkv, *refs):
    dq = refs[:nq]
    dkv = refs[nq : 2 * nq]
    dh = refs[2 * nq]
    acc = None
    for w, parts in ((wq, dq), (wkv, dkv)):
        at = 0
        for part in parts:
            n = part.shape[1]
            term = dot_nt(part[...], w[:, at : at + n])
            acc = term if acc is None else acc + term
            at += n
    dh[...] = acc.astype(BF)


def input_back(tok, wq, wkv, dqs, dkvs):
    rows = dqs[0].shape[0]
    width = wq.shape[0]
    rt = 256
    nq = len(dqs)
    block = lambda n: pl.BlockSpec((rt, n), lambda i: (i, 0))
    return pl.pallas_call(
        functools.partial(input_back_body, nq),
        grid=(rows // rt,),
        in_specs=[pl.BlockSpec(memory_space=pltpu.SMEM), whole_block(wq), whole_block(wkv)] + [block(v.shape[1]) for v in (*dqs, *dkvs)],
        out_specs=block(width),
        out_shape=jax.ShapeDtypeStruct((rows, width), BF),
        compiler_params=pltpu.CompilerParams(vmem_limit_bytes=VMEM_BYTES),
        cost_estimate=cost(4 * rows * width * wq.shape[1], 10 * rows * width),
        name="input_back",
    )(tok, wq, wkv, *dqs, *dkvs)


def token_grads_body(_, x, cot, own, other, gm, gain, out):
    xb = x[...].astype(F32)
    r = lax.rsqrt(jnp.mean(xb * xb, axis=1, keepdims=True) + NORM_EPS)
    xhat = xb * r
    su = (own[...].astype(F32) + other[...].astype(F32)) * gain[...].astype(F32)
    norm = r * (su - xhat * jnp.mean(su * xhat, axis=1, keepdims=True))
    out[...] = cot[...].astype(F32) + gm[...].astype(F32) + norm


def token_grads(tok, x, cot, own, other, gm, gain):
    rows, width = x.shape
    rt = 256
    block = pl.BlockSpec((rt, width), lambda i: (i, 0))
    return pl.pallas_call(
        token_grads_body,
        grid=(rows // rt,),
        in_specs=[pl.BlockSpec(memory_space=pltpu.SMEM)] + [block] * 5 + [whole_block(gain)],
        out_specs=block,
        out_shape=jax.ShapeDtypeStruct((rows, width), F32),
        compiler_params=pltpu.CompilerParams(vmem_limit_bytes=VMEM_BYTES),
        cost_estimate=cost(12 * rows * width, 14 * rows * width),
        name="token_grads",
    )(tok, x, cot, own, other, gm, gain)


def layer_out_body(nb, _, *refs):
    mid, live = refs[:2]
    moes = refs[2 : 2 + nb]
    out, stats = refs[2 + nb :]
    moe = sum(m[...].astype(F32) for m in moes) * RESID_SCALE
    outf = mid[...] + moe
    out[...] = outf.astype(BF)
    v = live[...]
    s0 = jnp.sum(v * jnp.sum(outf * outf, axis=1, keepdims=True))
    s2 = jnp.sum(v * jnp.sum(moe * moe, axis=1, keepdims=True))
    lane = lax.broadcasted_iota(jnp.int32, stats.shape, 1)

    @pl.when(pl.program_id(0) == 0)
    def _():
        stats[...] = jnp.zeros_like(stats)

    stats[...] += jnp.where(lane == 0, s0, jnp.where(lane == 2, s2, 0.0))


def layer_out_share(tok, mid, live, moes):
    rows, width = mid.shape
    shape = jax.ShapeDtypeStruct
    rt = 128
    block = lambda n: pl.BlockSpec((rt, n), lambda i: (i, 0))
    return pl.pallas_call(
        functools.partial(layer_out_body, len(moes)),
        grid=(rows // rt,),
        in_specs=[pl.BlockSpec(memory_space=pltpu.SMEM), block(width), block(1)] + [block(width)] * len(moes),
        out_specs=[block(width), pl.BlockSpec((8, 128), lambda i: (0, 0))],
        out_shape=[shape((rows, width), BF), shape((8, 128), F32)],
        compiler_params=pltpu.CompilerParams(vmem_limit_bytes=VMEM_BYTES),
        cost_estimate=cost(12 * rows * width, 14 * rows * width),
        name="layer_out",
    )(tok, mid, live, *moes)


def gather_rows_body(widths, count, turned, me, *refs):
    parts, outs = refs[:count], refs[-len(widths) :]
    size = parts[0].shape[0]
    for k, part in enumerate(parts):
        rows = pl.ds(pl.multiple_of((me[0] ^ k) * size, size), size)
        begin = 0
        for j, (out, w) in enumerate(zip(outs, widths, strict=True)):
            piece = part[:, begin : begin + w].astype(F32)
            if turned and j == len(widths) - 1:
                out[:, rows] = piece.T
            else:
                out[rows, :] = piece
            begin += w


def gather_rows(me, parts, widths, groups, turned, earlier=()):
    npart = len(parts)
    rows = npart * parts[0].shape[0]
    group = 1 if earlier else 0
    last = len(widths) - 1
    block = lambda j, w: (w, rows) if turned and j == last else (rows, w)
    shape = lambda j, w: (rows, w * groups) if j < 2 else block(j, w)
    return pl.pallas_call(
        functools.partial(gather_rows_body, widths, npart, turned),
        grid=(1,),
        in_specs=[pl.BlockSpec(memory_space=pltpu.SMEM)]
        + [whole_block(v) for v in parts]
        + [pl.BlockSpec(memory_space=pl.ANY)] * len(earlier),
        out_specs=[
            pl.BlockSpec(block(j, w), (lambda _: (0, group)) if j < 2 else (lambda _: (0, 0)))
            for j, w in enumerate(widths)
        ],
        out_shape=[jax.ShapeDtypeStruct(shape(j, w), F32) for j, w in enumerate(widths)],
        input_output_aliases={1 + npart + j: j for j in range(len(earlier))},
        compiler_params=pltpu.CompilerParams(vmem_limit_bytes=VMEM_BYTES),
        cost_estimate=cost(0, 6 * rows * sum(widths)),
        name="gather_rows",
    )(me, *parts, *earlier)


HD = 64
NEG = -1e30
BLK = 256


def swap_halves(v, lane):
    return jnp.where(lane % HD < HD // 2, pltpu.roll(v, 128 - HD // 2, 1), pltpu.roll(v, HD // 2, 1))


def mask_bias(start, valid, i, keys):
    row = lax.broadcasted_iota(jnp.int32, (BLK, keys), 0) + i * BLK
    key = lax.broadcasted_iota(jnp.int32, (BLK, keys), 1)
    first = jnp.maximum(start, row[:, :1] - (WINDOW - 1))
    ok = (key >= first) & (key <= row) & ((valid[:, :keys] > 0) | (key == row))
    return jnp.where(ok, 0.0, NEG).astype(F32)


def doc_starts(lengths, place):
    start = jnp.zeros_like(place)
    end = 0
    for j in range(lengths.shape[1]):
        end = end + lengths[0, j]
        start = jnp.where(place >= end, end, start)
    return start


def prepare_body(core, gu, down, cot, routes, pack, pay):
    width, f = gu.shape[2:]
    share = cot.shape[0]
    pack[:2] = gu[0]
    for k in range(width // f):
        pack[2, k * f : (k + 1) * f, :] = down[0, :, k * f : (k + 1) * f]
    pay[:share, :] = cot[...]
    pay[share:, :] = jnp.zeros((pay.shape[0] - share, width), BF)
    pay[share : share + routes.shape[0], :share] = routes[...].astype(F32).astype(BF)


def prepare(core, gu, down, cot, routes):
    width, f = gu.shape[2:]
    share = routes.shape[1]
    shape = jax.ShapeDtypeStruct
    return pl.pallas_call(
        prepare_body,
        grid_spec=pltpu.PrefetchScalarGridSpec(
            num_scalar_prefetch=1,
            grid=(1,),
            in_specs=[
                whole_block(gu),
                whole_block(down),
                pl.BlockSpec((share, width), lambda _, c: (c[0], 0)),
                whole_block(routes),
            ],
            out_specs=[
                pl.BlockSpec((3, width, f), lambda *_: (0, 0, 0)),
                pl.BlockSpec((share + 16, width), lambda *_: (0, 0)),
            ],
        ),
        out_shape=[shape((3, width, f), BF), shape((share + 16, width), BF)],
        compiler_params=pltpu.CompilerParams(vmem_limit_bytes=VMEM_BYTES),
        cost_estimate=cost(0, 12 * width * f),
        name="prepare",
    )(core, gu, down, cot, routes)


def attn_forward_body(nout, core, lengths, x_hbm, gain, wq_hbm, wkv_hbm, wo_hbm, valid, *refs):
    outs, bufs = refs[:nout], refs[nout : 2 * nout]
    x, wq, wkv, wo, isem, osem = refs[2 * nout :]
    h1, q, kd, vd, o, lse, cos, sin, own, *rest = bufs
    nb = x.shape[0] // BLK
    ins = [pltpu.make_async_copy(x_hbm.at[pl.ds(i * BLK, BLK), :], x.at[pl.ds(i * BLK, BLK), :], isem.at[i]) for i in range(nb)]
    weights = [
        pltpu.make_async_copy(source, to, isem.at[nb + n])
        for n, (source, to) in enumerate(((wq_hbm, wq), (wkv_hbm, wkv), (wo_hbm, wo)))
    ]
    for copy in (ins[0], *weights, *ins[1:]):
        copy.start()
    leaving = []
    nkv = wkv.shape[1] // 128
    lane = lax.broadcasted_iota(jnp.int32, (BLK, 128), 1)
    low = lane < HD
    ga = gain[...].astype(F32)
    frequencies = jnp.exp((lane[:1] % (HD // 2)).astype(F32) * (-2.0 * math.log(ROPE_BASE) / HD))
    half = own.shape[0]
    for i in range(x.shape[0] // BLK):
        rs = pl.ds(i * BLK, BLK)
        keys = (i + 1) * BLK
        place = lax.broadcasted_iota(jnp.int32, (BLK, 1), 0) + i * BLK
        start = doc_starts(lengths, place)
        angles = (place - start).astype(F32) * frequencies
        cb = jnp.cos(angles)
        sb = jnp.sin(angles)
        sb = jnp.where(lane % HD < HD // 2, -sb, sb)
        cos[rs, :] = cb
        sin[rs, :] = sb
        ins[i].wait()
        xb = x[rs, :].astype(F32)
        r = lax.rsqrt(jnp.mean(xb * xb, axis=1, keepdims=True) + NORM_EPS)
        hb = (xb * r * ga).astype(BF)
        h1[rs, :] = hb
        if i == 0:
            weights[0].wait()
            weights[1].wait()
        qp = dot(hb, wq[...])
        kvp = dot(hb, wkv[...])
        for n in range(nkv):
            ns = slice(n * 128, (n + 1) * 128)
            qn = qp[:, ns]
            q[rs, ns] = ((qn * cb + swap_halves(qn, lane) * sb) * ATTN_SCALE).astype(BF)
            kv = kvp[:, ns]
            rot = kv * cb + swap_halves(kv, lane) * sb
            kd[rs, ns] = jnp.where(low, rot, pltpu.roll(rot, HD, 1)).astype(BF)
            vd[rs, ns] = jnp.where(low, pltpu.roll(kv, HD, 1), kv).astype(BF)
        for j in (0, 1, 2, 3, 6, 7):
            leaving.append(pltpu.make_async_copy(bufs[j].at[rs, :], outs[j].at[rs, :], osem.at[i, j]))
            leaving[-1].start()
        bias = mask_bias(start, valid, i, keys)
        bias2 = jnp.concatenate([bias, bias], axis=0)
        lse_all = jnp.zeros((BLK, 128), F32)
        for n in range(nkv):
            ns = slice(n * 128, (n + 1) * 128)
            qn = q[rs, ns]
            zero = jnp.zeros_like(qn)
            q2 = jnp.concatenate([jnp.where(low, qn, zero), jnp.where(low, zero, qn)], axis=0)
            s = dot_nt(q2, kd[:keys, ns]) + bias2
            m = jnp.max(s, axis=1, keepdims=True)
            p = jnp.exp(s - m)
            total = jnp.sum(p, axis=1, keepdims=True)
            o2 = dot(p.astype(BF), vd[:keys, ns]) * (1.0 / total)
            o[rs, ns] = jnp.where(low, o2[:BLK], o2[BLK:]).astype(BF)
            l2 = m + jnp.log(total)
            lse_all = jnp.where(lane == 2 * n, l2[:BLK], jnp.where(lane == 2 * n + 1, l2[BLK:], lse_all))
        lse[rs, :] = lse_all
        for j in (4, 5):
            leaving.append(pltpu.make_async_copy(bufs[j].at[rs, :], outs[j].at[rs, :], osem.at[i, j]))
            leaving[-1].start()
        if i == 0:
            weights[2].wait()
        term = dot(o[rs, :], wo[...]).astype(BF)
        at = pl.ds(i * BLK % half, BLK)
        if not rest:
            own[rs, :] = term
            leaving.append(pltpu.make_async_copy(own.at[rs, :], outs[8].at[rs, :], osem.at[i, 8]))
            leaving[-1].start()
        else:
            mine = pltpu.make_async_copy(own.at[at, :], outs[8].at[at, :], osem.at[i, 8])
            other = pltpu.make_async_copy(rest[0].at[at, :], outs[9].at[at, :], osem.at[i, 8])

            @pl.when(core[0] == i * BLK // half)
            def _():
                own[at, :] = term
                mine.start()

            @pl.when(core[0] != i * BLK // half)
            def _():
                rest[0][at, :] = term
                other.start()

            leaving.append(mine)
    for copy in leaving:
        copy.wait()


def attn_forward(core, lengths, x, gain, wq, wkv, wo, valid, split):
    rows, width = x.shape
    wid = wq.shape[1]
    kvw = wkv.shape[1]
    shape = jax.ShapeDtypeStruct
    part = [((rows // 2, width), BF)] * 2 if split else [((rows, width), BF)]
    outs = [
        ((rows, width), BF),
        ((rows, wid), BF),
        ((rows, kvw), BF),
        ((rows, kvw), BF),
        ((rows, wid), BF),
        ((rows, 128), F32),
        ((rows, 128), F32),
        ((rows, 128), F32),
        *part,
    ]
    nb = rows // BLK
    smem, vmem, there = (pl.BlockSpec(memory_space=m) for m in (pltpu.SMEM, pltpu.VMEM, pl.ANY))
    return pl.pallas_call(
        functools.partial(attn_forward_body, len(outs)),
        in_specs=[smem, smem, there, vmem, there, there, there, vmem],
        out_specs=[there] * len(outs),
        out_shape=[shape(*s) for s in outs],
        scratch_shapes=[pltpu.VMEM(*s) for s in outs]
        + [
            pltpu.VMEM((rows, width), BF),
            pltpu.VMEM((width, wid), BF),
            pltpu.VMEM((width, kvw), BF),
            pltpu.VMEM((wid, width), BF),
            pltpu.SemaphoreType.DMA((nb + 3,)),
            pltpu.SemaphoreType.DMA((nb, 9)),
        ],
        compiler_params=pltpu.CompilerParams(vmem_limit_bytes=VMEM_BYTES),
        cost_estimate=cost(2 * rows * width * 3 * wid + 4 * rows * rows * 4 * wid, 12 * rows * width),
        name="attention_forward",
    )(core, lengths, x, gain, wq, wkv, wo, valid)


def attn_backward_body(first, npart, nmore, npiece, places, core, at, lengths, q, kd, vd, lse, cos, sin, valid, gain, *refs):
    it = iter(refs)
    take = lambda n: [next(it) for _ in range(n)]
    h1_hbm, wq_hbm, wkv_hbm = take(3)
    more = take(nmore)
    if places:
        cot, wo, o_hbm, *parts = take(3 + npart)
    else:
        (do,) = take(1)
    dq, dkv, sums = take(3)
    pieces = take(npiece)
    if places:
        do, gm = take(2)
    dk, dv, gw, h1, wq, wkv, sem = take(7)
    if places:
        da, o = take(2)
    wid = q.shape[1]
    width = h1.shape[1]
    cols = pl.ds(first * 128, wid)
    copies = [
        pltpu.make_async_copy(h1_hbm, h1, sem.at[0]),
        pltpu.make_async_copy(wq_hbm.at[:, cols], wq, sem.at[1]),
        pltpu.make_async_copy(wkv_hbm.at[:, cols], wkv, sem.at[2]),
    ]
    if places:
        copies.append(pltpu.make_async_copy(o_hbm, o, sem.at[3]))
    for copy in copies:
        copy.start()
    if places:
        for i in range(q.shape[0] // BLK):
            rs = pl.ds(i * BLK, BLK)
            g = placed(core, parts, i)
            gm[rs, :] = g.astype(BF)
            d = (RESID_SCALE * (cot[rs, :].astype(F32) + g)).astype(BF)
            da[rs, :] = d
            do[rs, :] = dot_nt(d, wo[...]).astype(BF)
    nkv = kd.shape[1] // 128
    wid = q.shape[1]
    lane = lax.broadcasted_iota(jnp.int32, (BLK, 128), 1)
    low = lane < HD
    dk[...] = jnp.zeros_like(dk)
    dv[...] = jnp.zeros_like(dv)
    nb = q.shape[0] // BLK
    for i in range(nb):
        rs = pl.ds(i * BLK, BLK)
        keys = (i + 1) * BLK
        cb, sb = cos[rs, :], sin[rs, :]
        place = lax.broadcasted_iota(jnp.int32, (BLK, 1), 0) + i * BLK
        bias = mask_bias(doc_starts(lengths, place), valid, i, keys)
        bias2 = jnp.concatenate([bias, bias], axis=0)
        lse_i = lse[rs, :]
        for n in range(nkv):
            ns = slice(n * 128, (n + 1) * 128)
            qn, dn = q[rs, ns], do[rs, ns]
            zero = jnp.zeros_like(qn)
            q2 = jnp.concatenate([jnp.where(low, qn, zero), jnp.where(low, zero, qn)], axis=0)
            d2 = jnp.concatenate([jnp.where(low, dn, zero), jnp.where(low, zero, dn)], axis=0)
            h = 2 * (first + n)
            l2 = jnp.concatenate([lse_i[:, h : h + 1], lse_i[:, h + 1 : h + 2]], axis=0)
            p = jnp.exp(dot_nt(q2, kd[:keys, ns]) + bias2 - l2)
            dp = dot_nt(d2, vd[:keys, ns])
            shift = jnp.sum(p * dp, axis=1, keepdims=True)
            ds = (p * (dp - shift)).astype(BF)
            dv[:keys, ns] += dot_tn(p.astype(BF), d2)
            dk[:keys, ns] += dot_tn(ds, q2)
            dq2 = dot(ds, kd[:keys, ns])
            dqn = jnp.where(low, dq2[:BLK], dq2[BLK:]) * ATTN_SCALE
            dq[rs, ns] = (dqn * cb - swap_halves(dqn, lane) * sb).astype(BF)
    for i in range(nb):
        rs = pl.ds(i * BLK, BLK)
        cb, sb = cos[rs, :], sin[rs, :]
        for n in range(nkv):
            ns = slice(n * 128, (n + 1) * 128)
            kk = dk[rs, ns]
            kk = kk + pltpu.roll(kk, HD, 1)
            vv = dv[rs, ns]
            vv = vv + pltpu.roll(vv, HD, 1)
            dkv[rs, ns] = jnp.where(low, kk * cb - swap_halves(kk, lane) * sb, vv).astype(BF)
    for copy in copies:
        copy.wait()
    gq = dot_tn(h1[...], dq[...])
    gk = dot_tn(h1[...], dkv[...])
    gw[:, :wid] = gq.astype(BF)
    gw[:, wid : 2 * wid] = gk.astype(BF)
    ga = jnp.sum(gq * wq[...].astype(F32) + gk * wkv[...].astype(F32), axis=1, keepdims=True) / gain[...].astype(F32)
    lanes = lax.broadcasted_iota(jnp.int32, (width, 128), 1)
    ga = jnp.where(lanes == GAIN_A, ga, 0.0)
    for v in more:
        ga = ga + v[...]
    sums[...] = ga
    if places:
        gwo = dot_tn(o[...], da[...]).astype(BF)
        depth = gwo.shape[0]
        for n in range(width // depth):
            rs = slice(n * depth, (n + 1) * depth)
            gw[rs, 2 * wid : 2 * wid + depth] = gwo[:, rs]
    else:
        gw[:, 2 * wid :] = ga.astype(BF)
    size = width // len(pieces)
    for k, piece in enumerate(pieces):
        piece[...] = gw[pl.ds(pl.multiple_of((at[0] ^ k) * size, size), size), :]


def placed(core, parts, i):
    if len(parts) == 1:
        return parts[0][i * BLK : (i + 1) * BLK, :].astype(F32)
    n = len(parts) // 2
    mine, other = parts[i % n][...].astype(F32), parts[n + i % n][...].astype(F32)
    return jnp.where(core[0] == i // n, mine, other)


def attn_backward(first, count, core, at, npiece, lengths, q, kd, vd, lse, h1, cos, sin, valid, wq, wkv, gain, sums, do=None, given=None):
    rows, width = h1.shape
    w = count * 128
    depth = given[1].shape[0] if given else 128
    cols = 2 * w + depth
    shape = jax.ShapeDtypeStruct
    part = pl.BlockSpec((rows, w), lambda _: (0, first // count))
    full = lambda *s: pl.BlockSpec(s, lambda _: (0, 0))
    there = pl.BlockSpec(memory_space=pl.ANY)
    size = width // npiece
    outs = [(rows, w)] * 2 + [(width, 128)] + [(size, cols)] * npiece
    types = [BF, BF, F32] + [BF] * npiece
    scratch = [
        pltpu.VMEM((rows, w), F32),
        pltpu.VMEM((rows, w), F32),
        pltpu.VMEM((width, cols), BF),
        pltpu.VMEM((rows, width), BF),
        pltpu.VMEM((width, w), BF),
        pltpu.VMEM((width, w), BF),
        pltpu.SemaphoreType.DMA((4,)),
    ]
    if given:
        cot, wo, o, *parts = given
        last = [cot, wo, o, *parts]
        last_specs = [whole_block(cot), whole_block(wo), there] + [whole_block(v) for v in parts]
        outs += [(rows, depth), (rows, width)]
        types += [BF, BF]
        scratch += [pltpu.VMEM((rows, width), BF), pltpu.VMEM((rows, depth), BF)]
    else:
        parts, last, last_specs = (), [do], [part]
    return pl.pallas_call(
        functools.partial(attn_backward_body, first, len(parts), len(sums), npiece, bool(given)),
        grid=(1,),
        in_specs=[pl.BlockSpec(memory_space=pltpu.SMEM)] * 3
        + [part] * 3
        + [whole_block(v) for v in (lse, cos, sin, valid, gain)]
        + [there] * 3
        + [whole_block(v) for v in sums]
        + last_specs,
        out_specs=[full(*s) for s in outs],
        out_shape=[shape(s, d) for s, d in zip(outs, types, strict=True)],
        scratch_shapes=scratch,
        compiler_params=pltpu.CompilerParams(vmem_limit_bytes=VMEM_BYTES),
        cost_estimate=cost(4 * rows * width * w + 20 * rows * rows * w, 10 * rows * width),
        name="attention_backward",
    )(core, at, lengths, q, kd, vd, lse, cos, sin, valid, gain, h1, wq, wkv, *sums, *last)


def on_device(
    tokens,
    gain_attn,
    query_weight_matrix,
    key_value_weight,
    w_out,
    gain_ffn,
    w_router,
    w_gate_up,
    w_down,
    routes,
    doc_lengths,
    valid_mask,
    cotangent,
):
    rows, width = tokens.shape
    share = routes.shape[0]
    n_ep, n_tp = lax.axis_size("ep"), lax.axis_size("tp")
    nexp = w_router.shape[1]
    inner = math.gcd(n_ep, 4)
    outer = n_ep // inner
    me = lax.axis_index("ep")
    me_in = me % inner
    core = lax.axis_index("tp")[None]
    pair = n_tp == 2

    def across(v, k):
        return lax.ppermute(v, "ep", [(i, i ^ k) for i in range(n_ep)])

    def along(v, k):
        return lax.ppermute(v, "ep", [(i, (i + k * inner) % n_ep) for i in range(n_ep)])

    def swap(v):
        return lax.ppermute(v, "tp", [(0, 1), (1, 0)])

    def after(v, *earlier):
        return lax.optimization_barrier((v, *earlier))[0]

    def total(terms):
        acc = terms[0].astype(F32)
        for term in terms[1:]:
            acc = acc + term.astype(F32)
        return acc

    def scatter_plane(pieces):
        return [pieces[0]] + [across(pieces[k], k) for k in range(1, inner)]

    def cut_rows(v, k):
        size = v.shape[0] // inner
        return lax.dynamic_slice_in_dim(v, (me_in ^ k) * size, size)

    def summed(terms):
        return total(terms).astype(BF)

    def column_steps(v):
        bit = 1
        while bit < outer:
            other = lax.ppermute(v, "ep", [(i, i ^ (bit * inner)) for i in range(n_ep)])
            yield other
            v = summed([v, release(other)])
            bit *= 2
        yield v

    def unpacked(v):
        f = v.shape[2]
        return v[:2], v[2].reshape(width // f, f, f).transpose(1, 0, 2).reshape(f, width)

    def packed(gu, down):
        f = gu.shape[2]
        return jnp.concatenate([gu, down.reshape(f, width // f, f).transpose(1, 0, 2).reshape(1, width, f)])

    def full_hidden(v):
        if pair:
            return [v, swap(v)]
        gu, down = unpacked(v)
        return [
            packed(
                lax.all_gather(gu, "tp", axis=2, tiled=True),
                lax.all_gather(down, "tp", axis=0, tiled=True),
            )
        ]

    def own_hidden(v):
        if pair:
            return v[0].astype(F32) + swap(v[1]).astype(F32)
        gu, down = unpacked(v[0].astype(F32))
        return packed(
            lax.psum_scatter(gu, "tp", scatter_dimension=2, tiled=True),
            lax.psum_scatter(down, "tp", scatter_dimension=0, tiled=True),
        )

    halves = 2 if pair else 1
    local = jnp.arange(outer, dtype=jnp.int32) * inner
    ids = (me - local) % n_ep
    ids_all = jnp.concatenate([((me ^ k) - local) % n_ep for k in range(inner)])
    valid_row = valid_mask[None, :]
    live_all = valid_mask.astype(F32)[:, None]
    live = lax.dynamic_slice_in_dim(live_all, core[0] * share, share)
    gain_a, gain_f = gain_attn[None, :], gain_ffn[None, :]
    wr = jnp.pad(w_router, ((0, 0), (0, 128 - nexp)))

    tok = core

    def finish(*values):
        nonlocal tok
        tok = after(tok, *values)

    def release(v):
        return after(v, tok)

    pack, pay = prepare(tok, w_gate_up, w_down, cotangent, routes.T)
    held = [pack]
    if outer > 1:
        held.append(along(pack, 1))
    pays = [pay] + [across(pay, k) for k in range(1, min(inner, 3))]
    chunks = [full_hidden(pack)]
    finish(pack)

    h1, q, kd, vd, o, lse, cos, sin, *part = attn_forward(
        tok, doc_lengths, tokens, gain_a, query_weight_matrix, key_value_weight, w_out, valid_row, pair
    )
    if pair:
        own, other = part[0], swap(part[1])
    else:
        own = lax.psum_scatter(part[0].astype(F32), "tp", scatter_dimension=0, tiled=True)
        other = jnp.zeros_like(own)
    finish(own, other, *pays, *chunks[0])
    mid, h2, stats = middle_norm(tok, tokens, own, other, gain_f, live_all)
    h2s = [h2] + [across(h2, k) for k in range(1, min(inner, 3))]
    finish(h2, *held[1:])

    near = min(2, outer)
    last = outer - 1
    far = list(range(3, inner))
    close = list(range(min(inner, 3)))
    state = [None] * inner
    saved = [dict() for _ in range(inner)]

    gates = [None] * inner

    def work(blocks, first, count):
        rows_in = [h2s[b] for b in blocks], [pays[b] for b in blocks]
        packs = [c for r in range(first, first + count) for c in chunks[r]]
        if state[blocks[0]] is None:
            out = experts(release(ids), *rows_in, wr, packs, halves)
        else:
            held_gates, before = [gates[b] for b in blocks], [state[b] for b in blocks]
            out = one_expert(release(ids), *rows_in, held_gates, before, packs, first)
        for b, (dx, moe, gat, dgu, *gate) in zip(blocks, out, strict=True):
            state[b] = (dx, moe)
            gates[b] = gate[0] if gate else gates[b]
            for r in range(count):
                saved[b][first + r] = (gat, dgu, r)
        finish(out[0][1])

    def expert_grads(experts_of):
        out = weight_grads(tok, h2s, pays, [[s[r] for r in experts_of] for s in saved], halves)
        finish(out[0])
        return out

    def next_held():
        v = release(held[-1])
        if len(held) < outer:
            held.append(along(v, 1))
        chunks.append(full_hidden(v))

    if outer > 1:
        next_held()
    work([0], 0, near)
    finish(*h2s)
    for k in far:
        pays.append(across(release(pay), k))
    if close[1:]:
        work(close[1:], 0, near)
    if outer > 2:
        finish(held[-1])
        next_held()
    finish(*pays)
    for k in far:
        h2s.append(across(release(h2), k))
    for r in range(near, last):
        work(close, r, 1)
        if r + 1 < last:
            finish(held[-1])
            next_held()
    finish(*h2s)
    for b in far:
        work([b], 0, max(last, near))
    if last >= near:
        finish(held[-1])
        next_held()

    first = 1 % outer
    later = [[r] for r in range(2, min(outer, 3))] + [[*range(3, outer), 0]]
    later = later if outer > 1 else []
    raw = expert_grads([first])
    parts = {first: own_hidden([v[0] for v in raw])}
    if last >= near and inner > 1:
        work(list(range(1, inner)), last, 1)
    ring = parts[first].astype(BF)
    finish(ring)
    if outer > 1:
        ring = along(ring, 1)
    dxs = [None] + [across(state[k][0], k) for k in range(1, inner)]
    if last >= near:
        work([0], last, 1)
    dxs[0] = state[0][0]
    raws = [expert_grads(rs) for rs in later]
    def ring_step(r):
        nonlocal ring
        term = release(ring).astype(F32) + parts[r]
        if r == 0:
            return term
        ring = term.astype(BF)
        finish(ring)
        ring = along(ring, 1)

    def take_part(rs, raw):
        if not pair:
            parts.update({r: own_hidden([raw[0][n]]) for n, r in enumerate(rs)})
            return
        other = swap(release(raw[1]))
        parts.update({r: raw[0][n].astype(F32) + other[n].astype(F32) for n, r in enumerate(rs)})
        if rs == [2]:
            finish(other)

    finish(*dxs, *([ring] if outer > 1 else []))
    if outer > 2:
        take_part(later[0], raws[0])
        ring_step(2)
    for rs, raw in zip(later, raws, strict=True):
        if rs != [2]:
            take_part(rs, raw)
    moes = [state[0][1]] + [across(release(state[k][1]), k) for k in range(1, inner)]
    gm, small = middle_back(tok, ids_all, h2, mid, gain_f, gates[0], wr, dxs, outer)
    if pair:
        gm = lax.all_to_all(gm, "tp", 0, 0).reshape(rows, width)
    else:
        gm = lax.all_gather(gm[0], "tp", axis=0, tiled=True)
    finish(gm)

    nkv = kd.shape[1] // 128
    groups = 2 if nkv % 2 == 0 else 1
    each = nkv // groups
    w = each * 128
    depth = w_out.shape[0]
    dqs, dkvs, sums = [], [], small
    at = me_in[None]
    for n in range(groups):
        first_one = n == 0
        out = attn_backward(
            n * each,
            each,
            tok,
            at,
            inner,
            doc_lengths,
            q,
            kd,
            vd,
            lse,
            h1,
            cos,
            sin,
            valid_row,
            query_weight_matrix,
            key_value_weight,
            gain_attn[:, None],
            [sums],
            None if first_one else do,
            (cotangent, w_out, o, gm) if first_one else None,
        )
        dq, dkv, sums, *pieces = out[: 3 + inner]
        if first_one:
            do, gm_all = out[3 + inner :]
        finish(pieces[0])
        dqs.append(dq)
        dkvs.append(dkv)
        if first_one and groups > 1:
            terms = scatter_plane(pieces)
            if outer > 3:
                finish(ring)
                ring_step(3)
    if groups == 1:
        sums_only = [cut_rows(sums.astype(BF), k) for k in range(inner)]
        terms = scatter_plane([jnp.concatenate(v, axis=1) for v in zip(pieces, sums_only, strict=True)])
    finish(*moes)
    out_share, stats_out = layer_out_share(tok, mid, live, moes)
    finish(out_share)
    spread = jnp.pad((stats + stats_out)[:1, :4], ((0, 0), (STATS, 128 - STATS - 4)))

    def closing_sum(terms):
        v = total([release(t) for t in terms])
        row = lax.broadcasted_iota(jnp.int32, v.shape, 0)
        lane = lax.broadcasted_iota(jnp.int32, v.shape, 1) - (v.shape[1] - 128)
        place = (row == 0) & (lane >= STATS) & (lane < STATS + 4)
        return jnp.where(place, jnp.pad(spread, ((0, 0), (v.shape[1] - 128, 0))), v).astype(BF)

    def spread_plane(v):
        return [v] + [across(v, k) for k in range(1, inner)]

    if groups > 1:
        finish(*terms)
        ahead = column_steps(summed([release(t) for t in terms]))
        moving = next(ahead)
        terms = scatter_plane([release(v) for v in pieces])
    dh1 = input_back(tok, query_weight_matrix, key_value_weight, dqs, dkvs)
    finish(dh1, *([ring] if outer > 1 else []), *([moving] if groups > 1 else []), *terms)
    if groups > 1:
        moving = next(ahead)
    closing = closing_sum(terms)
    if pair:
        dh_other = swap(release(dh1))
        out_other = swap(out_share)
    else:
        dh1, dh_other = lax.psum(dh1.astype(F32), "tp"), jnp.zeros_like(dh1)
    finish(dh_other, closing)
    grad_tokens = token_grads(tok, tokens, cotangent, dh1, dh_other, gm, gain_a)
    finish(grad_tokens)
    if pair:
        layer_out = jnp.where(
            core[0] == 0,
            jnp.concatenate([release(out_share), out_other]),
            jnp.concatenate([out_other, release(out_share)]),
        )
        finish(layer_out)
    else:
        layer_out = lax.all_gather(out_share, "tp", axis=0, tiled=True)
    spreads = []
    if groups > 1:
        finish(moving)
    behind = column_steps(release(closing))
    late = next(behind)
    if groups > 1:
        for whole in ahead:
            pass
        finish(whole)
        spreads.append(spread_plane(whole))
    for r in range(4, outer):
        ring_step(r)
    expert_sums = ring_step(0) if outer > 1 else parts[0]
    gu_grad, down_grad = unpacked(expert_sums)
    finish(late)
    for whole in behind:
        pass
    spreads.append(spread_plane(release(whole)))
    if groups > 1:
        *grads, folded = gather_rows(at, spreads[0], (w, w, depth), groups, False)
        finish(folded)
        grad_w_query, grad_w_kv, extras = gather_rows(release(at), spreads[1], (w, w, 128), groups, True, grads)
    else:
        grad_w_query, grad_w_kv, folded, extras = gather_rows(release(at), spreads[0], (w, w, depth, 128), 1, True)
    grad_w_out = jnp.concatenate([folded[n * depth : (n + 1) * depth] for n in range(width // depth)], axis=1)
    extras = extras[: STATS + 6]
    extras = extras + swap(extras) if pair else lax.psum(extras, "tp")
    s = jnp.sum(extras[STATS : STATS + 4, :: width // inner], axis=1)
    return (
        layer_out,
        grad_tokens,
        extras[GAIN_A],
        grad_w_query,
        grad_w_kv,
        grad_w_out,
        extras[GAIN_F],
        extras[:nexp].T,
        gu_grad[None],
        down_grad[None],
        jnp.sqrt(s[:3] / (s[3] * width)),
    )


def solution(mesh):
    return jax.shard_map(
        on_device,
        mesh=mesh,
        in_specs=(
            P("ep", None),
            P(),
            P(None, "tp"),
            P(None, "tp"),
            P("tp", None),
            P(),
            P(),
            P("ep", None, None, "tp"),
            P("ep", "tp", None),
            P(("ep", "tp"), None),
            P("ep", None),
            P("ep"),
            P("ep", None),
        ),
        out_specs=(
            P("ep", None),
            P("ep", None),
            P(),
            P(None, "tp"),
            P(None, "tp"),
            P("tp", None),
            P(),
            P(),
            P("ep", None, None, "tp"),
            P("ep", "tp", None),
            P(),
        ),
        check_vma=False,
    )
```

```python
import functools
import math

import jax
import jax.numpy as jnp
from jax import lax
from jax.experimental import pallas as pl
from jax.experimental.pallas import tpu as pltpu
from jax.sharding import PartitionSpec as P

SEQUENCE_LENGTH = 1024
WINDOW = 1024
ATTN_SCALE = 0.015625
RESID_SCALE = 0.22
TOPK = 8
NORM_EPS = 1e-06
ROPE_BASE = 10000.0
F32 = jnp.float32
BF = jnp.bfloat16
VMEM_BYTES = 60 * 1024 * 1024
COST = 0.02
GAIN_F, GAIN_A, STATS = 32, 33, 34


def cost(flops, bytes_accessed, transcendentals=0):
    return pl.CostEstimate(
        flops=int(COST * flops), bytes_accessed=int(COST * bytes_accessed), transcendentals=int(COST * transcendentals)
    )


def dot(a, b):
    return jnp.dot(a, b, preferred_element_type=F32)


def dot_nt(a, b):
    return lax.dot_general(a, b, (((1,), (1,)), ((), ())), preferred_element_type=F32)


def dot_tn(a, b):
    return lax.dot_general(a, b, (((0,), (0,)), ((), ())), preferred_element_type=F32)


def whole_block(v):
    return pl.BlockSpec(v.shape, lambda *_: (0,) * len(v.shape))


def gate_rows(h2, routes, wr):
    rows = h2.shape[0]
    lane = lax.broadcasted_iota(jnp.int32, (rows, 128), 1).astype(F32)
    picks = routes.astype(F32).T
    mask = picks[:, 0:1] == lane
    for k in range(1, TOPK):
        mask = mask | (picks[:, k : k + 1] == lane)
    sel = jnp.where(mask, dot(h2, wr[...]), -jnp.inf)
    weight = jnp.exp(sel - jnp.max(sel, axis=1, keepdims=True))
    return weight / jnp.sum(weight, axis=1, keepdims=True)


def gate_table(h2, pay, wr):
    rows = h2.shape[0]
    return gate_rows(h2[...], pay[rows : rows + 16, :rows], wr)


def middle_body(core, x, own, other, gain, live, mid, h2, stats):
    attn = RESID_SCALE * (own[...].astype(F32) + other[...].astype(F32))
    m = x[...].astype(F32) + attn
    mid[...] = m
    r = lax.rsqrt(jnp.mean(m * m, axis=1, keepdims=True) + NORM_EPS)
    h2[...] = (m * r * gain[...].astype(F32)).astype(BF)
    v = live[...]
    total = jnp.sum(v * jnp.sum(attn * attn, axis=1, keepdims=True))
    lane = lax.broadcasted_iota(jnp.int32, stats.shape, 1)
    stats[...] = jnp.where(lane == 1, total, jnp.where(lane == 3, jnp.sum(v), 0.0))


def middle_norm(core, x, own, other, gain, live):
    share, width = own.shape
    shape = jax.ShapeDtypeStruct
    part = lambda n: pl.BlockSpec((share, n), lambda _, c: (c[0], 0))
    full = lambda *s: pl.BlockSpec(s, lambda *_: (0, 0))
    return pl.pallas_call(
        middle_body,
        grid_spec=pltpu.PrefetchScalarGridSpec(
            num_scalar_prefetch=1,
            grid=(1,),
            in_specs=[part(width), whole_block(own), whole_block(other), whole_block(gain), part(1)],
            out_specs=[full(share, width), full(share, width), full(8, 128)],
        ),
        out_shape=[shape((share, width), F32), shape((share, width), BF), shape((8, 128), F32)],
        compiler_params=pltpu.CompilerParams(vmem_limit_bytes=VMEM_BYTES),
        cost_estimate=cost(10 * share * width, 12 * share * width),
        name="middle_norm",
    )(core, x, own, other, gain, live)


def experts_body(nb, nchunk, halves, *refs):
    ids = refs[0]
    at = 1
    h2s, pays = refs[at : at + nb], refs[at + nb : at + 2 * nb]
    at += 2 * nb
    wr = refs[at]
    packs = refs[at + 1 : at + 1 + nchunk]
    at += 1 + nchunk
    outs = [refs[at + 5 * b : at + 5 * b + 5] for b in range(nb)]
    at += 5 * nb
    dgacc, macc, xacc, buf, sem = refs[at:]
    c = pl.program_id(0)
    rows, width = h2s[0].shape
    f = buf.shape[3]
    lane = lax.broadcasted_iota(jnp.int32, (rows, 128), 1)

    @pl.when(c == 0)
    def _():
        pltpu.make_async_copy(packs[0], buf.at[0], sem.at[0]).start()
        for b in range(nb):
            outs[b][4][...] = gate_table(h2s[b], pays[b], wr)
        macc[...] = jnp.zeros_like(macc)
        xacc[...] = jnp.zeros_like(xacc)
        dgacc[...] = jnp.zeros_like(dgacc)

    for k in range(1, nchunk):

        @pl.when(c + 1 == k)
        def _(k=k):
            pltpu.make_async_copy(packs[k], buf.at[k % 2], sem.at[k % 2]).start()

    slot = lax.rem(c, 2)
    pltpu.make_async_copy(packs[0], buf.at[slot], sem.at[slot]).wait()
    r = c // halves
    e = ids[r]
    nd = width // f
    for b in range(nb):
        g, gat, dgu = pays[b], outs[b][2], outs[b][3]
        hb = h2s[b][...]
        gp = dot(hb, buf[slot, 0])
        up = dot(hb, buf[slot, 1])
        u = sum(dot_nt(g[:rows, k * f : (k + 1) * f], buf[slot, 2, k * f : (k + 1) * f, :]) for k in range(nd))
        gate = jnp.sum(jnp.where(lane == e, outs[b][4][...], 0.0), axis=1, keepdims=True)
        sg = jax.nn.sigmoid(gp)
        sl = gp * sg
        act = sl * up
        ga = (gate * act).astype(BF)
        dgacc[b] += jnp.where(lane == r, jnp.sum(act * u, axis=1, keepdims=True) * RESID_SCALE, 0.0)
        da = (RESID_SCALE * gate) * u
        dgp = (da * up * (sg + sl * (1.0 - sg))).astype(BF)
        dup = (da * sl).astype(BF)
        gat[0] = ga.T
        dgu[0, :, :f] = dgp
        dgu[0, :, f:] = dup
        for k in range(nd):
            macc[b, :, k * f : (k + 1) * f] += dot(ga, buf[slot, 2, k * f : (k + 1) * f, :])
        xacc[b] += dot_nt(dgp, buf[slot, 0]) + dot_nt(dup, buf[slot, 1])

    @pl.when(c == nchunk - 1)
    def _():
        for b in range(nb):
            dx, moe = outs[b][:2]
            moe[...] = macc[b].astype(BF)
            dx[:rows, :] = xacc[b].astype(BF)
            dx[rows:, :] = jnp.zeros((16, width), BF)
            dx[rows:, :rows] = gate_tail(dgacc[b])


def gate_tail(dg):
    dg = dg.T[:8]
    high = dg.astype(BF).astype(F32)
    return jnp.concatenate([high, dg - high], axis=0).astype(BF)


def experts(ids, h2s, pays, wr, packs, halves):
    rows, width = h2s[0].shape
    nb, nchunk = len(h2s), len(packs)
    f = packs[0].shape[2]
    ne, hidden = nchunk // halves, halves * f
    shape = jax.ShapeDtypeStruct
    once = lambda v: pl.BlockSpec(v.shape, lambda *_: (0,) * len(v.shape), pipeline_mode=pl.Buffered(1))
    out = pl.pallas_call(
        functools.partial(experts_body, nb, nchunk, halves),
        grid_spec=pltpu.PrefetchScalarGridSpec(
            num_scalar_prefetch=1,
            grid=(nchunk,),
            in_specs=[once(v) for v in (*h2s, *pays, wr)] + [pl.BlockSpec(memory_space=pl.ANY)] * nchunk,
            out_specs=[
                pl.BlockSpec((rows + 16, width), lambda c, _: (0, 0)),
                pl.BlockSpec((rows, width), lambda c, _: (0, 0)),
                pl.BlockSpec((1, f, rows), lambda c, _: (c // halves, c % halves, 0)),
                pl.BlockSpec((1, rows, 2 * f), lambda c, _: (c // halves, 0, c % halves)),
                pl.BlockSpec((rows, 128), lambda c, _: (0, 0)),
            ]
            * nb,
            scratch_shapes=[
                pltpu.VMEM((nb, rows, 128), F32),
                pltpu.VMEM((nb, rows, width), F32),
                pltpu.VMEM((nb, rows, width), F32),
                pltpu.VMEM((2, 3, width, f), BF),
                pltpu.SemaphoreType.DMA((2,)),
            ],
        ),
        out_shape=[
            shape((rows + 16, width), BF),
            shape((rows, width), BF),
            shape((ne, hidden, rows), BF),
            shape((ne, rows, 2 * hidden), BF),
            shape((rows, 128), F32),
        ]
        * nb,
        compiler_params=pltpu.CompilerParams(vmem_limit_bytes=VMEM_BYTES),
        cost_estimate=cost(12 * rows * width * f * nchunk * nb, 6 * nchunk * width * f + 12 * rows * width * nb),
        name="experts",
    )(ids, *h2s, *pays, wr, *packs)
    return [out[5 * b : 5 * b + 5] for b in range(nb)]


def weight_copies(packs, wgu, wd, sem, halves):
    out = []
    for h in range(halves):
        pack = packs[h]
        f = pack.shape[2]
        for j in range(2):
            cols = pl.ds((2 * h + j) * f, f)
            out.append(pltpu.make_async_copy(pack.at[j], wgu.at[:, cols], sem.at[len(out)]))
        for k in range(pack.shape[1] // f):
            rows, cols = pl.ds(h * f, f), pl.ds(k * f, f)
            out.append(pltpu.make_async_copy(pack.at[2, pl.ds(k * f, f), :], wd.at[rows, cols], sem.at[len(out)]))
    return out


def one_expert_body(nb, halves, r, ids, *refs):
    it = iter(refs)
    take = lambda n: [next(it) for _ in range(n)]
    h2s, pays, gates = take(nb), take(nb), take(nb)
    prevs = [take(2) for _ in range(nb)]
    packs = take(halves)
    outs = [take(4) for _ in range(nb)]
    ga_all, wgu, wd, sem = it
    rows, width = h2s[0].shape
    f = wd.shape[0] // halves
    copies = weight_copies(packs, wgu, wd, sem, halves)
    for copy in copies:
        copy.start()
    lane = lax.broadcasted_iota(jnp.int32, (rows, 128), 1)
    for copy in copies:
        copy.wait()
    for b in range(nb):
        dx, moe, gat, dgu = outs[b]
        gu = dot(h2s[b][...], wgu[...])
        u = dot_nt(pays[b][:rows, :], wd[...])
        gate = jnp.sum(jnp.where(lane == ids[r], gates[b][...], 0.0), axis=1, keepdims=True)
        small = RESID_SCALE * gate
        dg = jnp.zeros((rows, 1), F32)
        for h in range(halves):
            gp, up = gu[:, 2 * h * f : (2 * h + 1) * f], gu[:, (2 * h + 1) * f : (2 * h + 2) * f]
            uh = u[:, h * f : (h + 1) * f]
            sg = jax.nn.sigmoid(gp)
            sl = gp * sg
            act = sl * up
            ga = (gate * act).astype(BF)
            dg = dg + jnp.sum(act * uh, axis=1, keepdims=True)
            da = small * uh
            gat[0, h * f : (h + 1) * f, :] = ga.T
            ga_all[:, h * f : (h + 1) * f] = ga
            dgu[0, :, 2 * h * f : (2 * h + 1) * f] = (da * up * (sg + sl * (1.0 - sg))).astype(BF)
            dgu[0, :, (2 * h + 1) * f : (2 * h + 2) * f] = (da * sl).astype(BF)
        before = prevs[b]
        moe[...] = (before[1][...].astype(F32) + dot(ga_all[...], wd[...])).astype(BF)
        dx[:rows, :] = (before[0][:rows, :].astype(F32) + dot_nt(dgu[0], wgu[...])).astype(BF)
        mine = lax.broadcasted_iota(jnp.int32, (16, rows), 0) % 8 == r
        dx[rows:, :] = before[0][rows:, :]
        tail = gate_tail(jnp.where(lane == r, dg * RESID_SCALE, 0.0))
        dx[rows:, :rows] = jnp.where(mine, tail.astype(F32), before[0][rows:, :rows].astype(F32)).astype(BF)


def one_expert(ids, h2s, pays, gates, prevs, packs, r):
    rows, width = h2s[0].shape
    nb, halves = len(h2s), len(packs)
    f = packs[0].shape[2]
    hidden = halves * f
    flat = [v for prev in prevs for v in prev]
    shape = jax.ShapeDtypeStruct
    vmem = pl.BlockSpec(memory_space=pltpu.VMEM)
    out = pl.pallas_call(
        functools.partial(one_expert_body, nb, halves, r),
        in_specs=[pl.BlockSpec(memory_space=pltpu.SMEM)]
        + [vmem] * (5 * nb)
        + [pl.BlockSpec(memory_space=pl.ANY)] * halves,
        out_specs=[vmem] * (4 * nb),
        scratch_shapes=[
            pltpu.VMEM((rows, hidden), BF),
            pltpu.VMEM((width, 2 * hidden), BF),
            pltpu.VMEM((hidden, width), BF),
            pltpu.SemaphoreType.DMA((halves * (2 + width // f),)),
        ],
        out_shape=[
            shape((rows + 16, width), BF),
            shape((rows, width), BF),
            shape((1, hidden, rows), BF),
            shape((1, rows, 2 * hidden), BF),
        ]
        * nb,
        compiler_params=pltpu.CompilerParams(vmem_limit_bytes=VMEM_BYTES),
        cost_estimate=cost(12 * rows * width * hidden * nb, 6 * width * hidden + 12 * rows * width * nb),
        name="one_expert",
    )(ids, *h2s, *pays, *gates, *flat, *packs)
    return [out[4 * b : 4 * b + 4] for b in range(nb)]


def weight_grads_body(nb, halves, _, *refs):
    h2 = refs[:nb]
    g = refs[nb : 2 * nb]
    hidden, outs = refs[2 * nb : -halves], refs[-halves:]
    e, c = pl.program_id(0), pl.program_id(1)
    rows = h2[0].shape[0]
    width, f = outs[0].shape[2:]
    for n in range(len(hidden) // (2 * nb)):

        @pl.when(e == n)
        def _(n=n):
            gat, dgu = hidden[2 * nb * n : 2 * nb * n + nb], hidden[2 * nb * n + nb : 2 * nb * (n + 1)]
            acc = sum(dot_tn(h2[b][...], dgu[b][0]) for b in range(nb))
            down = sum(dot(gat[b][0], g[b][:rows, :]) for b in range(nb)) * RESID_SCALE
            for half in range(halves):

                @pl.when(c == half)
                def _(out=outs[half]):
                    out[0, 0] = acc[:, :f].astype(BF)
                    out[0, 1] = acc[:, f:].astype(BF)
                    for k in range(width // f):
                        out[0, 2, k * f : (k + 1) * f, :] = down[:, k * f : (k + 1) * f].astype(BF)


def weight_grads(tok, h2s, pays, saved, halves):
    nb, ne = len(h2s), len(saved[0])
    rows, width = h2s[0].shape
    f = saved[0][0][0].shape[1] // halves
    shape = jax.ShapeDtypeStruct
    once = lambda v: pl.BlockSpec(v.shape, lambda *_: (0,) * len(v.shape), pipeline_mode=pl.Buffered(1))
    specs, args = [], []
    for n in range(ne):
        half = lambda e, c, n=n: jnp.where(e < n, 0, jnp.where(e == n, c, halves - 1))
        for b in range(nb):
            ga, dg, o = saved[b][n]
            args.append(ga)
            specs.append(pl.BlockSpec((1, f, rows), lambda e, c, o=o, half=half: (o, half(e, c), 0)))
        for b in range(nb):
            ga, dg, o = saved[b][n]
            args.append(dg)
            specs.append(pl.BlockSpec((1, rows, 2 * f), lambda e, c, o=o, half=half: (o, 0, half(e, c))))
    return pl.pallas_call(
        functools.partial(weight_grads_body, nb, halves),
        grid=(ne, halves),
        in_specs=[pl.BlockSpec(memory_space=pltpu.SMEM)] + [once(v) for v in (*h2s, *pays)] + specs,
        out_specs=[pl.BlockSpec((1, 3, width, f), lambda e, c: (e, 0, 0, 0))] * halves,
        out_shape=[shape((ne, 3, width, f), BF)] * halves,
        compiler_params=pltpu.CompilerParams(vmem_limit_bytes=VMEM_BYTES),
        cost_estimate=cost(6 * rows * nb * width * f * halves, 6 * halves * width * f + 4 * rows * nb * width),
        name="expert_weight_grads",
    )(tok, *h2s, *pays, *args)


def middle_back_body(nb, nlocal, _, ids, h2, mid, gain, gate, wr, *refs):
    dxs, tails = refs[:nb], refs[nb : 2 * nb]
    gm, small, acc = refs[2 * nb :]
    rows, width = h2.shape
    at = pl.program_id(0)
    cols = pl.ds(pl.multiple_of(at * rows, rows), rows)
    lane = lax.broadcasted_iota(jnp.int32, (rows, 128), 1)
    gates = gate[...]
    dgate = jnp.zeros((rows, 128), F32)
    for b in range(nb):
        part = tails[b][:, cols].astype(F32)
        part = (part[:8] + part[8:]).T
        for r in range(nlocal):
            dgate = jnp.where(lane == ids[b * nlocal + r], part[:, r : r + 1], dgate)
    dsel = gates * (dgate - jnp.sum(gates * dgate, axis=1, keepdims=True))
    high = dsel.astype(BF)
    rest = (dsel - high.astype(F32)).astype(BF)
    router = dot_tn(h2[...], high) + dot_tn(h2[...], rest)
    dh = dot_nt(high, wr[...]) + dot_nt(rest, wr[...])
    for b in range(nb):
        dh = dh + dxs[b][...].astype(F32)
    m = mid[...]
    r2 = lax.rsqrt(jnp.mean(m * m, axis=1, keepdims=True) + NORM_EPS)
    xhat = m * r2
    col = jnp.broadcast_to(jnp.sum(dh * xhat, axis=0, keepdims=True), (8, width)).T[:, :1]
    su = dh * gain[...].astype(F32)
    grad = (r2 * (su - xhat * jnp.mean(su * xhat, axis=1, keepdims=True))).astype(BF)
    gm[0] = grad
    gm[1] = grad
    small_here = jnp.where(lax.broadcasted_iota(jnp.int32, (width, 128), 1) == GAIN_F, col, router)

    @pl.when(at == 0)
    def _():
        acc[...] = small_here

    @pl.when(at > 0)
    def _():
        acc[...] += small_here

    small[...] = acc[...]


def middle_back(tok, ids, h2, mid, gain, gates, wr, dxs, nlocal):
    rows, width = h2.shape
    rt = rows // 2 if rows % 512 == 0 else rows
    shape = jax.ShapeDtypeStruct
    block = pl.BlockSpec((rt, width), lambda i: (i, 0))
    tail = pl.BlockSpec((16, width), lambda i: (rows // 16, 0))
    whole = lambda v: pl.BlockSpec(v.shape, lambda i: (0, 0))
    small = pl.BlockSpec((width, 128), lambda i: (0, 0))
    return pl.pallas_call(
        functools.partial(middle_back_body, len(dxs), nlocal),
        grid=(rows // rt,),
        in_specs=[pl.BlockSpec(memory_space=pltpu.SMEM)] * 2
        + [block, block, whole(gain), pl.BlockSpec((rt, 128), lambda i: (i, 0)), whole(wr)]
        + [block] * len(dxs)
        + [tail] * len(dxs),
        out_specs=[pl.BlockSpec((2, rt, width), lambda i: (0, i, 0)), small],
        out_shape=[shape((2, rows, width), BF), shape((width, 128), F32)],
        scratch_shapes=[pltpu.VMEM((width, 128), F32)],
        compiler_params=pltpu.CompilerParams(vmem_limit_bytes=VMEM_BYTES),
        cost_estimate=cost(40 * rows * width, 20 * rows * width),
        name="middle_back",
    )(tok, ids, h2, mid, gain, gates, wr, *dxs, *dxs)


def input_back_body(nq, _, wq, wkv, *refs):
    dq = refs[:nq]
    dkv = refs[nq : 2 * nq]
    dh = refs[2 * nq]
    acc = None
    for w, parts in ((wq, dq), (wkv, dkv)):
        at = 0
        for part in parts:
            n = part.shape[1]
            term = dot_nt(part[...], w[:, at : at + n])
            acc = term if acc is None else acc + term
            at += n
    dh[...] = acc.astype(BF)


def input_back(tok, wq, wkv, dqs, dkvs):
    rows = dqs[0].shape[0]
    width = wq.shape[0]
    rt = 256
    nq = len(dqs)
    block = lambda n: pl.BlockSpec((rt, n), lambda i: (i, 0))
    return pl.pallas_call(
        functools.partial(input_back_body, nq),
        grid=(rows // rt,),
        in_specs=[pl.BlockSpec(memory_space=pltpu.SMEM), whole_block(wq), whole_block(wkv)] + [block(v.shape[1]) for v in (*dqs, *dkvs)],
        out_specs=block(width),
        out_shape=jax.ShapeDtypeStruct((rows, width), BF),
        compiler_params=pltpu.CompilerParams(vmem_limit_bytes=VMEM_BYTES),
        cost_estimate=cost(4 * rows * width * wq.shape[1], 10 * rows * width),
        name="input_back",
    )(tok, wq, wkv, *dqs, *dkvs)


def token_grads_body(_, x, cot, own, other, gm, gain, out):
    xb = x[...].astype(F32)
    r = lax.rsqrt(jnp.mean(xb * xb, axis=1, keepdims=True) + NORM_EPS)
    xhat = xb * r
    su = (own[...].astype(F32) + other[...].astype(F32)) * gain[...].astype(F32)
    norm = r * (su - xhat * jnp.mean(su * xhat, axis=1, keepdims=True))
    out[...] = cot[...].astype(F32) + gm[...].astype(F32) + norm


def token_grads(tok, x, cot, own, other, gm, gain):
    rows, width = x.shape
    rt = 256
    block = pl.BlockSpec((rt, width), lambda i: (i, 0))
    return pl.pallas_call(
        token_grads_body,
        grid=(rows // rt,),
        in_specs=[pl.BlockSpec(memory_space=pltpu.SMEM)] + [block] * 5 + [whole_block(gain)],
        out_specs=block,
        out_shape=jax.ShapeDtypeStruct((rows, width), F32),
        compiler_params=pltpu.CompilerParams(vmem_limit_bytes=VMEM_BYTES),
        cost_estimate=cost(12 * rows * width, 14 * rows * width),
        name="token_grads",
    )(tok, x, cot, own, other, gm, gain)


def layer_out_body(nb, _, *refs):
    mid, live = refs[:2]
    moes = refs[2 : 2 + nb]
    out, stats = refs[2 + nb :]
    moe = sum(m[...].astype(F32) for m in moes) * RESID_SCALE
    outf = mid[...] + moe
    out[...] = outf.astype(BF)
    v = live[...]
    s0 = jnp.sum(v * jnp.sum(outf * outf, axis=1, keepdims=True))
    s2 = jnp.sum(v * jnp.sum(moe * moe, axis=1, keepdims=True))
    lane = lax.broadcasted_iota(jnp.int32, stats.shape, 1)

    @pl.when(pl.program_id(0) == 0)
    def _():
        stats[...] = jnp.zeros_like(stats)

    stats[...] += jnp.where(lane == 0, s0, jnp.where(lane == 2, s2, 0.0))


def layer_out_share(tok, mid, live, moes):
    rows, width = mid.shape
    shape = jax.ShapeDtypeStruct
    rt = 128
    block = lambda n: pl.BlockSpec((rt, n), lambda i: (i, 0))
    return pl.pallas_call(
        functools.partial(layer_out_body, len(moes)),
        grid=(rows // rt,),
        in_specs=[pl.BlockSpec(memory_space=pltpu.SMEM), block(width), block(1)] + [block(width)] * len(moes),
        out_specs=[block(width), pl.BlockSpec((8, 128), lambda i: (0, 0))],
        out_shape=[shape((rows, width), BF), shape((8, 128), F32)],
        compiler_params=pltpu.CompilerParams(vmem_limit_bytes=VMEM_BYTES),
        cost_estimate=cost(12 * rows * width, 14 * rows * width),
        name="layer_out",
    )(tok, mid, live, *moes)


def gather_rows_body(widths, count, turned, me, *refs):
    parts, outs = refs[:count], refs[-len(widths) :]
    size = parts[0].shape[0]
    for k, part in enumerate(parts):
        rows = pl.ds(pl.multiple_of((me[0] ^ k) * size, size), size)
        begin = 0
        for j, (out, w) in enumerate(zip(outs, widths, strict=True)):
            piece = part[:, begin : begin + w].astype(F32)
            if turned and j == len(widths) - 1:
                out[:, rows] = piece.T
            else:
                out[rows, :] = piece
            begin += w


def gather_rows(me, parts, widths, groups, turned, earlier=()):
    npart = len(parts)
    rows = npart * parts[0].shape[0]
    group = 1 if earlier else 0
    last = len(widths) - 1
    block = lambda j, w: (w, rows) if turned and j == last else (rows, w)
    shape = lambda j, w: (rows, w * groups) if j < 2 else block(j, w)
    return pl.pallas_call(
        functools.partial(gather_rows_body, widths, npart, turned),
        grid=(1,),
        in_specs=[pl.BlockSpec(memory_space=pltpu.SMEM)]
        + [whole_block(v) for v in parts]
        + [pl.BlockSpec(memory_space=pl.ANY)] * len(earlier),
        out_specs=[
            pl.BlockSpec(block(j, w), (lambda _: (0, group)) if j < 2 else (lambda _: (0, 0)))
            for j, w in enumerate(widths)
        ],
        out_shape=[jax.ShapeDtypeStruct(shape(j, w), F32) for j, w in enumerate(widths)],
        input_output_aliases={1 + npart + j: j for j in range(len(earlier))},
        compiler_params=pltpu.CompilerParams(vmem_limit_bytes=VMEM_BYTES),
        cost_estimate=cost(0, 6 * rows * sum(widths)),
        name="gather_rows",
    )(me, *parts, *earlier)


HD = 64
NEG = -1e30
BLK = 256


def swap_halves(v, lane):
    return jnp.where(lane % HD < HD // 2, pltpu.roll(v, 128 - HD // 2, 1), pltpu.roll(v, HD // 2, 1))


def mask_bias(start, valid, i, keys):
    row = lax.broadcasted_iota(jnp.int32, (BLK, keys), 0) + i * BLK
    key = lax.broadcasted_iota(jnp.int32, (BLK, keys), 1)
    first = jnp.maximum(start, row[:, :1] - (WINDOW - 1))
    ok = (key >= first) & (key <= row) & ((valid[:, :keys] > 0) | (key == row))
    return jnp.where(ok, 0.0, NEG).astype(F32)


def doc_starts(lengths, place):
    start = jnp.zeros_like(place)
    end = 0
    for j in range(lengths.shape[1]):
        end = end + lengths[0, j]
        start = jnp.where(place >= end, end, start)
    return start


def prepare_body(core, gu, down, cot, routes, pack, pay):
    width, f = gu.shape[2:]
    share = cot.shape[0]
    pack[:2] = gu[0]
    for k in range(width // f):
        pack[2, k * f : (k + 1) * f, :] = down[0, :, k * f : (k + 1) * f]
    pay[:share, :] = cot[...]
    pay[share:, :] = jnp.zeros((pay.shape[0] - share, width), BF)
    pay[share : share + routes.shape[0], :share] = routes[...].astype(F32).astype(BF)


def prepare(core, gu, down, cot, routes):
    width, f = gu.shape[2:]
    share = routes.shape[1]
    shape = jax.ShapeDtypeStruct
    return pl.pallas_call(
        prepare_body,
        grid_spec=pltpu.PrefetchScalarGridSpec(
            num_scalar_prefetch=1,
            grid=(1,),
            in_specs=[
                whole_block(gu),
                whole_block(down),
                pl.BlockSpec((share, width), lambda _, c: (c[0], 0)),
                whole_block(routes),
            ],
            out_specs=[
                pl.BlockSpec((3, width, f), lambda *_: (0, 0, 0)),
                pl.BlockSpec((share + 16, width), lambda *_: (0, 0)),
            ],
        ),
        out_shape=[shape((3, width, f), BF), shape((share + 16, width), BF)],
        compiler_params=pltpu.CompilerParams(vmem_limit_bytes=VMEM_BYTES),
        cost_estimate=cost(0, 12 * width * f),
        name="prepare",
    )(core, gu, down, cot, routes)


def attn_forward_body(nout, core, lengths, x_hbm, gain, wq_hbm, wkv_hbm, wo_hbm, valid, *refs):
    outs, bufs = refs[:nout], refs[nout : 2 * nout]
    x, wq, wkv, wo, isem, osem = refs[2 * nout :]
    h1, q, kd, vd, o, lse, cos, sin, own, *rest = bufs
    nb = x.shape[0] // BLK
    ins = [pltpu.make_async_copy(x_hbm.at[pl.ds(i * BLK, BLK), :], x.at[pl.ds(i * BLK, BLK), :], isem.at[i]) for i in range(nb)]
    weights = [
        pltpu.make_async_copy(source, to, isem.at[nb + n])
        for n, (source, to) in enumerate(((wq_hbm, wq), (wkv_hbm, wkv), (wo_hbm, wo)))
    ]
    for copy in (ins[0], *weights, *ins[1:]):
        copy.start()
    leaving = []
    nkv = wkv.shape[1] // 128
    lane = lax.broadcasted_iota(jnp.int32, (BLK, 128), 1)
    low = lane < HD
    ga = gain[...].astype(F32)
    frequencies = jnp.exp((lane[:1] % (HD // 2)).astype(F32) * (-2.0 * math.log(ROPE_BASE) / HD))
    half = own.shape[0]
    for i in range(x.shape[0] // BLK):
        rs = pl.ds(i * BLK, BLK)
        keys = (i + 1) * BLK
        place = lax.broadcasted_iota(jnp.int32, (BLK, 1), 0) + i * BLK
        start = doc_starts(lengths, place)
        angles = (place - start).astype(F32) * frequencies
        cb = jnp.cos(angles)
        sb = jnp.sin(angles)
        sb = jnp.where(lane % HD < HD // 2, -sb, sb)
        cos[rs, :] = cb
        sin[rs, :] = sb
        ins[i].wait()
        xb = x[rs, :].astype(F32)
        r = lax.rsqrt(jnp.mean(xb * xb, axis=1, keepdims=True) + NORM_EPS)
        hb = (xb * r * ga).astype(BF)
        h1[rs, :] = hb
        if i == 0:
            weights[0].wait()
            weights[1].wait()
        qp = dot(hb, wq[...])
        kvp = dot(hb, wkv[...])
        for n in range(nkv):
            ns = slice(n * 128, (n + 1) * 128)
            qn = qp[:, ns]
            q[rs, ns] = ((qn * cb + swap_halves(qn, lane) * sb) * ATTN_SCALE).astype(BF)
            kv = kvp[:, ns]
            rot = kv * cb + swap_halves(kv, lane) * sb
            kd[rs, ns] = jnp.where(low, rot, pltpu.roll(rot, HD, 1)).astype(BF)
            vd[rs, ns] = jnp.where(low, pltpu.roll(kv, HD, 1), kv).astype(BF)
        for j in (0, 1, 2, 3, 6, 7):
            leaving.append(pltpu.make_async_copy(bufs[j].at[rs, :], outs[j].at[rs, :], osem.at[i, j]))
            leaving[-1].start()
        bias = mask_bias(start, valid, i, keys)
        bias2 = jnp.concatenate([bias, bias], axis=0)
        lse_all = jnp.zeros((BLK, 128), F32)
        for n in range(nkv):
            ns = slice(n * 128, (n + 1) * 128)
            qn = q[rs, ns]
            zero = jnp.zeros_like(qn)
            q2 = jnp.concatenate([jnp.where(low, qn, zero), jnp.where(low, zero, qn)], axis=0)
            s = dot_nt(q2, kd[:keys, ns]) + bias2
            m = jnp.max(s, axis=1, keepdims=True)
            p = jnp.exp(s - m)
            total = jnp.sum(p, axis=1, keepdims=True)
            o2 = dot(p.astype(BF), vd[:keys, ns]) * (1.0 / total)
            o[rs, ns] = jnp.where(low, o2[:BLK], o2[BLK:]).astype(BF)
            l2 = m + jnp.log(total)
            lse_all = jnp.where(lane == 2 * n, l2[:BLK], jnp.where(lane == 2 * n + 1, l2[BLK:], lse_all))
        lse[rs, :] = lse_all
        for j in (4, 5):
            leaving.append(pltpu.make_async_copy(bufs[j].at[rs, :], outs[j].at[rs, :], osem.at[i, j]))
            leaving[-1].start()
        if i == 0:
            weights[2].wait()
        term = dot(o[rs, :], wo[...]).astype(BF)
        at = pl.ds(i * BLK % half, BLK)
        if not rest:
            own[rs, :] = term
            leaving.append(pltpu.make_async_copy(own.at[rs, :], outs[8].at[rs, :], osem.at[i, 8]))
            leaving[-1].start()
        else:
            mine = pltpu.make_async_copy(own.at[at, :], outs[8].at[at, :], osem.at[i, 8])
            other = pltpu.make_async_copy(rest[0].at[at, :], outs[9].at[at, :], osem.at[i, 8])

            @pl.when(core[0] == i * BLK // half)
            def _():
                own[at, :] = term
                mine.start()

            @pl.when(core[0] != i * BLK // half)
            def _():
                rest[0][at, :] = term
                other.start()

            leaving.append(mine)
    for copy in leaving:
        copy.wait()


def attn_forward(core, lengths, x, gain, wq, wkv, wo, valid, split):
    rows, width = x.shape
    wid = wq.shape[1]
    kvw = wkv.shape[1]
    shape = jax.ShapeDtypeStruct
    part = [((rows // 2, width), BF)] * 2 if split else [((rows, width), BF)]
    outs = [
        ((rows, width), BF),
        ((rows, wid), BF),
        ((rows, kvw), BF),
        ((rows, kvw), BF),
        ((rows, wid), BF),
        ((rows, 128), F32),
        ((rows, 128), F32),
        ((rows, 128), F32),
        *part,
    ]
    nb = rows // BLK
    smem, vmem, there = (pl.BlockSpec(memory_space=m) for m in (pltpu.SMEM, pltpu.VMEM, pl.ANY))
    return pl.pallas_call(
        functools.partial(attn_forward_body, len(outs)),
        in_specs=[smem, smem, there, vmem, there, there, there, vmem],
        out_specs=[there] * len(outs),
        out_shape=[shape(*s) for s in outs],
        scratch_shapes=[pltpu.VMEM(*s) for s in outs]
        + [
            pltpu.VMEM((rows, width), BF),
            pltpu.VMEM((width, wid), BF),
            pltpu.VMEM((width, kvw), BF),
            pltpu.VMEM((wid, width), BF),
            pltpu.SemaphoreType.DMA((nb + 3,)),
            pltpu.SemaphoreType.DMA((nb, 9)),
        ],
        compiler_params=pltpu.CompilerParams(vmem_limit_bytes=VMEM_BYTES),
        cost_estimate=cost(2 * rows * width * 3 * wid + 4 * rows * rows * 4 * wid, 12 * rows * width),
        name="attention_forward",
    )(core, lengths, x, gain, wq, wkv, wo, valid)


def attn_backward_body(first, npart, nmore, npiece, places, core, at, lengths, q, kd, vd, lse, cos, sin, valid, gain, *refs):
    it = iter(refs)
    take = lambda n: [next(it) for _ in range(n)]
    h1_hbm, wq_hbm, wkv_hbm = take(3)
    more = take(nmore)
    if places:
        cot, wo, o_hbm, *parts = take(3 + npart)
    else:
        (do,) = take(1)
    dq, dkv, sums = take(3)
    pieces = take(npiece)
    if places:
        do, gm = take(2)
    dk, dv, gw, h1, wq, wkv, sem = take(7)
    if places:
        da, o = take(2)
    wid = q.shape[1]
    width = h1.shape[1]
    cols = pl.ds(first * 128, wid)
    copies = [
        pltpu.make_async_copy(h1_hbm, h1, sem.at[0]),
        pltpu.make_async_copy(wq_hbm.at[:, cols], wq, sem.at[1]),
        pltpu.make_async_copy(wkv_hbm.at[:, cols], wkv, sem.at[2]),
    ]
    if places:
        copies.append(pltpu.make_async_copy(o_hbm, o, sem.at[3]))
    for copy in copies:
        copy.start()
    if places:
        for i in range(q.shape[0] // BLK):
            rs = pl.ds(i * BLK, BLK)
            g = placed(core, parts, i)
            gm[rs, :] = g.astype(BF)
            d = (RESID_SCALE * (cot[rs, :].astype(F32) + g)).astype(BF)
            da[rs, :] = d
            do[rs, :] = dot_nt(d, wo[...]).astype(BF)
    nkv = kd.shape[1] // 128
    wid = q.shape[1]
    lane = lax.broadcasted_iota(jnp.int32, (BLK, 128), 1)
    low = lane < HD
    dk[...] = jnp.zeros_like(dk)
    dv[...] = jnp.zeros_like(dv)
    nb = q.shape[0] // BLK
    for i in range(nb):
        rs = pl.ds(i * BLK, BLK)
        keys = (i + 1) * BLK
        cb, sb = cos[rs, :], sin[rs, :]
        place = lax.broadcasted_iota(jnp.int32, (BLK, 1), 0) + i * BLK
        bias = mask_bias(doc_starts(lengths, place), valid, i, keys)
        bias2 = jnp.concatenate([bias, bias], axis=0)
        lse_i = lse[rs, :]
        for n in range(nkv):
            ns = slice(n * 128, (n + 1) * 128)
            qn, dn = q[rs, ns], do[rs, ns]
            zero = jnp.zeros_like(qn)
            q2 = jnp.concatenate([jnp.where(low, qn, zero), jnp.where(low, zero, qn)], axis=0)
            d2 = jnp.concatenate([jnp.where(low, dn, zero), jnp.where(low, zero, dn)], axis=0)
            h = 2 * (first + n)
            l2 = jnp.concatenate([lse_i[:, h : h + 1], lse_i[:, h + 1 : h + 2]], axis=0)
            p = jnp.exp(dot_nt(q2, kd[:keys, ns]) + bias2 - l2)
            dp = dot_nt(d2, vd[:keys, ns])
            shift = jnp.sum(p * dp, axis=1, keepdims=True)
            ds = (p * (dp - shift)).astype(BF)
            dv[:keys, ns] += dot_tn(p.astype(BF), d2)
            dk[:keys, ns] += dot_tn(ds, q2)
            dq2 = dot(ds, kd[:keys, ns])
            dqn = jnp.where(low, dq2[:BLK], dq2[BLK:]) * ATTN_SCALE
            dq[rs, ns] = (dqn * cb - swap_halves(dqn, lane) * sb).astype(BF)
    for i in range(nb):
        rs = pl.ds(i * BLK, BLK)
        cb, sb = cos[rs, :], sin[rs, :]
        for n in range(nkv):
            ns = slice(n * 128, (n + 1) * 128)
            kk = dk[rs, ns]
            kk = kk + pltpu.roll(kk, HD, 1)
            vv = dv[rs, ns]
            vv = vv + pltpu.roll(vv, HD, 1)
            dkv[rs, ns] = jnp.where(low, kk * cb - swap_halves(kk, lane) * sb, vv).astype(BF)
    for copy in copies:
        copy.wait()
    gq = dot_tn(h1[...], dq[...])
    gk = dot_tn(h1[...], dkv[...])
    gw[:, :wid] = gq.astype(BF)
    gw[:, wid : 2 * wid] = gk.astype(BF)
    ga = jnp.sum(gq * wq[...].astype(F32) + gk * wkv[...].astype(F32), axis=1, keepdims=True) / gain[...].astype(F32)
    lanes = lax.broadcasted_iota(jnp.int32, (width, 128), 1)
    ga = jnp.where(lanes == GAIN_A, ga, 0.0)
    for v in more:
        ga = ga + v[...]
    sums[...] = ga
    if places:
        gwo = dot_tn(o[...], da[...]).astype(BF)
        depth = gwo.shape[0]
        for n in range(width // depth):
            rs = slice(n * depth, (n + 1) * depth)
            gw[rs, 2 * wid : 2 * wid + depth] = gwo[:, rs]
    else:
        gw[:, 2 * wid :] = ga.astype(BF)
    size = width // len(pieces)
    for k, piece in enumerate(pieces):
        piece[...] = gw[pl.ds(pl.multiple_of((at[0] ^ k) * size, size), size), :]


def placed(core, parts, i):
    if len(parts) == 1:
        return parts[0][i * BLK : (i + 1) * BLK, :].astype(F32)
    n = len(parts) // 2
    mine, other = parts[i % n][...].astype(F32), parts[n + i % n][...].astype(F32)
    return jnp.where(core[0] == i // n, mine, other)


def attn_backward(first, count, core, at, npiece, lengths, q, kd, vd, lse, h1, cos, sin, valid, wq, wkv, gain, sums, do=None, given=None):
    rows, width = h1.shape
    w = count * 128
    depth = given[1].shape[0] if given else 128
    cols = 2 * w + depth
    shape = jax.ShapeDtypeStruct
    part = pl.BlockSpec((rows, w), lambda _: (0, first // count))
    full = lambda *s: pl.BlockSpec(s, lambda _: (0, 0))
    there = pl.BlockSpec(memory_space=pl.ANY)
    size = width // npiece
    outs = [(rows, w)] * 2 + [(width, 128)] + [(size, cols)] * npiece
    types = [BF, BF, F32] + [BF] * npiece
    scratch = [
        pltpu.VMEM((rows, w), F32),
        pltpu.VMEM((rows, w), F32),
        pltpu.VMEM((width, cols), BF),
        pltpu.VMEM((rows, width), BF),
        pltpu.VMEM((width, w), BF),
        pltpu.VMEM((width, w), BF),
        pltpu.SemaphoreType.DMA((4,)),
    ]
    if given:
        cot, wo, o, *parts = given
        last = [cot, wo, o, *parts]
        last_specs = [whole_block(cot), whole_block(wo), there] + [whole_block(v) for v in parts]
        outs += [(rows, depth), (rows, width)]
        types += [BF, BF]
        scratch += [pltpu.VMEM((rows, width), BF), pltpu.VMEM((rows, depth), BF)]
    else:
        parts, last, last_specs = (), [do], [part]
    return pl.pallas_call(
        functools.partial(attn_backward_body, first, len(parts), len(sums), npiece, bool(given)),
        grid=(1,),
        in_specs=[pl.BlockSpec(memory_space=pltpu.SMEM)] * 3
        + [part] * 3
        + [whole_block(v) for v in (lse, cos, sin, valid, gain)]
        + [there] * 3
        + [whole_block(v) for v in sums]
        + last_specs,
        out_specs=[full(*s) for s in outs],
        out_shape=[shape(s, d) for s, d in zip(outs, types, strict=True)],
        scratch_shapes=scratch,
        compiler_params=pltpu.CompilerParams(vmem_limit_bytes=VMEM_BYTES),
        cost_estimate=cost(4 * rows * width * w + 20 * rows * rows * w, 10 * rows * width),
        name="attention_backward",
    )(core, at, lengths, q, kd, vd, lse, cos, sin, valid, gain, h1, wq, wkv, *sums, *last)


def on_device(
    tokens,
    gain_attn,
    query_weight_matrix,
    key_value_weight,
    w_out,
    gain_ffn,
    w_router,
    w_gate_up,
    w_down,
    routes,
    doc_lengths,
    valid_mask,
    cotangent,
):
    rows, width = tokens.shape
    share = routes.shape[0]
    n_ep, n_tp = lax.axis_size("ep"), lax.axis_size("tp")
    nexp = w_router.shape[1]
    inner = math.gcd(n_ep, 4)
    outer = n_ep // inner
    me = lax.axis_index("ep")
    me_in = me % inner
    core = lax.axis_index("tp")[None]
    pair = n_tp == 2

    def across(v, k):
        return lax.ppermute(v, "ep", [(i, i ^ k) for i in range(n_ep)])

    def along(v, k):
        return lax.ppermute(v, "ep", [(i, (i + k * inner) % n_ep) for i in range(n_ep)])

    def swap(v):
        return lax.ppermute(v, "tp", [(0, 1), (1, 0)])

    def after(v, *earlier):
        return lax.optimization_barrier((v, *earlier))[0]

    def total(terms):
        acc = terms[0].astype(F32)
        for term in terms[1:]:
            acc = acc + term.astype(F32)
        return acc

    def scatter_plane(pieces):
        return [pieces[0]] + [across(pieces[k], k) for k in range(1, inner)]

    def cut_rows(v, k):
        size = v.shape[0] // inner
        return lax.dynamic_slice_in_dim(v, (me_in ^ k) * size, size)

    def summed(terms):
        return total(terms).astype(BF)

    def column_steps(v):
        bit = 1
        while bit < outer:
            other = lax.ppermute(v, "ep", [(i, i ^ (bit * inner)) for i in range(n_ep)])
            yield other
            v = summed([v, release(other)])
            bit *= 2
        yield v

    def unpacked(v):
        f = v.shape[2]
        return v[:2], v[2].reshape(width // f, f, f).transpose(1, 0, 2).reshape(f, width)

    def packed(gu, down):
        f = gu.shape[2]
        return jnp.concatenate([gu, down.reshape(f, width // f, f).transpose(1, 0, 2).reshape(1, width, f)])

    def full_hidden(v):
        if pair:
            return [v, swap(v)]
        gu, down = unpacked(v)
        return [
            packed(
                lax.all_gather(gu, "tp", axis=2, tiled=True),
                lax.all_gather(down, "tp", axis=0, tiled=True),
            )
        ]

    def own_hidden(v):
        if pair:
            return v[0].astype(F32) + swap(v[1]).astype(F32)
        gu, down = unpacked(v[0].astype(F32))
        return packed(
            lax.psum_scatter(gu, "tp", scatter_dimension=2, tiled=True),
            lax.psum_scatter(down, "tp", scatter_dimension=0, tiled=True),
        )

    halves = 2 if pair else 1
    local = jnp.arange(outer, dtype=jnp.int32) * inner
    ids = (me - local) % n_ep
    ids_all = jnp.concatenate([((me ^ k) - local) % n_ep for k in range(inner)])
    valid_row = valid_mask[None, :]
    live_all = valid_mask.astype(F32)[:, None]
    live = lax.dynamic_slice_in_dim(live_all, core[0] * share, share)
    gain_a, gain_f = gain_attn[None, :], gain_ffn[None, :]
    wr = jnp.pad(w_router, ((0, 0), (0, 128 - nexp)))

    tok = core

    def finish(*values):
        nonlocal tok
        tok = after(tok, *values)

    def release(v):
        return after(v, tok)

    pack, pay = prepare(tok, w_gate_up, w_down, cotangent, routes.T)
    held = [pack]
    if outer > 1:
        held.append(along(pack, 1))
    pays = [pay] + [across(pay, k) for k in range(1, min(inner, 3))]
    chunks = [full_hidden(pack)]
    finish(pack)

    h1, q, kd, vd, o, lse, cos, sin, *part = attn_forward(
        tok, doc_lengths, tokens, gain_a, query_weight_matrix, key_value_weight, w_out, valid_row, pair
    )
    if pair:
        own, other = part[0], swap(part[1])
    else:
        own = lax.psum_scatter(part[0].astype(F32), "tp", scatter_dimension=0, tiled=True)
        other = jnp.zeros_like(own)
    finish(own, other, *pays, *chunks[0])
    mid, h2, stats = middle_norm(tok, tokens, own, other, gain_f, live_all)
    h2s = [h2] + [across(h2, k) for k in range(1, min(inner, 3))]
    finish(h2, *held[1:])

    near = min(2, outer)
    last = outer - 1
    far = list(range(3, inner))
    close = list(range(min(inner, 3)))
    state = [None] * inner
    saved = [dict() for _ in range(inner)]

    gates = [None] * inner

    def work(blocks, first, count):
        rows_in = [h2s[b] for b in blocks], [pays[b] for b in blocks]
        packs = [c for r in range(first, first + count) for c in chunks[r]]
        if state[blocks[0]] is None:
            out = experts(release(ids), *rows_in, wr, packs, halves)
        else:
            held_gates, before = [gates[b] for b in blocks], [state[b] for b in blocks]
            out = one_expert(release(ids), *rows_in, held_gates, before, packs, first)
        for b, (dx, moe, gat, dgu, *gate) in zip(blocks, out, strict=True):
            state[b] = (dx, moe)
            gates[b] = gate[0] if gate else gates[b]
            for r in range(count):
                saved[b][first + r] = (gat, dgu, r)
        finish(out[0][1])

    def expert_grads(experts_of):
        out = weight_grads(tok, h2s, pays, [[s[r] for r in experts_of] for s in saved], halves)
        finish(out[0])
        return out

    def next_held():
        v = release(held[-1])
        if len(held) < outer:
            held.append(along(v, 1))
        chunks.append(full_hidden(v))

    if outer > 1:
        next_held()
    work([0], 0, near)
    finish(*h2s)
    for k in far:
        pays.append(across(release(pay), k))
    if close[1:]:
        work(close[1:], 0, near)
    if outer > 2:
        finish(held[-1])
        next_held()
    finish(*pays)
    for k in far:
        h2s.append(across(release(h2), k))
    for r in range(near, last):
        work(close, r, 1)
        if r + 1 < last:
            finish(held[-1])
            next_held()
    finish(*h2s)
    for b in far:
        work([b], 0, max(last, near))
    if last >= near:
        finish(held[-1])
        next_held()

    first = 1 % outer
    later = [[r] for r in range(2, min(outer, 3))] + [[*range(3, outer), 0]]
    later = later if outer > 1 else []
    raw = expert_grads([first])
    parts = {first: own_hidden([v[0] for v in raw])}
    if last >= near and inner > 1:
        work(list(range(1, inner)), last, 1)
    ring = parts[first].astype(BF)
    finish(ring)
    if outer > 1:
        ring = along(ring, 1)
    dxs = [None] + [across(state[k][0], k) for k in range(1, inner)]
    if last >= near:
        work([0], last, 1)
    dxs[0] = state[0][0]
    raws = [expert_grads(rs) for rs in later]
    def ring_step(r):
        nonlocal ring
        term = release(ring).astype(F32) + parts[r]
        if r == 0:
            return term
        ring = term.astype(BF)
        finish(ring)
        ring = along(ring, 1)

    def take_part(rs, raw):
        if not pair:
            parts.update({r: own_hidden([raw[0][n]]) for n, r in enumerate(rs)})
            return
        other = swap(release(raw[1]))
        parts.update({r: raw[0][n].astype(F32) + other[n].astype(F32) for n, r in enumerate(rs)})
        if rs == [2]:
            finish(other)

    finish(*dxs, *([ring] if outer > 1 else []))
    if outer > 2:
        take_part(later[0], raws[0])
        ring_step(2)
    for rs, raw in zip(later, raws, strict=True):
        if rs != [2]:
            take_part(rs, raw)
    moes = [state[0][1]] + [across(release(state[k][1]), k) for k in range(1, inner)]
    gm, small = middle_back(tok, ids_all, h2, mid, gain_f, gates[0], wr, dxs, outer)
    if pair:
        gm = lax.all_to_all(gm, "tp", 0, 0).reshape(rows, width)
    else:
        gm = lax.all_gather(gm[0], "tp", axis=0, tiled=True)
    finish(gm)

    nkv = kd.shape[1] // 128
    groups = 2 if nkv % 2 == 0 else 1
    each = nkv // groups
    w = each * 128
    depth = w_out.shape[0]
    dqs, dkvs, sums = [], [], small
    at = me_in[None]
    for n in range(groups):
        first_one = n == 0
        out = attn_backward(
            n * each,
            each,
            tok,
            at,
            inner,
            doc_lengths,
            q,
            kd,
            vd,
            lse,
            h1,
            cos,
            sin,
            valid_row,
            query_weight_matrix,
            key_value_weight,
            gain_attn[:, None],
            [sums],
            None if first_one else do,
            (cotangent, w_out, o, gm) if first_one else None,
        )
        dq, dkv, sums, *pieces = out[: 3 + inner]
        if first_one:
            do, gm_all = out[3 + inner :]
        finish(pieces[0])
        dqs.append(dq)
        dkvs.append(dkv)
        if first_one and groups > 1:
            terms = scatter_plane(pieces)
            if outer > 3:
                finish(ring)
                ring_step(3)
    if groups == 1:
        sums_only = [cut_rows(sums.astype(BF), k) for k in range(inner)]
        terms = scatter_plane([jnp.concatenate(v, axis=1) for v in zip(pieces, sums_only, strict=True)])
    finish(*moes)
    out_share, stats_out = layer_out_share(tok, mid, live, moes)
    finish(out_share)
    spread = jnp.pad((stats + stats_out)[:1, :4], ((0, 0), (STATS, 128 - STATS - 4)))

    def closing_sum(terms):
        v = total([release(t) for t in terms])
        row = lax.broadcasted_iota(jnp.int32, v.shape, 0)
        lane = lax.broadcasted_iota(jnp.int32, v.shape, 1) - (v.shape[1] - 128)
        place = (row == 0) & (lane >= STATS) & (lane < STATS + 4)
        return jnp.where(place, jnp.pad(spread, ((0, 0), (v.shape[1] - 128, 0))), v).astype(BF)

    def spread_plane(v):
        return [v] + [across(v, k) for k in range(1, inner)]

    if groups > 1:
        finish(*terms)
        ahead = column_steps(summed([release(t) for t in terms]))
        moving = next(ahead)
        terms = scatter_plane([release(v) for v in pieces])
    dh1 = input_back(tok, query_weight_matrix, key_value_weight, dqs, dkvs)
    finish(dh1, *([ring] if outer > 1 else []), *([moving] if groups > 1 else []), *terms)
    if groups > 1:
        moving = next(ahead)
    closing = closing_sum(terms)
    if pair:
        dh_other = swap(release(dh1))
        out_other = swap(out_share)
    else:
        dh1, dh_other = lax.psum(dh1.astype(F32), "tp"), jnp.zeros_like(dh1)
    finish(dh_other, closing)
    behind = column_steps(release(closing))
    late = next(behind)
    grad_tokens = token_grads(tok, tokens, cotangent, dh1, dh_other, gm, gain_a)
    finish(grad_tokens)
    if pair:
        layer_out = jnp.where(
            core[0] == 0,
            jnp.concatenate([release(out_share), out_other]),
            jnp.concatenate([out_other, release(out_share)]),
        )
        finish(layer_out)
    else:
        layer_out = lax.all_gather(out_share, "tp", axis=0, tiled=True)
    spreads = []
    if groups > 1:
        finish(moving)
    finish(late)
    late = next(behind)
    if groups > 1:
        for whole in ahead:
            pass
        finish(whole)
        spreads.append(spread_plane(whole))
    for r in range(4, outer):
        ring_step(r)
    expert_sums = ring_step(0) if outer > 1 else parts[0]
    gu_grad, down_grad = unpacked(expert_sums)
    finish(late)
    for late in behind:
        pass
    spreads.append(spread_plane(release(late)))
    if groups > 1:
        *grads, folded = gather_rows(at, spreads[0], (w, w, depth), groups, False)
        finish(folded)
        grad_w_query, grad_w_kv, extras = gather_rows(release(at), spreads[1], (w, w, 128), groups, True, grads)
    else:
        grad_w_query, grad_w_kv, folded, extras = gather_rows(release(at), spreads[0], (w, w, depth, 128), 1, True)
    grad_w_out = jnp.concatenate([folded[n * depth : (n + 1) * depth] for n in range(width // depth)], axis=1)
    extras = extras[: STATS + 6]
    extras = extras + swap(extras) if pair else lax.psum(extras, "tp")
    s = jnp.sum(extras[STATS : STATS + 4, :: width // inner], axis=1)
    return (
        layer_out,
        grad_tokens,
        extras[GAIN_A],
        grad_w_query,
        grad_w_kv,
        grad_w_out,
        extras[GAIN_F],
        extras[:nexp].T,
        gu_grad[None],
        down_grad[None],
        jnp.sqrt(s[:3] / (s[3] * width)),
    )


def solution(mesh):
    return jax.shard_map(
        on_device,
        mesh=mesh,
        in_specs=(
            P("ep", None),
            P(),
            P(None, "tp"),
            P(None, "tp"),
            P("tp", None),
            P(),
            P(),
            P("ep", None, None, "tp"),
            P("ep", "tp", None),
            P(("ep", "tp"), None),
            P("ep", None),
            P("ep"),
            P("ep", None),
        ),
        out_specs=(
            P("ep", None),
            P("ep", None),
            P(),
            P(None, "tp"),
            P(None, "tp"),
            P("tp", None),
            P(),
            P(),
            P("ep", None, None, "tp"),
            P("ep", "tp", None),
            P(),
        ),
        check_vma=False,
    )
```
